512 devices in a mesh: aper: 32 (over z_lo, x), band: 16 (over z_hi, y, core).
Axes of the slice: x: 4, y: 4, z: 16 (z_hi: 2, z_lo: 8; z = z_hi * 8 + z_lo), core: 2. Of those that a mesh axis runs over, the one named last changes fastest.
Arguments:
- pulse_data: bfloat16 [2, 4096, 8192], P(None, ('aper', 'band')), may hold values from -6 to 6
- window_start: int32 [4096, 16], P(('aper', 'band')), may hold values from 0 to 7680
- footprint: int32 [4096, 8], P(('aper', 'band')), may hold values from 0 to 15, all different within a row
- range_to_row_weight: bfloat16 [1024, 512], P('band'), may hold values from -0.25 to 0.25
- slow_taps: float32 [5], replicated, may hold values from 0.2 to 1
- ramp_rate: float32 [4096], replicated, may hold values from -0.5 to 0.5
- image_now: float32 [2, 1024, 8192], P(None, 'band', 'aper'), may hold values from -6 to 6
- step_and_variation_weight: float32 [2], replicated, may hold values from 0.5 to 1.5
Outputs:
- updated_image: float32 [2, 1024, 8192], P(None, 'band', 'aper')
The draws below stay inside these ranges and needn't reach their ends.
Inputs may be any that keep to these rules, and one draw needn't show every extreme that they name: `window_start`: each pulse's window of 512 bins lies inside its 8192 range bins. `footprint`: each row lists 8 distinct bands; every band is lit by some pulse.
All inputs are finite; a program needn't handle non-finite values.
Results may differ from the reference program's by a relative error of at most 0.0031.
Values may be sent and summed in bfloat16 or wider, within the bound.
No kernel may reach another device: no remote copies, remote signals or barrier semaphores. Data moves between devices by JAX's collectives and lax.ppermute only.
A program may use at most 128 MiB of HBM per device.

```python
import math
import jax
import jax.numpy as jnp
from jax import lax

BINS = 8192
WIN = 512
TAPS_K = 2
ROWS_B = 64
FOOT = 8
PULSES = 4096
NROWS = 1024
NCOLS = 8192
N_APER = 32
N_BAND = 16


def set_ends(drawn, key, low, top_value):
    longest = drawn.shape.index(max(drawn.shape))
    spots = []
    for shift in (0, 1):
        where = [jax.random.randint(jax.random.fold_in(key, axis), (), 0, length) for axis, length in enumerate(drawn.shape)]
        where[longest] = (where[longest] + shift) % drawn.shape[longest]
        spots.append(tuple(where))
    return drawn.at[spots[0]].set(low).at[spots[1]].set(top_value)


def steps_of(own_key, extent, pieces, smallest, high):
    level = 1.0
    for position, parts in pieces:
        draws = jax.random.uniform(jax.random.fold_in(jax.random.fold_in(own_key, 6), position), (parts,), jnp.float32, smallest / len(pieces), high / len(pieces))
        level = level * jnp.repeat(jnp.exp(draws), extent[position] // parts).reshape((-1,) + (1,) * (len(extent) - 1 - position))
    return level


def different_ones(own_key, rows, number_of, top, lift):
    ranking = jax.random.permutation(jax.random.fold_in(own_key, 1), number_of)
    favour = ranking
    for power in range(3):
        favour = favour * favour // number_of
    favour = favour * lift // number_of
    tickets = jax.random.randint(jax.random.fold_in(own_key, 2), (rows, number_of), 0, 4096) + favour
    fixed_rows = jax.random.permutation(jax.random.fold_in(own_key, 3), rows)[jnp.arange(number_of) % rows]
    tickets = jnp.where(jnp.arange(rows)[:, None] == fixed_rows[None, :], 1 << 14, tickets)
    score = tickets * number_of + jnp.arange(number_of)
    return lax.top_k(score.astype(jnp.int32), top)[1].astype(jnp.int32)


def normal_values(rng, dims, scale, bound, shards=(), held_as=jnp.bfloat16):
    loudness = steps_of(rng, dims, shards, -0.22, 0.18) if shards else 1.0
    drawn = jax.random.normal(rng, dims, jnp.float32) * scale * loudness
    return jnp.minimum(jnp.maximum(drawn, -bound), bound).astype(held_as)


def setup_inputs(seed: int = 0) -> dict:
    keys = jax.random.split(jax.random.key(seed), 9)
    pulse_data = normal_values(keys[0], (2, PULSES, BINS), 1.0, 6.0, ((1, 512),))
    window_start = set_ends(jax.random.randint(keys[1], (PULSES, N_BAND), 0, BINS - WIN + 1), jax.random.fold_in(keys[1], 1), 0, BINS - WIN).astype(jnp.int32)
    footprint = different_ones(keys[2], PULSES, N_BAND, FOOT, 8192)
    range_to_row_weight = normal_values(keys[3], (NROWS, WIN), WIN ** -0.5, 0.25, ((0, 16),))
    slow_taps = jnp.clip(jax.random.uniform(keys[4], (2 * TAPS_K + 1,), jnp.float32, 0.2, 1.0), 0.2, 1.0)
    ramp_rate = jnp.clip(jax.random.uniform(keys[5], (PULSES,), jnp.float32, -0.5, 0.5), -0.5, 0.5)
    image_now = normal_values(keys[6], (2, NROWS, NCOLS), 1.0, 6.0, ((1, 16), (2, 32)), jnp.float32)
    step_and_variation_weight = jnp.clip(jax.random.uniform(keys[7], (2,), jnp.float32, 0.5, 1.5), 0.5, 1.5)
    return dict(pulse_data=pulse_data, window_start=window_start, footprint=footprint, range_to_row_weight=range_to_row_weight, slow_taps=slow_taps, ramp_rate=ramp_rate, image_now=image_now, step_and_variation_weight=step_and_variation_weight)


smooth_eps = 0.05

def variation_term(padded):
    row_step = padded[:, 1:, :-1] - padded[:, :-1, :-1]
    col_step = padded[:, :-1, 1:] - padded[:, :-1, :-1]
    magnitude = jnp.sqrt(lax.optimization_barrier(jnp.sum(row_step * row_step + col_step * col_step, axis=0)) + smooth_eps)
    row_flow = row_step / magnitude
    col_flow = col_step / magnitude
    return -(row_flow[:, 1:, 1:] - row_flow[:, :-1, 1:] + col_flow[:, 1:, 1:] - col_flow[:, 1:, :-1])

def reference(pulse_data, window_start, footprint, range_to_row_weight, slow_taps, ramp_rate, image_now, step_and_variation_weight):
    band_ids = jnp.arange(N_BAND, dtype=jnp.int32)
    lit_mask = jnp.any(footprint[:, :, None] == band_ids[None, None, :], axis=1)

    def lift_band(band_index):
        starts = window_start[:, band_index].astype(jnp.int32)
        fragment_list = jax.vmap(lambda pulse_rows, start_bin: lax.dynamic_slice_in_dim(pulse_rows, start_bin, WIN, 1), in_axes=(1, 0))(pulse_data, starts)
        weight = jnp.where(lit_mask[:, band_index], 1.0, 0.0).astype(jnp.bfloat16)
        fragment_list = fragment_list * weight[:, None, None]
        row_lookup = lax.dynamic_slice_in_dim(range_to_row_weight, (band_index * ROWS_B).astype(jnp.int32), ROWS_B, 0)
        raised_output = jnp.einsum('lfw,ew->lfe', fragment_list.astype(jnp.float32), row_lookup.astype(jnp.float32))
        return raised_output.astype(jnp.bfloat16).reshape(PULSES, 2 * ROWS_B)
    lifted_all = lax.map(lift_band, band_ids)
    blended = jnp.zeros(lifted_all.shape, jnp.float32)
    for offset in range(2 * TAPS_K + 1):
        blended = blended + slow_taps[offset] * jnp.roll(lifted_all, TAPS_K - offset, axis=1).astype(jnp.float32)
    blended = blended.astype(jnp.bfloat16)
    flat_width = N_BAND * 2 * ROWS_B
    by_group = jnp.transpose(blended, (1, 0, 2)).reshape(N_APER, PULSES // N_APER, flat_width)
    ramp_groups = ramp_rate.reshape(N_APER, PULSES // N_APER)
    columns = jnp.arange(NCOLS, dtype=jnp.int32).astype(jnp.float32)

    def accumulate(running_total, group_block):
        blend_part, ramp_part = group_block
        phase_angle = ramp_part[:, None] * columns[None, :]
        cos_table = jnp.cos(phase_angle).astype(jnp.bfloat16)
        sin_table = jnp.sin(phase_angle).astype(jnp.bfloat16)
        cos_sum = running_total[0] + jnp.dot(cos_table.T, blend_part, preferred_element_type=jnp.float32)
        sin_sum = running_total[1] + jnp.dot(sin_table.T, blend_part, preferred_element_type=jnp.float32)
        return ((cos_sum, sin_sum), None)
    empty_sum = jnp.zeros((NCOLS, flat_width), jnp.float32)
    totals = lax.scan(accumulate, (empty_sum, empty_sum), (by_group, ramp_groups))[0]
    cos_sum = totals[0].reshape(NCOLS, N_BAND, 2, ROWS_B)
    sin_sum = totals[1].reshape(NCOLS, N_BAND, 2, ROWS_B)
    grad_real = cos_sum[:, :, 0] - sin_sum[:, :, 1]
    grad_imag = sin_sum[:, :, 0] + cos_sum[:, :, 1]
    gradient = jnp.stack([grad_real, grad_imag]).reshape(2, NCOLS, NROWS).transpose(0, 2, 1)
    gradient = gradient * (1.0 / math.sqrt(PULSES))
    padded = jnp.pad(image_now, ((0, 0), (1, 1), (1, 1)))
    return image_now - step_and_variation_weight[0] * (gradient + step_and_variation_weight[1] * variation_term(padded))
```

```python
import math

import jax
import jax.numpy as jnp
from jax import lax
from jax.experimental import pallas as pl
from jax.experimental.pallas import tpu as pltpu
from jax.sharding import PartitionSpec as P

TAPS_K = 2
LANES = 128
EDGE = 8
Z_HI, Z_LO, N_X, N_YC = 2, 8, 4, 8
N_Z = Z_HI * Z_LO
smooth_eps = 0.05
BF16, F32 = jnp.bfloat16, jnp.float32
VMEM = pl.BlockSpec(memory_space=pltpu.VMEM)
SMEM = pl.BlockSpec(memory_space=pltpu.SMEM)


def device_index(z_hi, z_lo, x, yc):
    return ((z_lo * N_X + x) * Z_HI + z_hi) * N_YC + yc


def z_rings():
    return [
        [device_index(z // Z_LO, z % Z_LO, x, yc) for z in range(N_Z)]
        for x in range(N_X)
        for yc in range(N_YC)
    ]


def mirrored():
    return [
        (device_index(h, z, x, yc), device_index(1 - h, Z_LO - 1 - z, x, yc))
        for h in range(Z_HI)
        for z in range(Z_LO)
        for x in range(N_X)
        for yc in range(N_YC)
    ]


def extended(value, sides, width, wrap):
    for axis, dim in sides:
        size, length = (lax.axis_size(axis), value.shape[dim])
        up = [(i, (i + 1) % size) for i in range(size if wrap else size - 1)]
        down = [(j, i) for i, j in up]
        last = lax.slice_in_dim(value, length - width, length, axis=dim)
        leading = lax.slice_in_dim(value, 0, width, axis=dim)
        before = lax.ppermute(last, axis, up)
        after = lax.ppermute(leading, axis, down)
        value = jnp.concatenate([before, value, after], axis=dim)
    return value


def variation_term(padded):
    row_step = padded[:, 1:, :-1] - padded[:, :-1, :-1]
    col_step = padded[:, :-1, 1:] - padded[:, :-1, :-1]
    magnitude = jnp.sqrt(jnp.sum(row_step * row_step + col_step * col_step, axis=0) + smooth_eps)
    row_flow = row_step / magnitude
    col_flow = col_step / magnitude
    return -(
        row_flow[:, 1:, 1:] - row_flow[:, :-1, 1:] + col_flow[:, 1:, 1:] - col_flow[:, 1:, :-1]
    )


def cut_windows(start_ref, foot_ref, pulse_ref, out_ref, flat_ref, window_ref):
    comps, pulses, bins = pulse_ref.shape
    parts = bins // LANES
    pitch = comps * (parts + 1)
    block = out_ref.shape[0] * out_ref.shape[1] // (Z_HI * N_YC)
    for part in range(parts):
        for comp in range(comps):
            flat_ref[pl.ds(part * comps + comp, pulses, stride=pitch), :] = pulse_ref[
                comp, :, part * LANES : (part + 1) * LANES
            ].astype(F32)
    window_ref[...] = jnp.zeros_like(window_ref)
    lane = lax.broadcasted_iota(jnp.int32, (block // pulses, LANES), 1)
    for pulse in range(pulses):
        for k in range(foot_ref.shape[1]):
            band = foot_ref[pulse, k]
            start = start_ref[pulse, band]
            row = pulse * pitch + comps * (start // LANES)
            shift = start % LANES
            here = flat_ref[pl.ds(row, block // pulses), :]
            following = flat_ref[pl.ds(row + comps, block // pulses), :]
            both = jnp.where(lane >= shift, here, following)
            both = pltpu.roll(both, (LANES - shift) % LANES, 1)
            place = ((band % N_YC) * Z_HI + band // N_YC) * block + pulse
            window_ref[pl.ds(place, block // pulses, stride=pulses), :] = both
    out_ref[...] = window_ref[...].astype(BF16).reshape(out_ref.shape)


def lift_windows(where_ref, window_ref, own_ref, other_ref, out_ref):
    sources, height = window_ref.shape[:2]
    half = height // Z_HI
    parts = own_ref.shape[1] // LANES
    rows = half // parts
    band_rows = own_ref.shape[0]
    my_half = where_ref[0]
    dims = (((1,), (1,)), ((), ()))
    for weight_ref, z_half in ((own_ref, my_half), (other_ref, 1 - my_half)):
        lifted = jnp.zeros((sources * rows, band_rows), F32)
        for part in range(parts):
            first = pl.multiple_of(z_half * half + part * rows, rows)
            piece = window_ref[:, pl.ds(first, rows), :].reshape(sources * rows, LANES)
            lifted = lifted + lax.dot_general(
                piece,
                weight_ref[:, part * LANES : (part + 1) * LANES],
                dims,
                preferred_element_type=F32,
            )
        lifted = lifted.reshape(sources, 2, rows // 2, band_rows)
        both = jnp.concatenate([lifted[:, 0], lifted[:, 1]], axis=-1)
        both = both.reshape(sources * rows // 2, 2 * band_rows).astype(BF16)
        for z in range(Z_LO):
            out_ref[z_half * Z_LO + z] = both


def sin_cos(angle):
    turns = jnp.round(angle * (2.0 / math.pi))
    rest = angle - turns * 1.5703125
    rest = rest - turns * 4.837512969970703125e-4
    rest = rest - turns * 7.54978995489188216e-8
    square = rest * rest
    sine = -1.9515295891e-4 * square + 8.3321608736e-3
    sine = (sine * square - 1.6666654611e-1) * square * rest + rest
    cosine = 2.443315711809948e-5 * square - 1.388731625493765e-3
    cosine = (cosine * square + 4.166664568298827e-2) * square * square - 0.5 * square + 1.0
    quarter = turns.astype(jnp.int32) & 3
    swap = (quarter & 1) == 1
    sin_out = jnp.where(swap, cosine, sine)
    cos_out = jnp.where(swap, sine, cosine)
    sin_out = jnp.where(quarter >= 2, -sin_out, sin_out)
    cos_out = jnp.where((quarter == 1) | (quarter == 2), -cos_out, cos_out)
    return sin_out, cos_out


FINE = 16


def sum_pulses(
    where_ref, taps_ref, ramp_ref, lifted_ref, out_ref, table_ref, rate_ref, pad_ref, blend_ref, fine_ref, coarse_ref
):
    z_lo, x = where_ref[1], where_ref[2]
    n_groups = ramp_ref.shape[0]
    half_pulses, width = lifted_ref.shape[1:]
    main = Z_LO * LANES
    depth = main + LANES
    blocks, columns = out_ref.shape[:2]

    lane = lax.broadcasted_iota(jnp.int32, (1, LANES), 1)
    ends = jnp.zeros((1, LANES), F32)
    for i in range(Z_LO):
        group = i * N_X + x
        rate_ref[i : i + 1, :] = ramp_ref[pl.ds(group, 1), :]
        before = ramp_ref[pl.ds((group + n_groups - 1) % n_groups, 1), :]
        after = ramp_ref[pl.ds((group + 1) % n_groups, 1), :]
        place = 2 * EDGE * i
        move = (place + EDGE) % LANES
        before = pltpu.roll(before, move, 1) if move else before
        after = pltpu.roll(after, move, 1) if move else after
        ends = jnp.where((lane >= place) & (lane < place + EDGE), before, ends)
        ends = jnp.where((lane >= place + EDGE) & (lane < place + 2 * EDGE), after, ends)
    rate_ref[Z_LO : Z_LO + 1, :] = ends

    zero = jnp.zeros((2 * EDGE, width), F32)
    pad_ref[: 2 * EDGE] = zero
    pad_ref[2 * EDGE + LANES :] = zero
    for i in range(Z_LO):
        for h in range(Z_HI):
            pad_ref[pl.ds(2 * EDGE + h * half_pulses, half_pulses), :] = lifted_ref[
                h * Z_LO + i
            ].astype(F32)
        blended = jnp.zeros((LANES + 2 * EDGE, width), F32)
        for t in range(2 * TAPS_K + 1):
            blended = blended + taps_ref[t] * pad_ref[pl.ds(EDGE - TAPS_K + t, LANES + 2 * EDGE), :]
        turned = pltpu.roll(blended, width // 2, 1)
        lane_full = lax.broadcasted_iota(jnp.int32, blended.shape, 1)
        turned = jnp.where(lane_full < width // 2, -turned, turned)
        for k, value in enumerate((blended, turned)):
            value = value.astype(BF16)
            blend_ref[pl.ds(k * depth + i * LANES, LANES), :] = value[EDGE : EDGE + LANES]
            outside = jnp.concatenate([value[:EDGE], value[EDGE + LANES :]], axis=0)
            blend_ref[pl.ds(k * depth + main + i * 2 * EDGE, 2 * EDGE), :] = outside

    n_coarse = blocks * columns // FINE
    first = z_lo * (blocks * columns)
    fine_step = lax.broadcasted_iota(jnp.int32, (FINE, LANES), 0).astype(F32)
    coarse_step = (
        first + FINE * lax.broadcasted_iota(jnp.int32, (n_coarse, LANES), 0)
    ).astype(F32)
    for i in range(Z_LO + 1):
        rate = rate_ref[i : i + 1, :]
        fine_sin, fine_cos = sin_cos(rate * fine_step)
        coarse_sin, coarse_cos = sin_cos(rate * coarse_step)
        coarse_ref[0] = coarse_sin
        coarse_ref[1] = coarse_cos
        for a in range(n_coarse):
            s = coarse_ref[0, a : a + 1, :]
            c = coarse_ref[1, a : a + 1, :]
            table_ref[a * FINE : (a + 1) * FINE, i * LANES : (i + 1) * LANES] = (
                c * fine_cos - s * fine_sin
            ).astype(BF16)
            table_ref[a * FINE : (a + 1) * FINE, depth + i * LANES : depth + (i + 1) * LANES] = (
                s * fine_cos + c * fine_sin
            ).astype(BF16)

    for block in range(blocks):
        out_ref[block] = jnp.dot(
            table_ref[block * columns : (block + 1) * columns, :],
            blend_ref[...],
            preferred_element_type=F32,
        )


def finish(scale, step_ref, sums_ref, base_ref, out_ref):
    total = sums_ref[0]
    for k in range(1, sums_ref.shape[0]):
        total = total + sums_ref[k]
    total = total.T * (step_ref[0] * scale)
    out_ref[...] = base_ref[...] - total.reshape(out_ref.shape)


def call(kernel, out_shape, in_specs, args, scratch=(), out_specs=VMEM):
    return pl.pallas_call(
        kernel,
        out_shape=out_shape,
        in_specs=in_specs,
        out_specs=out_specs,
        scratch_shapes=scratch,
        compiler_params=pltpu.CompilerParams(vmem_limit_bytes=40 * 1024 * 1024),
    )(*args)


def local(
    pulse_data,
    window_start,
    footprint,
    range_to_row_weight,
    slow_taps,
    ramp_rate,
    image_now,
    step_and_variation_weight,
):
    band_count = lax.axis_size("band")
    groups = lax.axis_size("aper")
    comps, pulses, bins = pulse_data.shape
    band_rows, window_len = range_to_row_weight.shape
    columns = image_now.shape[2]
    group = lax.axis_index("aper")
    z_hi = lax.axis_index("band") // N_YC
    where = jnp.stack([z_hi, group // N_X, group % N_X]).astype(jnp.int32)

    other_weight = lax.ppermute(range_to_row_weight, ("aper", "band"), mirrored())
    parts = window_len // LANES
    block = parts * comps * pulses
    windows = call(
        cut_windows,
        jax.ShapeDtypeStruct((N_YC, Z_HI * block, LANES), BF16),
        [SMEM, SMEM, VMEM],
        (window_start, footprint, pulse_data),
        [
            pltpu.VMEM((pulses * comps * (bins // LANES + 1), LANES), F32),
            pltpu.VMEM((band_count * block, LANES), F32),
        ],
    )
    in_plane = [[h * N_YC + i for i in range(N_YC)] for h in range(Z_HI)]
    windows = lax.all_to_all(windows, "band", 0, 0, axis_index_groups=in_plane, tiled=True)
    width = comps * band_rows
    lifted = call(
        lift_windows,
        jax.ShapeDtypeStruct((N_Z, N_YC * pulses, width), BF16),
        [SMEM, VMEM, VMEM, VMEM],
        (where, windows, range_to_row_weight, other_weight),
    )
    lifted = lax.all_to_all(lifted, ("aper", "band"), 0, 0, axis_index_groups=z_rings(), tiled=True)
    depth = (Z_LO + 1) * LANES
    sums = call(
        sum_pulses,
        jax.ShapeDtypeStruct((N_X, columns, width), F32),
        [SMEM, SMEM, VMEM, VMEM],
        (where, slow_taps, ramp_rate.reshape(groups, LANES), lifted),
        [
            pltpu.VMEM((N_X * columns, 2 * depth), BF16),
            pltpu.VMEM((2 * EDGE, LANES), F32),
            pltpu.VMEM((LANES + 4 * EDGE, width), F32),
            pltpu.VMEM((2 * depth, width), BF16),
            pltpu.VMEM((FINE, LANES), F32),
            pltpu.VMEM((2, N_X * columns // FINE, LANES), F32),
        ],
    )
    along_x = [[z * N_X + x for x in range(N_X)] for z in range(Z_LO)]
    sums = lax.all_to_all(sums, "aper", 0, 0, axis_index_groups=along_x, tiled=True)

    padded_image = extended(image_now, (("band", 1), ("aper", 2)), 1, False)
    base = image_now - step_and_variation_weight[0] * (
        step_and_variation_weight[1] * variation_term(padded_image)
    )
    scale = 1.0 / math.sqrt(groups * LANES)
    return call(
        lambda *refs: finish(scale, *refs),
        jax.ShapeDtypeStruct(image_now.shape, F32),
        [SMEM, VMEM, VMEM],
        (step_and_variation_weight, sums, base),
    )


def solution(mesh):
    return jax.shard_map(
        local,
        mesh=mesh,
        in_specs=(
            P(None, ("aper", "band"), None),
            P(("aper", "band"), None),
            P(("aper", "band"), None),
            P("band", None),
            P(),
            P(),
            P(None, "band", "aper"),
            P(),
        ),
        out_specs=P(None, "band", "aper"),
        check_vma=False,
    )
```

```python
import math

import jax
import jax.numpy as jnp
from jax import lax
from jax.experimental import pallas as pl
from jax.experimental.pallas import tpu as pltpu
from jax.sharding import PartitionSpec as P

TAPS_K = 2
LANES = 128
EDGE = 8
Z_HI, Z_LO, N_X, N_YC = 2, 8, 4, 8
N_Z = Z_HI * Z_LO
smooth_eps = 0.05
BF16, F32 = jnp.bfloat16, jnp.float32
VMEM = pl.BlockSpec(memory_space=pltpu.VMEM)
SMEM = pl.BlockSpec(memory_space=pltpu.SMEM)
ANY = pl.BlockSpec(memory_space=pl.ANY)


def device_index(z_hi, z_lo, x, yc):
    return ((z_lo * N_X + x) * Z_HI + z_hi) * N_YC + yc


def z_rings():
    return [
        [device_index(z // Z_LO, z % Z_LO, x, yc) for z in range(N_Z)]
        for x in range(N_X)
        for yc in range(N_YC)
    ]


def halves_swapped():
    return [
        (device_index(h, z, x, yc), device_index(1 - h, (z + Z_LO // 2) % Z_LO, x, yc))
        for h in range(Z_HI)
        for z in range(Z_LO)
        for x in range(N_X)
        for yc in range(N_YC)
    ]


def place_of():
    group, band = lax.axis_index("aper"), lax.axis_index("band")
    return band // N_YC, group // N_X, group % N_X, band % N_YC


def three_parts(value, spare_ref):
    first = value.astype(BF16).astype(F32)
    second = (value - first).astype(BF16).astype(F32)
    spare_ref[0:4] = first
    spare_ref[4:8] = second
    spare_ref[8:12] = value - first - second
    spare_ref[12:16] = jnp.zeros_like(value)
    return spare_ref[...].astype(BF16)


def joined(rows):
    rows = rows.astype(F32)
    return rows[0:4] + rows[4:8] + rows[8:12]


TOP, LOW = EDGE - 1, EDGE + 64


def with_corners(columns, above, below):
    lane = lax.broadcasted_iota(jnp.int32, columns.shape, 1)
    row = lax.broadcasted_iota(jnp.int32, columns.shape, 0)
    above = pltpu.roll(above, TOP, 1)
    below = pltpu.roll(below, (LOW + 1) % LANES, 1)
    for comp in range(2):
        columns = jnp.where((lane == TOP) & (row == comp), above[2 * comp : 2 * comp + 1], columns)
        columns = jnp.where(
            (lane == LOW) & (row == 2 + comp), below[2 * comp + 1 : 2 * comp + 2], columns
        )
    return columns


def cut_windows(
    start_hbm,
    foot_hbm,
    pulse_hbm,
    image_hbm,
    out_ref,
    start_ref,
    foot_ref,
    pulse_ref,
    edge_ref,
    flat_ref,
    window_ref,
    spare_ref,
    sem,
):
    rows = image_hbm.shape[1]
    copies = [
        pltpu.make_async_copy(pulse_hbm, pulse_ref, sem.at[0]),
        pltpu.make_async_copy(start_hbm, start_ref, sem.at[1]),
        pltpu.make_async_copy(foot_hbm, foot_ref, sem.at[2]),
        pltpu.make_async_copy(image_hbm.at[:, pl.ds(0, EDGE), :], edge_ref.at[0], sem.at[3]),
        pltpu.make_async_copy(image_hbm.at[:, pl.ds(rows - EDGE, EDGE), :], edge_ref.at[1], sem.at[4]),
    ]
    for copy in copies:
        copy.start()
    window_ref[...] = jnp.zeros_like(window_ref)
    comps, pulses, bins = pulse_ref.shape
    parts = bins // LANES
    pitch = comps * (parts + 1)
    block = window_ref.shape[0] // (Z_HI * N_YC)
    for copy in copies:
        copy.wait()
    for part in range(parts):
        for comp in range(comps):
            flat_ref[pl.ds(part * comps + comp, pulses, stride=pitch), :] = pulse_ref[
                comp, :, part * LANES : (part + 1) * LANES
            ].astype(F32)
    lane = lax.broadcasted_iota(jnp.int32, (block // pulses, LANES), 1)
    for pulse in range(pulses):
        for k in range(foot_ref.shape[1]):
            band = foot_ref[pulse, k]
            start = start_ref[pulse, band]
            row = pulse * pitch + comps * (start >> 7)
            shift = start & (LANES - 1)
            here = flat_ref[pl.ds(row, block // pulses), :]
            following = flat_ref[pl.ds(row + comps, block // pulses), :]
            both = jnp.where(lane >= shift, here, following)
            both = pltpu.roll(both, (LANES - shift) & (LANES - 1), 1)
            place = ((band & (N_YC - 1)) * Z_HI + (band >> 3)) * block + pulse
            window_ref[pl.ds(place, block // pulses, stride=pulses), :] = both
    tall = Z_HI * block
    out_ref[:, :tall, :] = window_ref[...].astype(BF16).reshape(N_YC, tall, LANES)
    out_ref[:, tall:, :] = jnp.zeros((N_YC, 2 * EDGE, LANES), BF16)
    yc = place_of()[3]
    for side, line, to in ((0, 0, yc + N_YC - 1), (1, EDGE - 1, yc + 1)):
        edge = [edge_ref[side, comp, line : line + 1, :] for comp in range(comps)]
        edge = [e[:, i * LANES : (i + 1) * LANES] for e in edge for i in range(2)]
        out_ref[to % N_YC, tall:, :] = three_parts(jnp.concatenate(edge, axis=0), spare_ref)


def side_columns(image_ref, out_ref, pad_ref):
    rows, columns = image_ref.shape[1:]
    pad_ref[...] = jnp.zeros_like(pad_ref)
    out_ref[...] = jnp.zeros_like(out_ref)
    for comp in range(2):
        for side, line in ((0, 0), (1, LANES - 1)):
            pad_ref[EDGE : EDGE + rows, :] = image_ref[
                comp, :, side * (columns - LANES) : side * (columns - LANES) + LANES
            ]
            out_ref[2 * side + comp : 2 * side + comp + 1, :] = pad_ref[...].T[line : line + 1, :]


def lift_windows(
    window_ref, own_ref, other_ref, column_ref, out_ref, edge_ref, spare_ref
):
    z_hi, _, _, yc = place_of()
    sources, height = window_ref.shape[0], window_ref.shape[1] - 2 * EDGE
    half = height // Z_HI
    parts = own_ref.shape[1] // LANES
    rows = half // parts
    band_rows = own_ref.shape[0]
    tall = sources * rows // 2

    above = joined(window_ref[(yc + N_YC - 1) % N_YC, height:, :])
    below = joined(window_ref[(yc + 1) % N_YC, height:, :])
    foreign = jnp.where(yc == 0, above, below)
    above = jnp.where(yc > 0, above, jnp.zeros_like(above))
    below = jnp.where(yc < N_YC - 1, below, jnp.zeros_like(below))
    edge_ref[0:4] = above
    edge_ref[4:8] = below
    columns = with_corners(column_ref[0:4], above, below)

    dims = (((1,), (1,)), ((), ()))
    for weight_ref, z_half, extra in ((own_ref, z_hi, columns), (other_ref, 1 - z_hi, foreign)):
        lifted = jnp.zeros((sources * rows, band_rows), F32)
        for part in range(parts):
            first = pl.multiple_of(z_half * half + part * rows, rows)
            piece = window_ref[:, pl.ds(first, rows), :].reshape(sources * rows, LANES)
            lifted = lifted + lax.dot_general(
                piece,
                weight_ref[:, part * LANES : (part + 1) * LANES],
                dims,
                preferred_element_type=F32,
            )
        lifted = lifted.reshape(sources, 2, rows // 2, band_rows)
        both = jnp.concatenate([lifted[:, 0], lifted[:, 1]], axis=-1)
        both = both.reshape(tall, 2 * band_rows).astype(BF16)
        extra = three_parts(extra, spare_ref)
        for z in range(Z_LO):
            out_ref[z_half * Z_LO + z, :tall, :] = both
            out_ref[z_half * Z_LO + z, tall:, :] = extra


def sin_cos(angle):
    turns = jnp.round(angle * (2.0 / math.pi))
    rest = angle - turns * 1.5703125
    rest = rest - turns * 4.837512969970703125e-4
    rest = rest - turns * 7.54978995489188216e-8
    square = rest * rest
    sine = -1.9515295891e-4 * square + 8.3321608736e-3
    sine = (sine * square - 1.6666654611e-1) * square * rest + rest
    cosine = 2.443315711809948e-5 * square - 1.388731625493765e-3
    cosine = (cosine * square + 4.166664568298827e-2) * square * square - 0.5 * square + 1.0
    quarter = turns.astype(jnp.int32) & 3
    swap = (quarter & 1) == 1
    sin_out = jnp.where(swap, cosine, sine)
    cos_out = jnp.where(swap, sine, cosine)
    sin_out = jnp.where(quarter >= 2, -sin_out, sin_out)
    cos_out = jnp.where((quarter == 1) | (quarter == 2), -cos_out, cos_out)
    return sin_out, cos_out


FINE = 16


def make_table(after_ref, ramp_ref, taps_ref, table_ref, tap_rows_ref, rate_ref, coarse_ref):
    del after_ref
    _, z_lo, x, _ = place_of()
    n_groups = ramp_ref.shape[0]
    depth = table_ref.shape[1] // 2
    for t in range(2 * TAPS_K + 1):
        tap_rows_ref[t : t + 1, :] = jnp.full((1, LANES), taps_ref[t], F32)

    lane = lax.broadcasted_iota(jnp.int32, (1, LANES), 1)
    ends = jnp.zeros((1, LANES), F32)
    for i in range(Z_LO):
        group = i * N_X + x
        rate_ref[i : i + 1, :] = ramp_ref[pl.ds(group, 1), :]
        before = ramp_ref[pl.ds((group + n_groups - 1) % n_groups, 1), :]
        after = ramp_ref[pl.ds((group + 1) % n_groups, 1), :]
        place = 2 * EDGE * i
        move = (place + EDGE) % LANES
        before = pltpu.roll(before, move, 1) if move else before
        after = pltpu.roll(after, move, 1) if move else after
        ends = jnp.where((lane >= place) & (lane < place + EDGE), before, ends)
        ends = jnp.where((lane >= place + EDGE) & (lane < place + 2 * EDGE), after, ends)
    rate_ref[Z_LO : Z_LO + 1, :] = ends

    n_coarse = table_ref.shape[0] // FINE
    first = z_lo * table_ref.shape[0]
    fine_step = lax.broadcasted_iota(jnp.int32, (FINE, LANES), 0).astype(F32)
    coarse_step = (
        first + FINE * lax.broadcasted_iota(jnp.int32, (n_coarse, LANES), 0)
    ).astype(F32)
    for i in range(Z_LO + 1):
        rate = rate_ref[i : i + 1, :]
        fine_sin, fine_cos = sin_cos(rate * fine_step)
        coarse_sin, coarse_cos = sin_cos(rate * coarse_step)
        coarse_ref[0] = coarse_sin
        coarse_ref[1] = coarse_cos
        for a in range(n_coarse):
            s = coarse_ref[0, a : a + 1, :]
            c = coarse_ref[1, a : a + 1, :]
            table_ref[a * FINE : (a + 1) * FINE, i * LANES : (i + 1) * LANES] = (
                c * fine_cos - s * fine_sin
            ).astype(BF16)
            table_ref[a * FINE : (a + 1) * FINE, depth + i * LANES : depth + (i + 1) * LANES] = (
                s * fine_cos + c * fine_sin
            ).astype(BF16)


def sum_pulses(
    tap_rows_ref, table_ref, lifted_ref, column_ref, edge_ref, out_ref, edge_out_ref, pad_ref, blend_ref
):
    z_hi, z_lo, x, yc = place_of()
    width = lifted_ref.shape[2]
    half_pulses = LANES // Z_HI
    main = Z_LO * LANES
    depth = main + LANES
    blocks, columns = out_ref.shape[0], out_ref.shape[1] - EDGE

    zero = jnp.zeros((2 * EDGE, width), F32)
    pad_ref[: 2 * EDGE] = zero
    pad_ref[2 * EDGE + LANES :] = zero
    for i in range(Z_LO):
        for h in range(Z_HI):
            pad_ref[pl.ds(2 * EDGE + h * half_pulses, half_pulses), :] = lifted_ref[
                h * Z_LO + i, :half_pulses, :
            ].astype(F32)
        blended = jnp.zeros((LANES + 2 * EDGE, width), F32)
        for t in range(2 * TAPS_K + 1):
            blended = blended + tap_rows_ref[t : t + 1, :] * pad_ref[
                pl.ds(EDGE - TAPS_K + t, LANES + 2 * EDGE), :
            ]
        turned = pltpu.roll(blended, width // 2, 1)
        lane_full = lax.broadcasted_iota(jnp.int32, blended.shape, 1)
        turned = jnp.where(lane_full < width // 2, -turned, turned)
        for k, value in enumerate((blended, turned)):
            value = value.astype(BF16)
            blend_ref[pl.ds(k * depth + i * LANES, LANES), :] = value[EDGE : EDGE + LANES]
            outside = jnp.concatenate([value[:EDGE], value[EDGE + LANES :]], axis=0)
            blend_ref[pl.ds(k * depth + main + i * 2 * EDGE, 2 * EDGE), :] = outside

    for block in range(blocks):
        out_ref[block, :columns, :] = jnp.dot(
            table_ref[block * columns : (block + 1) * columns, :],
            blend_ref[...],
            preferred_element_type=F32,
        )

    def came(half, z):
        return joined(lifted_ref[half * Z_LO + z % Z_LO, half_pulses:, :])

    first_band = (z_hi == 1) & (yc == 0)
    last_band = (z_hi == 0) & (yc == N_YC - 1)
    foreign = came(1 - z_hi, z_lo)
    above = jnp.where(first_band, foreign, edge_ref[0:4])
    below = jnp.where(last_band, foreign, edge_ref[4:8])
    edge_out_ref[0:4] = above
    edge_out_ref[4:8] = below
    own = with_corners(column_ref[0:4], above, below)
    left = came(z_hi, z_lo + Z_LO - 1)
    left_fixed = with_corners(left, above, came(1 - z_hi, z_lo + Z_LO - 1))
    left = jnp.where(last_band, left_fixed, left)
    right = came(z_hi, z_lo + 1)
    right_fixed = with_corners(right, came(1 - z_hi, z_lo + 1), below)
    right = jnp.where(first_band, right_fixed, right)
    out_ref[:, columns:, :] = jnp.zeros((blocks, EDGE, LANES), F32)
    out_ref[(x + 1) % N_X, columns : columns + 2, :] = jnp.where(x < N_X - 1, own, left)[2:4]
    out_ref[(x + N_X - 1) % N_X, columns : columns + 2, :] = jnp.where(x > 0, own, right)[0:2]


def finish(scale, step_ref, sums_ref, edge_ref, image_ref, out_ref, pad_ref, side_ref, flow_ref):
    _, z_lo, x, _ = place_of()
    group = z_lo * N_X + x
    comps, rows, columns = image_ref.shape
    tall = pad_ref.shape[1]
    total = sums_ref[0, :columns, :]
    for k in range(1, N_X):
        total = total + sums_ref[k, :columns, :]
    total = total.T.reshape(image_ref.shape) * scale

    zero = jnp.zeros((2, LANES), F32)
    left = sums_ref[(x + N_X - 1) % N_X, columns : columns + 2, :]
    right = sums_ref[(x + 1) % N_X, columns : columns + 2, :]
    side_ref[...] = jnp.zeros_like(side_ref)
    side_ref[0:2, :] = jnp.where(group > 0, left, zero)
    side_ref[2:4, :] = jnp.where(group < Z_LO * N_X - 1, right, zero)
    sides = side_ref[...].T[:tall]
    lane = lax.broadcasted_iota(jnp.int32, (tall, LANES), 1)
    blank = jnp.zeros((tall, LANES), F32)
    pad_ref[...] = jnp.zeros_like(pad_ref)
    for comp in range(comps):
        pad_ref[comp, EDGE : EDGE + rows, LANES : LANES + columns] = image_ref[comp]
        for half in range(2):
            span = pl.ds((1 + half) * LANES, LANES)
            pad_ref[comp, TOP : TOP + 1, span] = edge_ref[2 * comp + half : 2 * comp + half + 1, :]
            pad_ref[comp, LOW : LOW + 1, span] = edge_ref[4 + 2 * comp + half : 5 + 2 * comp + half, :]
        pad_ref[comp, :, :LANES] = jnp.where(lane == LANES - 1, sides[:, comp : comp + 1], blank)
        pad_ref[comp, :, LANES + columns :] = jnp.where(
            lane == 0, sides[:, 2 + comp : 3 + comp], blank
        )

    high, wide = rows + EDGE, columns + LANES
    row_step, col_step = [], []
    square = jnp.zeros((high, wide), F32) + smooth_eps
    for comp in range(comps):
        here = pad_ref[comp, :high, :]
        following = pltpu.roll(here, here.shape[1] - 1, 1)[:, :wide]
        here = here[:, :wide]
        row_step.append(pad_ref[comp, 1 : high + 1, :wide] - here)
        col_step.append(following - here)
        square = square + row_step[-1] * row_step[-1] + col_step[-1] * col_step[-1]
    inverse = lax.rsqrt(square)
    step, weight = step_ref[0], step_ref[1]
    for comp in range(comps):
        row_flow = row_step[comp] * inverse
        col_flow = col_step[comp] * inverse
        flow_ref[...] = row_flow
        across = col_flow - pltpu.roll(col_flow, 1, 1)
        down = row_flow[EDGE:, LANES:] - flow_ref[EDGE - 1 : high - 1, LANES:]
        variation = -(down + across[EDGE:, LANES:])
        out_ref[comp] = image_ref[comp] - step * (total[comp] + weight * variation)


def call(kernel, out_shape, in_specs, args, scratch=(), cost=None):
    out_specs = jax.tree.map(lambda _: VMEM, out_shape)
    return pl.pallas_call(
        kernel,
        out_shape=out_shape,
        in_specs=in_specs,
        out_specs=out_specs,
        scratch_shapes=scratch,
        cost_estimate=cost,
        compiler_params=pltpu.CompilerParams(vmem_limit_bytes=16 * 1024 * 1024),
    )(*args)


def local(
    pulse_data,
    window_start,
    footprint,
    range_to_row_weight,
    slow_taps,
    ramp_rate,
    image_now,
    step_and_variation_weight,
):
    band_count = lax.axis_size("band")
    groups = lax.axis_size("aper")
    comps, pulses, bins = pulse_data.shape
    band_rows, window_len = range_to_row_weight.shape
    columns = image_now.shape[2]
    shape = jax.ShapeDtypeStruct

    other_weight = lax.ppermute(range_to_row_weight, ("aper", "band"), halves_swapped())
    block = window_len // LANES * comps * pulses
    windows = call(
        cut_windows,
        shape((N_YC, Z_HI * block + 2 * EDGE, LANES), BF16),
        [ANY, ANY, ANY, ANY],
        (window_start, footprint, pulse_data, image_now),
        [
            pltpu.SMEM(window_start.shape, jnp.int32),
            pltpu.SMEM(footprint.shape, jnp.int32),
            pltpu.VMEM(pulse_data.shape, BF16),
            pltpu.VMEM((2, comps, EDGE, columns), F32),
            pltpu.VMEM((pulses * comps * (bins // LANES + 1), LANES), F32),
            pltpu.VMEM((band_count * block, LANES), F32),
            pltpu.VMEM((2 * EDGE, LANES), F32),
            pltpu.SemaphoreType.DMA((5,)),
        ],
    )
    in_plane = [[h * N_YC + i for i in range(N_YC)] for h in range(Z_HI)]
    windows = lax.all_to_all(windows, "band", 0, 0, axis_index_groups=in_plane, tiled=True)
    side = call(
        side_columns,
        shape((EDGE, LANES), F32),
        [VMEM],
        (image_now,),
        [pltpu.VMEM((LANES, LANES), F32)],
        pl.CostEstimate(flops=1 << 20, bytes_accessed=1 << 17, transcendentals=0),
    )
    width = comps * band_rows
    lifted, edges = call(
        lift_windows,
        (
            shape((N_Z, N_YC * pulses + 2 * EDGE, width), BF16),
            shape((EDGE, LANES), F32),
        ),
        [VMEM, VMEM, VMEM, VMEM],
        (windows, range_to_row_weight, other_weight, side),
        [pltpu.VMEM((2 * EDGE, LANES), F32)],
    )
    lifted = lax.all_to_all(lifted, ("aper", "band"), 0, 0, axis_index_groups=z_rings(), tiled=True)
    depth = (Z_LO + 1) * LANES
    table, tap_rows = call(
        make_table,
        (shape((N_X * columns, 2 * depth), BF16), shape((EDGE, LANES), F32)),
        [ANY, VMEM, SMEM],
        (edges, ramp_rate.reshape(groups, LANES), slow_taps),
        [
            pltpu.VMEM((2 * EDGE, LANES), F32),
            pltpu.VMEM((2, N_X * columns // FINE, LANES), F32),
        ],
        pl.CostEstimate(flops=1 << 24, bytes_accessed=1 << 23, transcendentals=0),
    )
    sums, edges = call(
        sum_pulses,
        (shape((N_X, columns + EDGE, width), F32), shape((EDGE, LANES), F32)),
        [VMEM, VMEM, VMEM, VMEM, VMEM],
        (tap_rows, table, lifted, side, edges),
        [
            pltpu.VMEM((LANES + 4 * EDGE, width), F32),
            pltpu.VMEM((2 * depth, width), BF16),
        ],
    )
    along_x = [[z * N_X + x for x in range(N_X)] for z in range(Z_LO)]
    sums = lax.all_to_all(sums, "aper", 0, 0, axis_index_groups=along_x, tiled=True)
    scale = 1.0 / math.sqrt(groups * LANES)
    return call(
        lambda *refs: finish(scale, *refs),
        shape(image_now.shape, F32),
        [SMEM, VMEM, VMEM, VMEM],
        (step_and_variation_weight, sums, edges, image_now),
        [
            pltpu.VMEM((comps, band_rows + 2 * EDGE, columns + 2 * LANES), F32),
            pltpu.VMEM((LANES, LANES), F32),
            pltpu.VMEM((band_rows + EDGE, columns + LANES), F32),
        ],
    )


def solution(mesh):
    return jax.shard_map(
        local,
        mesh=mesh,
        in_specs=(
            P(None, ("aper", "band"), None),
            P(("aper", "band"), None),
            P(("aper", "band"), None),
            P("band", None),
            P(),
            P(),
            P(None, "band", "aper"),
            P(),
        ),
        out_specs=P(None, "band", "aper"),
        check_vma=False,
    )
```

```python
import math

import jax
import jax.numpy as jnp
from jax import lax
from jax.experimental import pallas as pl
from jax.experimental.pallas import tpu as pltpu
from jax.sharding import PartitionSpec as P

TAPS_K = 2
LANES = 128
EDGE = 8
Z_HI, Z_LO, N_X, N_YC = 2, 8, 4, 8
N_Z = Z_HI * Z_LO
smooth_eps = 0.05
BF16, F32 = jnp.bfloat16, jnp.float32
VMEM = pl.BlockSpec(memory_space=pltpu.VMEM)
SMEM = pl.BlockSpec(memory_space=pltpu.SMEM)
ANY = pl.BlockSpec(memory_space=pl.ANY)
HBM = pl.BlockSpec(memory_space=pltpu.HBM)


def device_index(z_hi, z_lo, x, yc):
    return ((z_lo * N_X + x) * Z_HI + z_hi) * N_YC + yc


def z_rings():
    return [
        [device_index(z // Z_LO, z % Z_LO, x, yc) for z in range(N_Z)]
        for x in range(N_X)
        for yc in range(N_YC)
    ]


def halves_swapped():
    return [
        (device_index(h, z, x, yc), device_index(1 - h, (z + Z_LO // 2) % Z_LO, x, yc))
        for h in range(Z_HI)
        for z in range(Z_LO)
        for x in range(N_X)
        for yc in range(N_YC)
    ]


def place_of():
    group, band = lax.axis_index("aper"), lax.axis_index("band")
    return band // N_YC, group // N_X, group % N_X, band % N_YC


def two_parts(value, spare_ref):
    first = value.astype(BF16).astype(F32)
    spare_ref[0:4] = first
    spare_ref[4:8] = value - first
    return spare_ref[...].astype(BF16)


def joined(rows):
    rows = rows.astype(F32)
    return rows[0:4] + rows[4:8]


TOP, LOW = EDGE - 1, EDGE + 64


def with_corners(columns, above, below):
    lane = lax.broadcasted_iota(jnp.int32, columns.shape, 1)
    row = lax.broadcasted_iota(jnp.int32, columns.shape, 0)
    above = pltpu.roll(above, TOP, 1)
    below = pltpu.roll(below, (LOW + 1) % LANES, 1)
    for comp in range(2):
        columns = jnp.where((lane == TOP) & (row == comp), above[2 * comp : 2 * comp + 1], columns)
        columns = jnp.where(
            (lane == LOW) & (row == 2 + comp), below[2 * comp + 1 : 2 * comp + 2], columns
        )
    return columns


def cut_windows(
    start_hbm,
    foot_hbm,
    pulse_hbm,
    image_hbm,
    out_ref,
    start_ref,
    foot_ref,
    pulse_ref,
    edge_ref,
    flat_ref,
    window_ref,
    spare_ref,
    sem,
):
    rows = image_hbm.shape[1]
    copies = [
        pltpu.make_async_copy(pulse_hbm, pulse_ref, sem.at[0]),
        pltpu.make_async_copy(start_hbm, start_ref, sem.at[1]),
        pltpu.make_async_copy(foot_hbm, foot_ref, sem.at[2]),
        pltpu.make_async_copy(image_hbm.at[:, pl.ds(0, EDGE), :], edge_ref.at[0], sem.at[3]),
        pltpu.make_async_copy(image_hbm.at[:, pl.ds(rows - EDGE, EDGE), :], edge_ref.at[1], sem.at[4]),
    ]
    for copy in copies:
        copy.start()
    window_ref[...] = jnp.zeros_like(window_ref)
    comps, pulses, bins = pulse_ref.shape
    parts = bins // LANES
    pitch = comps * (parts + 1)
    block = window_ref.shape[0] // (Z_HI * N_YC)
    for copy in copies:
        copy.wait()
    for part in range(parts):
        for comp in range(comps):
            flat_ref[pl.ds(part * comps + comp, pulses, stride=pitch), :] = pulse_ref[
                comp, :, part * LANES : (part + 1) * LANES
            ].astype(F32)
    lane = lax.broadcasted_iota(jnp.int32, (block // pulses, LANES), 1)
    for pulse in range(pulses):
        for k in range(foot_ref.shape[1]):
            band = foot_ref[pulse, k]
            start = start_ref[pulse, band]
            row = pulse * pitch + comps * (start >> 7)
            shift = start & (LANES - 1)
            here = flat_ref[pl.ds(row, block // pulses), :]
            following = flat_ref[pl.ds(row + comps, block // pulses), :]
            both = jnp.where(lane >= shift, here, following)
            both = pltpu.roll(both, (LANES - shift) & (LANES - 1), 1)
            place = ((band & (N_YC - 1)) * Z_HI + (band >> 3)) * block + pulse
            window_ref[pl.ds(place, block // pulses, stride=pulses), :] = both
    tall = Z_HI * block
    out_ref[:, :tall, :] = window_ref[...].astype(BF16).reshape(N_YC, tall, LANES)
    out_ref[:, tall:, :] = jnp.zeros((N_YC, EDGE, LANES), BF16)
    yc = place_of()[3]
    for side, line, to in ((0, 0, yc + N_YC - 1), (1, EDGE - 1, yc + 1)):
        edge = [edge_ref[side, comp, line : line + 1, :] for comp in range(comps)]
        edge = [e[:, i * LANES : (i + 1) * LANES] for e in edge for i in range(2)]
        out_ref[to % N_YC, tall:, :] = two_parts(jnp.concatenate(edge, axis=0), spare_ref)


def side_columns(image_hbm, weight_hbm, other_ref, out_ref, weight_ref, pad_ref, block_ref, sem):
    z_hi = place_of()[0]
    rows, columns = image_hbm.shape[1:]
    copies = [
        pltpu.make_async_copy(weight_hbm, weight_ref.at[z_hi], sem.at[0]),
        pltpu.make_async_copy(image_hbm.at[:, :, pl.ds(0, LANES)], block_ref.at[0], sem.at[1]),
        pltpu.make_async_copy(
            image_hbm.at[:, :, pl.ds(columns - LANES, LANES)], block_ref.at[1], sem.at[2]
        ),
    ]
    for copy in copies:
        copy.start()
    weight_ref[1 - z_hi] = other_ref[...]
    pad_ref[...] = jnp.zeros_like(pad_ref)
    out_ref[...] = jnp.zeros_like(out_ref)
    for copy in copies:
        copy.wait()
    for comp in range(2):
        for side, line in ((0, 0), (1, LANES - 1)):
            pad_ref[EDGE : EDGE + rows, :] = block_ref[side, comp]
            out_ref[2 * side + comp : 2 * side + comp + 1, :] = pad_ref[...].T[line : line + 1, :]


def lift_windows(
    window_ref, weight_ref, column_ref, out_ref, edge_ref, spare_ref
):
    z_hi, _, _, yc = place_of()
    sources, height = window_ref.shape[0], window_ref.shape[1] - EDGE
    half = height // Z_HI
    band_rows, window_len = weight_ref.shape[1:]
    parts = window_len // LANES
    rows = half // parts
    tall = sources * rows // 2

    above = joined(window_ref[(yc + N_YC - 1) % N_YC, height:, :])
    below = joined(window_ref[(yc + 1) % N_YC, height:, :])
    foreign = jnp.where(yc == 0, above, below)
    above = jnp.where(yc > 0, above, jnp.zeros_like(above))
    below = jnp.where(yc < N_YC - 1, below, jnp.zeros_like(below))
    edge_ref[0:4] = above
    edge_ref[4:8] = below
    columns = with_corners(column_ref[0:4], above, below)

    dims = (((1,), (1,)), ((), ()))
    for z_half in range(Z_HI):
        extra = jnp.where(z_half == z_hi, columns, foreign)
        lifted = jnp.zeros((sources * rows, band_rows), F32)
        for part in range(parts):
            first = z_half * half + part * rows
            piece = window_ref[:, pl.ds(first, rows), :].reshape(sources * rows, LANES)
            lifted = lifted + lax.dot_general(
                piece,
                weight_ref[z_half, :, part * LANES : (part + 1) * LANES],
                dims,
                preferred_element_type=F32,
            )
        lifted = lifted.reshape(sources, 2, rows // 2, band_rows)
        both = jnp.concatenate([lifted[:, 0], lifted[:, 1]], axis=-1)
        both = both.reshape(tall, 2 * band_rows).astype(BF16)
        extra = two_parts(extra, spare_ref)
        for z in range(Z_LO):
            out_ref[z_half * Z_LO + z, :tall, :] = both
            out_ref[z_half * Z_LO + z, tall:, :] = extra


def sin_cos(angle):
    turns = jnp.round(angle * (2.0 / math.pi))
    rest = angle - turns * 1.5703125
    rest = rest - turns * 4.837512969970703125e-4
    rest = rest - turns * 7.54978995489188216e-8
    square = rest * rest
    sine = -1.9515295891e-4 * square + 8.3321608736e-3
    sine = (sine * square - 1.6666654611e-1) * square * rest + rest
    cosine = 2.443315711809948e-5 * square - 1.388731625493765e-3
    cosine = (cosine * square + 4.166664568298827e-2) * square * square - 0.5 * square + 1.0
    quarter = turns.astype(jnp.int32) & 3
    swap = (quarter & 1) == 1
    sin_out = jnp.where(swap, cosine, sine)
    cos_out = jnp.where(swap, sine, cosine)
    sin_out = jnp.where(quarter >= 2, -sin_out, sin_out)
    cos_out = jnp.where((quarter == 1) | (quarter == 2), -cos_out, cos_out)
    return sin_out, cos_out


FINE = 16


def make_table(
    after_ref,
    ramp_hbm,
    taps_hbm,
    near_ref,
    far_hbm,
    tap_rows_ref,
    ramp_ref,
    taps_ref,
    far_ref,
    rate_ref,
    coarse_ref,
    sem,
):
    del after_ref
    copies = [
        pltpu.make_async_copy(ramp_hbm, ramp_ref, sem.at[0]),
        pltpu.make_async_copy(taps_hbm, taps_ref, sem.at[1]),
    ]
    for copy in copies:
        copy.start()
    _, z_lo, x, _ = place_of()
    n_groups = ramp_ref.shape[0]
    half, depth = near_ref.shape[0], near_ref.shape[1] // 2
    for copy in copies:
        copy.wait()
    for t in range(2 * TAPS_K + 1):
        tap_rows_ref[t : t + 1, :] = jnp.full((1, LANES), taps_ref[t], F32)

    lane = lax.broadcasted_iota(jnp.int32, (1, LANES), 1)
    ends = jnp.zeros((1, LANES), F32)
    for i in range(Z_LO):
        group = i * N_X + x
        rate_ref[i : i + 1, :] = ramp_ref[pl.ds(group, 1), :]
        before = ramp_ref[pl.ds((group + n_groups - 1) % n_groups, 1), :]
        after = ramp_ref[pl.ds((group + 1) % n_groups, 1), :]
        place = 2 * EDGE * i
        move = (place + EDGE) % LANES
        before = pltpu.roll(before, move, 1) if move else before
        after = pltpu.roll(after, move, 1) if move else after
        ends = jnp.where((lane >= place) & (lane < place + EDGE), before, ends)
        ends = jnp.where((lane >= place + EDGE) & (lane < place + 2 * EDGE), after, ends)
    rate_ref[Z_LO : Z_LO + 1, :] = ends

    n_coarse = 2 * half // FINE
    first = z_lo * 2 * half
    fine_step = lax.broadcasted_iota(jnp.int32, (FINE, LANES), 0).astype(F32)
    coarse_step = (
        first + FINE * lax.broadcasted_iota(jnp.int32, (n_coarse, LANES), 0)
    ).astype(F32)
    for i in range(Z_LO + 1):
        rate = rate_ref[i : i + 1, :]
        fine_sin, fine_cos = sin_cos(rate * fine_step)
        coarse_sin, coarse_cos = sin_cos(rate * coarse_step)
        coarse_ref[0] = coarse_sin
        coarse_ref[1] = coarse_cos
        for a in range(n_coarse):
            s = coarse_ref[0, a : a + 1, :]
            c = coarse_ref[1, a : a + 1, :]
            table_ref = near_ref if a < n_coarse // 2 else far_ref
            row = a % (n_coarse // 2) * FINE
            table_ref[row : row + FINE, i * LANES : (i + 1) * LANES] = (
                c * fine_cos - s * fine_sin
            ).astype(BF16)
            table_ref[row : row + FINE, depth + i * LANES : depth + (i + 1) * LANES] = (
                s * fine_cos + c * fine_sin
            ).astype(BF16)
    copy = pltpu.make_async_copy(far_ref, far_hbm, sem.at[2])
    copy.start()
    copy.wait()


def sum_pulses(
    tap_rows_ref,
    near_ref,
    far_hbm,
    lifted_ref,
    column_ref,
    edge_ref,
    out_ref,
    edge_out_ref,
    pad_ref,
    blend_ref,
    far_ref,
    sem,
):
    copy = pltpu.make_async_copy(far_hbm, far_ref, sem)
    copy.start()
    z_hi, z_lo, x, yc = place_of()
    width = lifted_ref.shape[2]
    half_pulses = LANES // Z_HI
    main = Z_LO * LANES
    depth = main + LANES
    blocks, columns = out_ref.shape[0], out_ref.shape[1] - EDGE

    zero = jnp.zeros((2 * EDGE, width), F32)
    pad_ref[: 2 * EDGE] = zero
    pad_ref[2 * EDGE + LANES :] = zero
    for i in range(Z_LO):
        for h in range(Z_HI):
            pad_ref[pl.ds(2 * EDGE + h * half_pulses, half_pulses), :] = lifted_ref[
                h * Z_LO + i, :half_pulses, :
            ].astype(F32)
        blended = jnp.zeros((LANES + 2 * EDGE, width), F32)
        for t in range(2 * TAPS_K + 1):
            blended = blended + tap_rows_ref[t : t + 1, :] * pad_ref[
                pl.ds(EDGE - TAPS_K + t, LANES + 2 * EDGE), :
            ]
        turned = pltpu.roll(blended, width // 2, 1)
        lane_full = lax.broadcasted_iota(jnp.int32, blended.shape, 1)
        turned = jnp.where(lane_full < width // 2, -turned, turned)
        for k, value in enumerate((blended, turned)):
            value = value.astype(BF16)
            blend_ref[pl.ds(k * depth + i * LANES, LANES), :] = value[EDGE : EDGE + LANES]
            outside = jnp.concatenate([value[:EDGE], value[EDGE + LANES :]], axis=0)
            blend_ref[pl.ds(k * depth + main + i * 2 * EDGE, 2 * EDGE), :] = outside

    for block in range(blocks):
        if block == blocks // 2:
            copy.wait()
        table_ref = near_ref if block < blocks // 2 else far_ref
        row = block % (blocks // 2) * columns
        out_ref[block, :columns, :] = jnp.dot(
            table_ref[row : row + columns, :],
            blend_ref[...],
            preferred_element_type=F32,
        )

    def came(half, z):
        return joined(lifted_ref[half * Z_LO + z % Z_LO, half_pulses:, :])

    first_band = (z_hi == 1) & (yc == 0)
    last_band = (z_hi == 0) & (yc == N_YC - 1)
    foreign = came(1 - z_hi, z_lo)
    above = jnp.where(first_band, foreign, edge_ref[0:4])
    below = jnp.where(last_band, foreign, edge_ref[4:8])
    edge_out_ref[0:4] = above
    edge_out_ref[4:8] = below
    own = with_corners(column_ref[0:4], above, below)
    left = came(z_hi, z_lo + Z_LO - 1)
    left_fixed = with_corners(left, above, came(1 - z_hi, z_lo + Z_LO - 1))
    left = jnp.where(last_band, left_fixed, left)
    right = came(z_hi, z_lo + 1)
    right_fixed = with_corners(right, came(1 - z_hi, z_lo + 1), below)
    right = jnp.where(first_band, right_fixed, right)
    out_ref[:, columns:, :] = jnp.zeros((blocks, EDGE, LANES), F32)
    out_ref[(x + 1) % N_X, columns : columns + 2, :] = jnp.where(x < N_X - 1, own, left)[2:4]
    out_ref[(x + N_X - 1) % N_X, columns : columns + 2, :] = jnp.where(x > 0, own, right)[0:2]


def variation_inside(step_ref, image_hbm, edge_ref, out_ref, line_ref, pad_ref, flow_ref, sem):
    comps, rows, columns = image_hbm.shape
    copies = [
        pltpu.make_async_copy(
            image_hbm.at[comp],
            pad_ref.at[comp, pl.ds(EDGE, rows), pl.ds(LANES, columns)],
            sem.at[comp],
        )
        for comp in range(comps)
    ]
    for copy in copies:
        copy.start()
    for comp in range(comps):
        pad_ref[comp, :, :LANES] = jnp.zeros((LANES, LANES), F32)
        pad_ref[comp, :EDGE, LANES:] = jnp.zeros((EDGE, columns), F32)
        pad_ref[comp, LOW:, LANES:] = jnp.zeros((LANES - LOW, columns), F32)
        for half in range(2):
            span = pl.ds((1 + half) * LANES, LANES)
            pad_ref[comp, TOP : TOP + 1, span] = edge_ref[2 * comp + half : 2 * comp + half + 1, :]
            pad_ref[comp, LOW : LOW + 1, span] = edge_ref[4 + 2 * comp + half : 5 + 2 * comp + half, :]
    for copy in copies:
        copy.wait()
    line_ref[...] = jnp.zeros_like(line_ref)
    for comp in range(comps):
        first = pad_ref[comp, :, LANES : 2 * LANES].T
        last = pad_ref[comp, :, columns : columns + LANES].T
        line_ref[comp : comp + 1, :] = first[0:1]
        line_ref[2 + comp : 3 + comp, :] = last[LANES - 1 : LANES]

    high, wide = rows + EDGE, columns + LANES
    lane = lax.broadcasted_iota(jnp.int32, (high, wide), 1)
    whole = (lane >= LANES) & (lane < wide - 1)
    row_step, col_step = [], []
    square = jnp.zeros((high, wide), F32) + smooth_eps
    for comp in range(comps):
        here = pad_ref[comp, :high, :]
        row_step.append(pad_ref[comp, 1 : high + 1, :] - here)
        col_step.append(pltpu.roll(here, wide - 1, 1) - here)
        square = square + row_step[-1] * row_step[-1] + col_step[-1] * col_step[-1]
    inverse = jnp.where(whole, lax.rsqrt(square), jnp.zeros_like(square))
    weight = step_ref[0] * step_ref[1]
    for comp in range(comps):
        row_flow = row_step[comp] * inverse
        col_flow = col_step[comp] * inverse
        flow_ref[...] = row_flow
        across = col_flow - pltpu.roll(col_flow, 1, 1)
        down = row_flow[EDGE:, LANES:] - flow_ref[EDGE - 1 : high - 1, LANES:]
        variation = -(down + across[EDGE:, LANES:])
        out_ref[comp] = pad_ref[comp, EDGE:high, LANES:] - weight * variation


def finish(scale, step_ref, sums_ref, base_ref, line_ref, out_ref, side_ref):
    _, z_lo, x, _ = place_of()
    group = z_lo * N_X + x
    comps, rows, columns = base_ref.shape
    total = sums_ref[0, :columns, :]
    for k in range(1, N_X):
        total = total + sums_ref[k, :columns, :]
    total = total.T.reshape(base_ref.shape) * (scale * step_ref[0])

    zero = jnp.zeros((comps, LANES), F32)
    left = jnp.where(group > 0, sums_ref[(x + N_X - 1) % N_X, columns : columns + comps, :], zero)
    right = jnp.where(
        group < Z_LO * N_X - 1, sums_ref[(x + 1) % N_X, columns : columns + comps, :], zero
    )
    first, last = line_ref[0:comps, :], line_ref[comps : 2 * comps, :]

    def flows(here, beside):
        down = pltpu.roll(here, LANES - 1, 1) - here
        across = beside - here
        inverse = lax.rsqrt(jnp.sum(down * down + across * across, axis=0, keepdims=True) + smooth_eps)
        return down * inverse, across * inverse

    side_ref[...] = jnp.zeros_like(side_ref)
    side_ref[0:comps, :] = flows(left, first)[1]
    down, across = flows(last, right)
    side_ref[comps : 2 * comps, :] = pltpu.roll(down, 1, 1) - down - across
    sides = side_ref[...].T[EDGE : EDGE + rows] * (step_ref[0] * step_ref[1])
    lane = lax.broadcasted_iota(jnp.int32, (rows, LANES), 1)
    blank = jnp.zeros((rows, LANES), F32)
    for comp in range(comps):
        added = jnp.where(lane == 0, sides[:, comp : comp + 1], blank)
        out_ref[comp, :, :LANES] = base_ref[comp, :, :LANES] - total[comp, :, :LANES] - added
        added = jnp.where(lane == LANES - 1, sides[:, comps + comp : comps + comp + 1], blank)
        tail = columns - LANES
        out_ref[comp, :, tail:] = base_ref[comp, :, tail:] - total[comp, :, tail:] - added


def in_hbm(*values):
    return tuple(pltpu.with_memory_space_constraint(value, pltpu.HBM) for value in values)


def call(kernel, out_shape, in_specs, args, scratch=(), cost=None, out_specs=None):
    if out_specs is None:
        out_specs = jax.tree.map(lambda _: VMEM, out_shape)
    return pl.pallas_call(
        kernel,
        out_shape=out_shape,
        in_specs=in_specs,
        out_specs=out_specs,
        scratch_shapes=scratch,
        cost_estimate=cost,
        compiler_params=pltpu.CompilerParams(vmem_limit_bytes=16 * 1024 * 1024),
    )(*args)


def local(
    pulse_data,
    window_start,
    footprint,
    range_to_row_weight,
    slow_taps,
    ramp_rate,
    image_now,
    step_and_variation_weight,
):
    band_count = lax.axis_size("band")
    groups = lax.axis_size("aper")
    comps, pulses, bins = pulse_data.shape
    band_rows, window_len = range_to_row_weight.shape
    columns = image_now.shape[2]
    shape = jax.ShapeDtypeStruct

    other_weight = lax.ppermute(range_to_row_weight, ("aper", "band"), halves_swapped())
    block = window_len // LANES * comps * pulses
    windows = call(
        cut_windows,
        shape((N_YC, Z_HI * block + EDGE, LANES), BF16),
        [HBM, HBM, HBM, HBM],
        in_hbm(window_start, footprint, pulse_data, image_now),
        [
            pltpu.SMEM(window_start.shape, jnp.int32),
            pltpu.SMEM(footprint.shape, jnp.int32),
            pltpu.VMEM(pulse_data.shape, BF16),
            pltpu.VMEM((2, comps, EDGE, columns), F32),
            pltpu.VMEM((pulses * comps * (bins // LANES + 1), LANES), F32),
            pltpu.VMEM((band_count * block, LANES), F32),
            pltpu.VMEM((EDGE, LANES), F32),
            pltpu.SemaphoreType.DMA((5,)),
        ],
    )
    in_plane = [[h * N_YC + i for i in range(N_YC)] for h in range(Z_HI)]
    windows = lax.all_to_all(windows, "band", 0, 0, axis_index_groups=in_plane, tiled=True)
    side, weights = call(
        side_columns,
        (shape((EDGE, LANES), F32), shape((Z_HI, band_rows, window_len), BF16)),
        [HBM, HBM, VMEM],
        (*in_hbm(image_now, range_to_row_weight), other_weight),
        [
            pltpu.VMEM((LANES, LANES), F32),
            pltpu.VMEM((2, comps, band_rows, LANES), F32),
            pltpu.SemaphoreType.DMA((3,)),
        ],
        pl.CostEstimate(flops=1 << 34, bytes_accessed=1 << 27, transcendentals=0),
    )
    width = comps * band_rows
    lifted, edges = call(
        lift_windows,
        (
            shape((N_Z, N_YC * pulses + EDGE, width), BF16),
            shape((EDGE, LANES), F32),
        ),
        [VMEM] * 3,
        (windows, weights, side),
        [pltpu.VMEM((EDGE, LANES), F32)],
    )
    lifted = lax.all_to_all(lifted, ("aper", "band"), 0, 0, axis_index_groups=z_rings(), tiled=True)
    depth = (Z_LO + 1) * LANES
    half = N_X * columns // 2
    near, far, tap_rows = call(
        make_table,
        (
            shape((half, 2 * depth), BF16),
            pltpu.HBM((half, 2 * depth), BF16),
            shape((EDGE, LANES), F32),
        ),
        [ANY, HBM, HBM],
        (edges, *in_hbm(ramp_rate.reshape(groups, LANES), slow_taps)),
        [
            pltpu.VMEM((groups, LANES), F32),
            pltpu.SMEM(slow_taps.shape, F32),
            pltpu.VMEM((half, 2 * depth), BF16),
            pltpu.VMEM((2 * EDGE, LANES), F32),
            pltpu.VMEM((2, 2 * half // FINE, LANES), F32),
            pltpu.SemaphoreType.DMA((3,)),
        ],
        pl.CostEstimate(flops=1 << 24, bytes_accessed=1 << 23, transcendentals=0),
        [VMEM, HBM, VMEM],
    )
    sums, edges = call(
        sum_pulses,
        (shape((N_X, columns + EDGE, width), F32), shape((EDGE, LANES), F32)),
        [VMEM, VMEM, HBM, VMEM, VMEM, VMEM],
        (tap_rows, near, *in_hbm(far), lifted, side, edges),
        [
            pltpu.VMEM((LANES + 4 * EDGE, width), F32),
            pltpu.VMEM((2 * depth, width), BF16),
            pltpu.VMEM((half, 2 * depth), BF16),
            pltpu.SemaphoreType.DMA,
        ],
    )
    along_x = [[z * N_X + x for x in range(N_X)] for z in range(Z_LO)]
    sums = lax.all_to_all(sums, "aper", 0, 0, axis_index_groups=along_x, tiled=True)
    base, lines = call(
        variation_inside,
        (shape(image_now.shape, F32), shape((EDGE, LANES), F32)),
        [SMEM, HBM, VMEM],
        (step_and_variation_weight, *in_hbm(image_now), edges),
        [
            pltpu.VMEM((comps, LANES, columns + LANES), F32),
            pltpu.VMEM((band_rows + EDGE, columns + LANES), F32),
            pltpu.SemaphoreType.DMA((comps,)),
        ],
        pl.CostEstimate(flops=1 << 24, bytes_accessed=1 << 23, transcendentals=0),
    )
    scale = 1.0 / math.sqrt(groups * LANES)
    return call(
        lambda *refs: finish(scale, *refs),
        shape(image_now.shape, F32),
        [SMEM, VMEM, VMEM, VMEM],
        (step_and_variation_weight, sums, base, lines),
        [pltpu.VMEM((LANES, LANES), F32)],
    )


def solution(mesh):
    return jax.shard_map(
        local,
        mesh=mesh,
        in_specs=(
            P(None, ("aper", "band"), None),
            P(("aper", "band"), None),
            P(("aper", "band"), None),
            P("band", None),
            P(),
            P(),
            P(None, "band", "aper"),
            P(),
        ),
        out_specs=P(None, "band", "aper"),
        check_vma=False,
    )
```

```python
import math

import jax
import jax.numpy as jnp
from jax import lax
from jax.experimental import pallas as pl
from jax.experimental.pallas import tpu as pltpu
from jax.sharding import PartitionSpec as P

TAPS_K = 2
LANES = 128
EDGE = 8
Z_HI, Z_LO, N_X, N_YC = 2, 8, 4, 8
N_Z = Z_HI * Z_LO
smooth_eps = 0.05
BF16, F32 = jnp.bfloat16, jnp.float32
VMEM = pl.BlockSpec(memory_space=pltpu.VMEM)
SMEM = pl.BlockSpec(memory_space=pltpu.SMEM)
ANY = pl.BlockSpec(memory_space=pl.ANY)
HBM = pl.BlockSpec(memory_space=pltpu.HBM)


def device_index(z_hi, z_lo, x, yc):
    return ((z_lo * N_X + x) * Z_HI + z_hi) * N_YC + yc


def z_rings():
    return [
        [device_index(z // Z_LO, z % Z_LO, x, yc) for z in range(N_Z)]
        for x in range(N_X)
        for yc in range(N_YC)
    ]


def halves_swapped():
    return [
        (device_index(h, z, x, yc), device_index(1 - h, (z + Z_LO // 2) % Z_LO, x, yc))
        for h in range(Z_HI)
        for z in range(Z_LO)
        for x in range(N_X)
        for yc in range(N_YC)
    ]


def place_of():
    group, band = lax.axis_index("aper"), lax.axis_index("band")
    return band // N_YC, group // N_X, group % N_X, band % N_YC


def two_parts(value, spare_ref):
    first = value.astype(BF16).astype(F32)
    spare_ref[0:4] = first
    spare_ref[4:8] = value - first
    return spare_ref[...].astype(BF16)


def joined(rows):
    rows = rows.astype(F32)
    return rows[0:4] + rows[4:8]


TOP, LOW = EDGE - 1, EDGE + 64


def with_corners(columns, above, below):
    lane = lax.broadcasted_iota(jnp.int32, columns.shape, 1)
    row = lax.broadcasted_iota(jnp.int32, columns.shape, 0)
    above = pltpu.roll(above, TOP, 1)
    below = pltpu.roll(below, (LOW + 1) % LANES, 1)
    for comp in range(2):
        columns = jnp.where((lane == TOP) & (row == comp), above[2 * comp : 2 * comp + 1], columns)
        columns = jnp.where(
            (lane == LOW) & (row == 2 + comp), below[2 * comp + 1 : 2 * comp + 2], columns
        )
    return columns


def cut_windows(
    start_hbm,
    foot_hbm,
    pulse_hbm,
    image_hbm,
    out_ref,
    start_ref,
    foot_ref,
    pulse_ref,
    edge_ref,
    flat_ref,
    window_ref,
    spare_ref,
    sem,
):
    rows = image_hbm.shape[1]
    copies = [
        pltpu.make_async_copy(pulse_hbm, pulse_ref, sem.at[0]),
        pltpu.make_async_copy(start_hbm, start_ref, sem.at[1]),
        pltpu.make_async_copy(foot_hbm, foot_ref, sem.at[2]),
        pltpu.make_async_copy(image_hbm.at[:, pl.ds(0, EDGE), :], edge_ref.at[0], sem.at[3]),
        pltpu.make_async_copy(image_hbm.at[:, pl.ds(rows - EDGE, EDGE), :], edge_ref.at[1], sem.at[4]),
    ]
    for copy in copies:
        copy.start()
    window_ref[...] = jnp.zeros_like(window_ref)
    comps, pulses, bins = pulse_ref.shape
    parts = bins // LANES
    pitch = comps * (parts + 1)
    block = window_ref.shape[0] // (Z_HI * N_YC)
    for copy in copies:
        copy.wait()
    for part in range(parts):
        for comp in range(comps):
            flat_ref[pl.ds(part * comps + comp, pulses, stride=pitch), :] = pulse_ref[
                comp, :, part * LANES : (part + 1) * LANES
            ].astype(F32)
    lane = lax.broadcasted_iota(jnp.int32, (block // pulses, LANES), 1)
    for pulse in range(pulses):
        for k in range(foot_ref.shape[1]):
            band = foot_ref[pulse, k]
            start = start_ref[pulse, band]
            row = pulse * pitch + comps * (start >> 7)
            shift = start & (LANES - 1)
            here = flat_ref[pl.ds(row, block // pulses), :]
            following = flat_ref[pl.ds(row + comps, block // pulses), :]
            both = jnp.where(lane >= shift, here, following)
            both = pltpu.roll(both, (LANES - shift) & (LANES - 1), 1)
            place = ((band & (N_YC - 1)) * Z_HI + (band >> 3)) * block + pulse
            window_ref[pl.ds(place, block // pulses, stride=pulses), :] = both
    tall = Z_HI * block
    out_ref[:, :tall, :] = window_ref[...].astype(BF16).reshape(N_YC, tall, LANES)
    out_ref[:, tall:, :] = jnp.zeros((N_YC, EDGE, LANES), BF16)
    yc = place_of()[3]
    for side, line, to in ((0, 0, yc + N_YC - 1), (1, EDGE - 1, yc + 1)):
        edge = [edge_ref[side, comp, line : line + 1, :] for comp in range(comps)]
        edge = [e[:, i * LANES : (i + 1) * LANES] for e in edge for i in range(2)]
        out_ref[to % N_YC, tall:, :] = two_parts(jnp.concatenate(edge, axis=0), spare_ref)


def side_columns(image_hbm, weight_hbm, other_ref, out_ref, weight_ref, pad_ref, block_ref, sem):
    z_hi = place_of()[0]
    rows, columns = image_hbm.shape[1:]
    copies = [
        pltpu.make_async_copy(weight_hbm, weight_ref.at[z_hi], sem.at[0]),
        pltpu.make_async_copy(image_hbm.at[:, :, pl.ds(0, LANES)], block_ref.at[0], sem.at[1]),
        pltpu.make_async_copy(
            image_hbm.at[:, :, pl.ds(columns - LANES, LANES)], block_ref.at[1], sem.at[2]
        ),
    ]
    for copy in copies:
        copy.start()
    weight_ref[1 - z_hi] = other_ref[...]
    pad_ref[...] = jnp.zeros_like(pad_ref)
    out_ref[...] = jnp.zeros_like(out_ref)
    for copy in copies:
        copy.wait()
    for comp in range(2):
        for side, line in ((0, 0), (1, LANES - 1)):
            pad_ref[EDGE : EDGE + rows, :] = block_ref[side, comp]
            out_ref[2 * side + comp : 2 * side + comp + 1, :] = pad_ref[...].T[line : line + 1, :]


def lift_windows(
    window_ref, weight_ref, column_ref, out_ref, edge_ref, spare_ref
):
    z_hi, _, _, yc = place_of()
    sources, height = window_ref.shape[0], window_ref.shape[1] - EDGE
    half = height // Z_HI
    band_rows, window_len = weight_ref.shape[1:]
    parts = window_len // LANES
    rows = half // parts
    tall = sources * rows // 2

    above = joined(window_ref[(yc + N_YC - 1) % N_YC, height:, :])
    below = joined(window_ref[(yc + 1) % N_YC, height:, :])
    foreign = jnp.where(yc == 0, above, below)
    above = jnp.where(yc > 0, above, jnp.zeros_like(above))
    below = jnp.where(yc < N_YC - 1, below, jnp.zeros_like(below))
    edge_ref[0:4] = above
    edge_ref[4:8] = below
    columns = with_corners(column_ref[0:4], above, below)

    dims = (((1,), (1,)), ((), ()))
    for z_half in range(Z_HI):
        extra = jnp.where(z_half == z_hi, columns, foreign)
        lifted = jnp.zeros((sources * rows, band_rows), F32)
        for part in range(parts):
            first = z_half * half + part * rows
            piece = window_ref[:, pl.ds(first, rows), :].reshape(sources * rows, LANES)
            lifted = lifted + lax.dot_general(
                piece,
                weight_ref[z_half, :, part * LANES : (part + 1) * LANES],
                dims,
                preferred_element_type=F32,
            )
        lifted = lifted.reshape(sources, 2, rows // 2, band_rows)
        both = jnp.concatenate([lifted[:, 0], lifted[:, 1]], axis=-1)
        both = both.reshape(tall, 2 * band_rows).astype(BF16)
        extra = two_parts(extra, spare_ref)
        for z in range(Z_LO):
            out_ref[z_half * Z_LO + z, :tall, :] = both
            out_ref[z_half * Z_LO + z, tall:, :] = extra


def sin_cos(angle):
    turns = jnp.round(angle * (2.0 / math.pi))
    rest = angle - turns * 1.5703125
    rest = rest - turns * 4.837512969970703125e-4
    rest = rest - turns * 7.54978995489188216e-8
    square = rest * rest
    sine = -1.9515295891e-4 * square + 8.3321608736e-3
    sine = (sine * square - 1.6666654611e-1) * square * rest + rest
    cosine = 2.443315711809948e-5 * square - 1.388731625493765e-3
    cosine = (cosine * square + 4.166664568298827e-2) * square * square - 0.5 * square + 1.0
    quarter = turns.astype(jnp.int32) & 3
    swap = (quarter & 1) == 1
    sin_out = jnp.where(swap, cosine, sine)
    cos_out = jnp.where(swap, sine, cosine)
    sin_out = jnp.where(quarter >= 2, -sin_out, sin_out)
    cos_out = jnp.where((quarter == 1) | (quarter == 2), -cos_out, cos_out)
    return sin_out, cos_out


FINE = 16


def make_table(
    after_ref,
    ramp_hbm,
    taps_hbm,
    near_ref,
    fine_ref,
    coarse_ref,
    tap_rows_ref,
    ramp_ref,
    taps_ref,
    rate_ref,
    spare_ref,
    sem,
):
    del after_ref
    copies = [
        pltpu.make_async_copy(ramp_hbm, ramp_ref, sem.at[0]),
        pltpu.make_async_copy(taps_hbm, taps_ref, sem.at[1]),
    ]
    for copy in copies:
        copy.start()
    _, z_lo, x, _ = place_of()
    n_groups = ramp_ref.shape[0]
    half = near_ref.shape[0]
    for copy in copies:
        copy.wait()
    for t in range(2 * TAPS_K + 1):
        tap_rows_ref[t : t + 1, :] = jnp.full((1, LANES), taps_ref[t], F32)

    lane = lax.broadcasted_iota(jnp.int32, (1, LANES), 1)
    ends = jnp.zeros((1, LANES), F32)
    for i in range(Z_LO):
        group = i * N_X + x
        rate_ref[i : i + 1, :] = ramp_ref[pl.ds(group, 1), :]
        before = ramp_ref[pl.ds((group + n_groups - 1) % n_groups, 1), :]
        after = ramp_ref[pl.ds((group + 1) % n_groups, 1), :]
        place = 2 * EDGE * i
        move = (place + EDGE) % LANES
        before = pltpu.roll(before, move, 1) if move else before
        after = pltpu.roll(after, move, 1) if move else after
        ends = jnp.where((lane >= place) & (lane < place + EDGE), before, ends)
        ends = jnp.where((lane >= place + EDGE) & (lane < place + 2 * EDGE), after, ends)
    rate_ref[Z_LO : Z_LO + 1, :] = ends

    n_coarse = 2 * half // FINE
    first = z_lo * 2 * half
    fine_step = lax.broadcasted_iota(jnp.int32, (FINE, LANES), 0).astype(F32)
    coarse_step = (
        first + FINE * lax.broadcasted_iota(jnp.int32, (n_coarse, LANES), 0)
    ).astype(F32)
    for i in range(Z_LO + 1):
        span = pl.ds(i * LANES, LANES)
        rate = rate_ref[i : i + 1, :]
        fine_sin, fine_cos = sin_cos(rate * fine_step)
        coarse_sin, coarse_cos = sin_cos(rate * coarse_step)
        fine_ref[0, :, span], fine_ref[1, :, span] = fine_sin, fine_cos
        spare_ref[0], spare_ref[1] = coarse_sin, coarse_cos
        coarse_ref[0, :, span] = coarse_sin[n_coarse // 2 :]
        coarse_ref[1, :, span] = coarse_cos[n_coarse // 2 :]
        for a in range(n_coarse // 2):
            fill(
                near_ref,
                a * FINE,
                i,
                (spare_ref[0, a : a + 1, :], spare_ref[1, a : a + 1, :]),
                (fine_sin, fine_cos),
            )


def fill(table_ref, row, i, coarse, fine):
    depth = table_ref.shape[1] // 2
    (s, c), (fine_sin, fine_cos) = coarse, fine
    table_ref[row : row + FINE, i * LANES : (i + 1) * LANES] = (
        c * fine_cos - s * fine_sin
    ).astype(BF16)
    table_ref[row : row + FINE, depth + i * LANES : depth + (i + 1) * LANES] = (
        s * fine_cos + c * fine_sin
    ).astype(BF16)


def sum_pulses(
    tap_rows_ref,
    near_ref,
    fine_ref,
    coarse_ref,
    lifted_ref,
    column_ref,
    edge_ref,
    out_ref,
    edge_out_ref,
    pad_ref,
    blend_ref,
    far_ref,
):
    z_hi, z_lo, x, yc = place_of()
    width = lifted_ref.shape[2]
    half_pulses = LANES // Z_HI
    main = Z_LO * LANES
    depth = main + LANES
    blocks, columns = out_ref.shape[0], out_ref.shape[1] - EDGE

    zero = jnp.zeros((2 * EDGE, width), F32)
    pad_ref[: 2 * EDGE] = zero
    pad_ref[2 * EDGE + LANES :] = zero
    for i in range(Z_LO):
        for h in range(Z_HI):
            pad_ref[pl.ds(2 * EDGE + h * half_pulses, half_pulses), :] = lifted_ref[
                h * Z_LO + i, :half_pulses, :
            ].astype(F32)
        blended = jnp.zeros((LANES + 2 * EDGE, width), F32)
        for t in range(2 * TAPS_K + 1):
            blended = blended + tap_rows_ref[t : t + 1, :] * pad_ref[
                pl.ds(EDGE - TAPS_K + t, LANES + 2 * EDGE), :
            ]
        turned = pltpu.roll(blended, width // 2, 1)
        lane_full = lax.broadcasted_iota(jnp.int32, blended.shape, 1)
        turned = jnp.where(lane_full < width // 2, -turned, turned)
        for k, value in enumerate((blended, turned)):
            value = value.astype(BF16)
            blend_ref[pl.ds(k * depth + i * LANES, LANES), :] = value[EDGE : EDGE + LANES]
            outside = jnp.concatenate([value[:EDGE], value[EDGE + LANES :]], axis=0)
            blend_ref[pl.ds(k * depth + main + i * 2 * EDGE, 2 * EDGE), :] = outside

    for i in range(Z_LO + 1):
        span = pl.ds(i * LANES, LANES)
        fine = fine_ref[0, :, span], fine_ref[1, :, span]
        for a in range(far_ref.shape[0] // FINE):
            coarse = coarse_ref[0, a : a + 1, span], coarse_ref[1, a : a + 1, span]
            fill(far_ref, a * FINE, i, coarse, fine)
    for block in range(blocks):
        table_ref = near_ref if block < blocks // 2 else far_ref
        row = block % (blocks // 2) * columns
        out_ref[block, :columns, :] = jnp.dot(
            table_ref[row : row + columns, :],
            blend_ref[...],
            preferred_element_type=F32,
        )

    def came(half, z):
        return joined(lifted_ref[half * Z_LO + z % Z_LO, half_pulses:, :])

    first_band = (z_hi == 1) & (yc == 0)
    last_band = (z_hi == 0) & (yc == N_YC - 1)
    foreign = came(1 - z_hi, z_lo)
    above = jnp.where(first_band, foreign, edge_ref[0:4])
    below = jnp.where(last_band, foreign, edge_ref[4:8])
    edge_out_ref[0:4] = above
    edge_out_ref[4:8] = below
    own = with_corners(column_ref[0:4], above, below)
    left = came(z_hi, z_lo + Z_LO - 1)
    left_fixed = with_corners(left, above, came(1 - z_hi, z_lo + Z_LO - 1))
    left = jnp.where(last_band, left_fixed, left)
    right = came(z_hi, z_lo + 1)
    right_fixed = with_corners(right, came(1 - z_hi, z_lo + 1), below)
    right = jnp.where(first_band, right_fixed, right)
    out_ref[:, columns:, :] = jnp.zeros((blocks, EDGE, LANES), F32)
    out_ref[(x + 1) % N_X, columns : columns + 2, :] = jnp.where(x < N_X - 1, own, left)[2:4]
    out_ref[(x + N_X - 1) % N_X, columns : columns + 2, :] = jnp.where(x > 0, own, right)[0:2]


def variation_inside(step_ref, image_hbm, edge_ref, out_ref, line_ref, pad_ref, flow_ref, sem):
    comps, rows, columns = image_hbm.shape
    copies = [
        pltpu.make_async_copy(
            image_hbm.at[comp],
            pad_ref.at[comp, pl.ds(EDGE, rows), pl.ds(LANES, columns)],
            sem.at[comp],
        )
        for comp in range(comps)
    ]
    for copy in copies:
        copy.start()
    for comp in range(comps):
        pad_ref[comp, :, :LANES] = jnp.zeros((LANES, LANES), F32)
        pad_ref[comp, :EDGE, LANES:] = jnp.zeros((EDGE, columns), F32)
        pad_ref[comp, LOW:, LANES:] = jnp.zeros((LANES - LOW, columns), F32)
        for half in range(2):
            span = pl.ds((1 + half) * LANES, LANES)
            pad_ref[comp, TOP : TOP + 1, span] = edge_ref[2 * comp + half : 2 * comp + half + 1, :]
            pad_ref[comp, LOW : LOW + 1, span] = edge_ref[4 + 2 * comp + half : 5 + 2 * comp + half, :]
    for copy in copies:
        copy.wait()
    line_ref[...] = jnp.zeros_like(line_ref)
    for comp in range(comps):
        first = pad_ref[comp, :, LANES : 2 * LANES].T
        last = pad_ref[comp, :, columns : columns + LANES].T
        line_ref[comp : comp + 1, :] = first[0:1]
        line_ref[2 + comp : 3 + comp, :] = last[LANES - 1 : LANES]

    high, wide = rows + EDGE, columns + LANES
    lane = lax.broadcasted_iota(jnp.int32, (high, wide), 1)
    whole = (lane >= LANES) & (lane < wide - 1)
    row_step, col_step = [], []
    square = jnp.zeros((high, wide), F32) + smooth_eps
    for comp in range(comps):
        here = pad_ref[comp, :high, :]
        row_step.append(pad_ref[comp, 1 : high + 1, :] - here)
        col_step.append(pltpu.roll(here, wide - 1, 1) - here)
        square = square + row_step[-1] * row_step[-1] + col_step[-1] * col_step[-1]
    inverse = jnp.where(whole, lax.rsqrt(square), jnp.zeros_like(square))
    weight = step_ref[0] * step_ref[1]
    for comp in range(comps):
        row_flow = row_step[comp] * inverse
        col_flow = col_step[comp] * inverse
        flow_ref[...] = row_flow
        across = col_flow - pltpu.roll(col_flow, 1, 1)
        down = row_flow[EDGE:, LANES:] - flow_ref[EDGE - 1 : high - 1, LANES:]
        variation = -(down + across[EDGE:, LANES:])
        out_ref[comp] = pad_ref[comp, EDGE:high, LANES:] - weight * variation


def finish(scale, step_ref, sums_ref, base_ref, line_ref, out_ref, side_ref):
    _, z_lo, x, _ = place_of()
    group = z_lo * N_X + x
    comps, rows, columns = base_ref.shape
    total = sums_ref[0, :columns, :]
    for k in range(1, N_X):
        total = total + sums_ref[k, :columns, :]
    total = total.T.reshape(base_ref.shape) * (scale * step_ref[0])

    zero = jnp.zeros((comps, LANES), F32)
    left = jnp.where(group > 0, sums_ref[(x + N_X - 1) % N_X, columns : columns + comps, :], zero)
    right = jnp.where(
        group < Z_LO * N_X - 1, sums_ref[(x + 1) % N_X, columns : columns + comps, :], zero
    )
    first, last = line_ref[0:comps, :], line_ref[comps : 2 * comps, :]

    def flows(here, beside):
        down = pltpu.roll(here, LANES - 1, 1) - here
        across = beside - here
        inverse = lax.rsqrt(jnp.sum(down * down + across * across, axis=0, keepdims=True) + smooth_eps)
        return down * inverse, across * inverse

    side_ref[...] = jnp.zeros_like(side_ref)
    side_ref[0:comps, :] = flows(left, first)[1]
    down, across = flows(last, right)
    side_ref[comps : 2 * comps, :] = pltpu.roll(down, 1, 1) - down - across
    sides = side_ref[...].T[EDGE : EDGE + rows] * (step_ref[0] * step_ref[1])
    lane = lax.broadcasted_iota(jnp.int32, (rows, LANES), 1)
    blank = jnp.zeros((rows, LANES), F32)
    for comp in range(comps):
        added = jnp.where(lane == 0, sides[:, comp : comp + 1], blank)
        out_ref[comp, :, :LANES] = base_ref[comp, :, :LANES] - total[comp, :, :LANES] - added
        added = jnp.where(lane == LANES - 1, sides[:, comps + comp : comps + comp + 1], blank)
        tail = columns - LANES
        out_ref[comp, :, tail:] = base_ref[comp, :, tail:] - total[comp, :, tail:] - added


def in_hbm(*values):
    return tuple(pltpu.with_memory_space_constraint(value, pltpu.HBM) for value in values)


def call(kernel, out_shape, in_specs, args, scratch=(), cost=None, out_specs=None):
    if out_specs is None:
        out_specs = [VMEM] * len(out_shape) if isinstance(out_shape, tuple) else VMEM
    return pl.pallas_call(
        kernel,
        out_shape=out_shape,
        in_specs=in_specs,
        out_specs=out_specs,
        scratch_shapes=scratch,
        cost_estimate=cost,
        compiler_params=pltpu.CompilerParams(vmem_limit_bytes=16 * 1024 * 1024),
    )(*args)


def local(
    pulse_data,
    window_start,
    footprint,
    range_to_row_weight,
    slow_taps,
    ramp_rate,
    image_now,
    step_and_variation_weight,
):
    band_count = lax.axis_size("band")
    groups = lax.axis_size("aper")
    comps, pulses, bins = pulse_data.shape
    band_rows, window_len = range_to_row_weight.shape
    columns = image_now.shape[2]
    shape = jax.ShapeDtypeStruct

    other_weight = lax.ppermute(range_to_row_weight, ("aper", "band"), halves_swapped())
    block = window_len // LANES * comps * pulses
    windows = call(
        cut_windows,
        pltpu.VMEM((N_YC, Z_HI * block + EDGE, LANES), BF16),
        [HBM, HBM, HBM, HBM],
        in_hbm(window_start, footprint, pulse_data, image_now),
        [
            pltpu.SMEM(window_start.shape, jnp.int32),
            pltpu.SMEM(footprint.shape, jnp.int32),
            pltpu.VMEM(pulse_data.shape, BF16),
            pltpu.VMEM((2, comps, EDGE, columns), F32),
            pltpu.VMEM((pulses * comps * (bins // LANES + 1), LANES), F32),
            pltpu.VMEM((band_count * block, LANES), F32),
            pltpu.VMEM((EDGE, LANES), F32),
            pltpu.SemaphoreType.DMA((5,)),
        ],
    )
    in_plane = [[h * N_YC + i for i in range(N_YC)] for h in range(Z_HI)]
    windows = lax.all_to_all(windows, "band", 0, 0, axis_index_groups=in_plane, tiled=True)
    side, weights = call(
        side_columns,
        (shape((EDGE, LANES), F32), shape((Z_HI, band_rows, window_len), BF16)),
        [HBM, HBM, VMEM],
        (*in_hbm(image_now, range_to_row_weight), other_weight),
        [
            pltpu.VMEM((LANES, LANES), F32),
            pltpu.VMEM((2, comps, band_rows, LANES), F32),
            pltpu.SemaphoreType.DMA((3,)),
        ],
        pl.CostEstimate(flops=1 << 34, bytes_accessed=1 << 27, transcendentals=0),
    )
    width = comps * band_rows
    lifted, edges = call(
        lift_windows,
        (
            pltpu.VMEM((N_Z, N_YC * pulses + EDGE, width), BF16),
            shape((EDGE, LANES), F32),
        ),
        [VMEM] * 3,
        (windows, weights, side),
        [pltpu.VMEM((EDGE, LANES), F32)],
    )
    lifted = lax.all_to_all(lifted, ("aper", "band"), 0, 0, axis_index_groups=z_rings(), tiled=True)
    depth = (Z_LO + 1) * LANES
    half = N_X * columns // 2
    near, fine, coarse, tap_rows = call(
        make_table,
        (
            shape((half, 2 * depth), BF16),
            shape((2, FINE, depth), F32),
            shape((2, half // FINE, depth), F32),
            shape((EDGE, LANES), F32),
        ),
        [ANY, HBM, HBM],
        (edges, *in_hbm(ramp_rate.reshape(groups, LANES), slow_taps)),
        [
            pltpu.VMEM((groups, LANES), F32),
            pltpu.SMEM(slow_taps.shape, F32),
            pltpu.VMEM((2 * EDGE, LANES), F32),
            pltpu.VMEM((2, 2 * half // FINE, LANES), F32),
            pltpu.SemaphoreType.DMA((2,)),
        ],
        pl.CostEstimate(flops=1 << 24, bytes_accessed=1 << 23, transcendentals=0),
    )
    sums, edges = call(
        sum_pulses,
        (pltpu.VMEM((N_X, columns + EDGE, width), F32), shape((EDGE, LANES), F32)),
        [VMEM] * 7,
        (tap_rows, near, fine, coarse, lifted, side, edges),
        [
            pltpu.VMEM((LANES + 4 * EDGE, width), F32),
            pltpu.VMEM((2 * depth, width), BF16),
            pltpu.VMEM((half, 2 * depth), BF16),
        ],
    )
    along_x = [[z * N_X + x for x in range(N_X)] for z in range(Z_LO)]
    sums = lax.all_to_all(sums, "aper", 0, 0, axis_index_groups=along_x, tiled=True)
    base, lines = call(
        variation_inside,
        (shape(image_now.shape, F32), shape((EDGE, LANES), F32)),
        [SMEM, HBM, VMEM],
        (step_and_variation_weight, *in_hbm(image_now), edges),
        [
            pltpu.VMEM((comps, LANES, columns + LANES), F32),
            pltpu.VMEM((band_rows + EDGE, columns + LANES), F32),
            pltpu.SemaphoreType.DMA((comps,)),
        ],
        pl.CostEstimate(flops=1 << 24, bytes_accessed=1 << 23, transcendentals=0),
    )
    scale = 1.0 / math.sqrt(groups * LANES)
    return call(
        lambda *refs: finish(scale, *refs),
        shape(image_now.shape, F32),
        [SMEM, VMEM, VMEM, VMEM],
        (step_and_variation_weight, sums, base, lines),
        [pltpu.VMEM((LANES, LANES), F32)],
    )


def solution(mesh):
    return jax.shard_map(
        local,
        mesh=mesh,
        in_specs=(
            P(None, ("aper", "band"), None),
            P(("aper", "band"), None),
            P(("aper", "band"), None),
            P("band", None),
            P(),
            P(),
            P(None, "band", "aper"),
            P(),
        ),
        out_specs=P(None, "band", "aper"),
        check_vma=False,
    )
```

```python
import math

import jax
import jax.numpy as jnp
from jax import lax
from jax.experimental import pallas as pl
from jax.experimental.pallas import tpu as pltpu
from jax.sharding import PartitionSpec as P

TAPS_K = 2
LANES = 128
EDGE = 8
Z_HI, Z_LO, N_X, N_YC = 2, 8, 4, 8
N_Z = Z_HI * Z_LO
smooth_eps = 0.05
BF16, F32 = jnp.bfloat16, jnp.float32
VMEM = pl.BlockSpec(memory_space=pltpu.VMEM)
SMEM = pl.BlockSpec(memory_space=pltpu.SMEM)
ANY = pl.BlockSpec(memory_space=pl.ANY)
HBM = pl.BlockSpec(memory_space=pltpu.HBM)


def device_index(z_hi, z_lo, x, yc):
    return ((z_lo * N_X + x) * Z_HI + z_hi) * N_YC + yc


def z_rings():
    return [
        [device_index(z // Z_LO, z % Z_LO, x, yc) for z in range(N_Z)]
        for x in range(N_X)
        for yc in range(N_YC)
    ]


def halves_swapped():
    return [
        (device_index(h, z, x, yc), device_index(1 - h, (z + Z_LO // 2) % Z_LO, x, yc))
        for h in range(Z_HI)
        for z in range(Z_LO)
        for x in range(N_X)
        for yc in range(N_YC)
    ]


def place_of():
    group, band = lax.axis_index("aper"), lax.axis_index("band")
    return band // N_YC, group // N_X, group % N_X, band % N_YC


def two_parts(value, spare_ref):
    first = value.astype(BF16).astype(F32)
    spare_ref[0:4] = first
    spare_ref[4:8] = value - first
    return spare_ref[...].astype(BF16)


def joined(rows):
    rows = rows.astype(F32)
    return rows[0:4] + rows[4:8]


TOP, LOW = EDGE - 1, EDGE + 64


def with_corners(columns, above, below):
    lane = lax.broadcasted_iota(jnp.int32, columns.shape, 1)
    row = lax.broadcasted_iota(jnp.int32, columns.shape, 0)
    above = pltpu.roll(above, TOP, 1)
    below = pltpu.roll(below, (LOW + 1) % LANES, 1)
    for comp in range(2):
        columns = jnp.where((lane == TOP) & (row == comp), above[2 * comp : 2 * comp + 1], columns)
        columns = jnp.where(
            (lane == LOW) & (row == 2 + comp), below[2 * comp + 1 : 2 * comp + 2], columns
        )
    return columns


def cut_windows(
    start_hbm,
    foot_hbm,
    pulse_hbm,
    image_hbm,
    weight_hbm,
    out_ref,
    sent_ref,
    start_ref,
    foot_ref,
    pulse_ref,
    edge_ref,
    flat_ref,
    window_ref,
    spare_ref,
    sem,
):
    rows = image_hbm.shape[1]
    copies = [
        pltpu.make_async_copy(pulse_hbm, pulse_ref, sem.at[0]),
        pltpu.make_async_copy(start_hbm, start_ref, sem.at[1]),
        pltpu.make_async_copy(foot_hbm, foot_ref, sem.at[2]),
        pltpu.make_async_copy(image_hbm.at[:, pl.ds(0, EDGE), :], edge_ref.at[0], sem.at[3]),
        pltpu.make_async_copy(image_hbm.at[:, pl.ds(rows - EDGE, EDGE), :], edge_ref.at[1], sem.at[4]),
    ]
    handed = pltpu.make_async_copy(weight_hbm, sent_ref, sem.at[5])
    handed.start()
    for copy in copies:
        copy.start()
    window_ref[...] = jnp.zeros_like(window_ref)
    comps, pulses, bins = pulse_ref.shape
    parts = bins // LANES
    pitch = comps * (parts + 1)
    block = window_ref.shape[0] // (Z_HI * N_YC)
    for copy in copies:
        copy.wait()
    for part in range(parts):
        for comp in range(comps):
            flat_ref[pl.ds(part * comps + comp, pulses, stride=pitch), :] = pulse_ref[
                comp, :, part * LANES : (part + 1) * LANES
            ].astype(F32)
    lane = lax.broadcasted_iota(jnp.int32, (block // pulses, LANES), 1)
    for pulse in range(pulses):
        for k in range(foot_ref.shape[1]):
            band = foot_ref[pulse, k]
            start = start_ref[pulse, band]
            row = pulse * pitch + comps * (start >> 7)
            shift = start & (LANES - 1)
            here = flat_ref[pl.ds(row, block // pulses), :]
            following = flat_ref[pl.ds(row + comps, block // pulses), :]
            both = jnp.where(lane >= shift, here, following)
            both = pltpu.roll(both, (LANES - shift) & (LANES - 1), 1)
            place = ((band & (N_YC - 1)) * Z_HI + (band >> 3)) * block + pulse
            window_ref[pl.ds(place, block // pulses, stride=pulses), :] = both
    tall = Z_HI * block
    out_ref[:, :tall, :] = window_ref[...].astype(BF16).reshape(N_YC, tall, LANES)
    out_ref[:, tall:, :] = jnp.zeros((N_YC, EDGE, LANES), BF16)
    yc = place_of()[3]
    for side, line, to in ((0, 0, yc + N_YC - 1), (1, EDGE - 1, yc + 1)):
        edge = [edge_ref[side, comp, line : line + 1, :] for comp in range(comps)]
        edge = [e[:, i * LANES : (i + 1) * LANES] for e in edge for i in range(2)]
        out_ref[to % N_YC, tall:, :] = two_parts(jnp.concatenate(edge, axis=0), spare_ref)
    handed.wait()


def side_columns(image_hbm, weight_hbm, other_ref, out_ref, weight_ref, pad_ref, block_ref, sem):
    z_hi = place_of()[0]
    rows, columns = image_hbm.shape[1:]
    copies = [
        pltpu.make_async_copy(weight_hbm, weight_ref.at[z_hi], sem.at[0]),
        pltpu.make_async_copy(image_hbm.at[:, :, pl.ds(0, LANES)], block_ref.at[0], sem.at[1]),
        pltpu.make_async_copy(
            image_hbm.at[:, :, pl.ds(columns - LANES, LANES)], block_ref.at[1], sem.at[2]
        ),
    ]
    for copy in copies:
        copy.start()
    weight_ref[1 - z_hi] = other_ref[...]
    pad_ref[...] = jnp.zeros_like(pad_ref)
    out_ref[...] = jnp.zeros_like(out_ref)
    for copy in copies:
        copy.wait()
    for comp in range(2):
        for side, line in ((0, 0), (1, LANES - 1)):
            pad_ref[EDGE : EDGE + rows, :] = block_ref[side, comp]
            out_ref[2 * side + comp : 2 * side + comp + 1, :] = pad_ref[...].T[line : line + 1, :]


def lift_windows(
    window_ref, weight_ref, column_ref, out_ref, edge_ref, spare_ref
):
    z_hi, _, _, yc = place_of()
    sources, height = window_ref.shape[0], window_ref.shape[1] - EDGE
    half = height // Z_HI
    band_rows, window_len = weight_ref.shape[1:]
    parts = window_len // LANES
    rows = half // parts
    tall = sources * rows // 2

    above = joined(window_ref[(yc + N_YC - 1) % N_YC, height:, :])
    below = joined(window_ref[(yc + 1) % N_YC, height:, :])
    foreign = jnp.where(yc == 0, above, below)
    above = jnp.where(yc > 0, above, jnp.zeros_like(above))
    below = jnp.where(yc < N_YC - 1, below, jnp.zeros_like(below))
    edge_ref[0:4] = above
    edge_ref[4:8] = below
    columns = with_corners(column_ref[0:4], above, below)

    dims = (((1,), (1,)), ((), ()))
    for z_half in range(Z_HI):
        extra = jnp.where(z_half == z_hi, columns, foreign)
        lifted = jnp.zeros((sources * rows, band_rows), F32)
        for part in range(parts):
            first = z_half * half + part * rows
            piece = window_ref[:, pl.ds(first, rows), :].reshape(sources * rows, LANES)
            lifted = lifted + lax.dot_general(
                piece,
                weight_ref[z_half, :, part * LANES : (part + 1) * LANES],
                dims,
                preferred_element_type=F32,
            )
        lifted = lifted.reshape(sources, 2, rows // 2, band_rows)
        both = jnp.concatenate([lifted[:, 0], lifted[:, 1]], axis=-1)
        both = both.reshape(tall, 2 * band_rows).astype(BF16)
        extra = two_parts(extra, spare_ref)
        for z in range(Z_LO):
            out_ref[z_half * Z_LO + z, :tall, :] = both
            out_ref[z_half * Z_LO + z, tall:, :] = extra


def sin_cos(angle):
    turns = jnp.round(angle * (2.0 / math.pi))
    rest = angle - turns * 1.5703125
    rest = rest - turns * 4.837512969970703125e-4
    rest = rest - turns * 7.54978995489188216e-8
    square = rest * rest
    sine = -1.9515295891e-4 * square + 8.3321608736e-3
    sine = (sine * square - 1.6666654611e-1) * square * rest + rest
    cosine = 2.443315711809948e-5 * square - 1.388731625493765e-3
    cosine = (cosine * square + 4.166664568298827e-2) * square * square - 0.5 * square + 1.0
    quarter = turns.astype(jnp.int32) & 3
    swap = (quarter & 1) == 1
    sin_out = jnp.where(swap, cosine, sine)
    cos_out = jnp.where(swap, sine, cosine)
    sin_out = jnp.where(quarter >= 2, -sin_out, sin_out)
    cos_out = jnp.where((quarter == 1) | (quarter == 2), -cos_out, cos_out)
    return sin_out, cos_out


FINE = 16
STEP = 2 * TAPS_K + 1


def make_table(
    after_ref,
    ramp_hbm,
    taps_hbm,
    step_hbm,
    near_ref,
    fine_ref,
    coarse_ref,
    tap_rows_ref,
    ramp_ref,
    taps_ref,
    step_ref,
    rate_ref,
    spare_ref,
    sem,
):
    del after_ref
    copies = [
        pltpu.make_async_copy(ramp_hbm, ramp_ref, sem.at[0]),
        pltpu.make_async_copy(taps_hbm, taps_ref, sem.at[1]),
        pltpu.make_async_copy(step_hbm, step_ref, sem.at[2]),
    ]
    for copy in copies:
        copy.start()
    _, z_lo, x, _ = place_of()
    n_groups = ramp_ref.shape[0]
    half = near_ref.shape[0]
    for copy in copies:
        copy.wait()
    for t in range(2 * TAPS_K + 1):
        tap_rows_ref[t : t + 1, :] = jnp.full((1, LANES), taps_ref[t], F32)
    scale = 1.0 / math.sqrt(n_groups * LANES)
    tap_rows_ref[STEP : STEP + 1, :] = jnp.full((1, LANES), step_ref[0] * scale, F32)
    tap_rows_ref[STEP + 1 : STEP + 2, :] = jnp.full((1, LANES), step_ref[0] * step_ref[1], F32)

    lane = lax.broadcasted_iota(jnp.int32, (1, LANES), 1)
    ends = jnp.zeros((1, LANES), F32)
    for i in range(Z_LO):
        group = i * N_X + x
        rate_ref[i : i + 1, :] = ramp_ref[pl.ds(group, 1), :]
        before = ramp_ref[pl.ds((group + n_groups - 1) % n_groups, 1), :]
        after = ramp_ref[pl.ds((group + 1) % n_groups, 1), :]
        place = 2 * EDGE * i
        move = (place + EDGE) % LANES
        before = pltpu.roll(before, move, 1) if move else before
        after = pltpu.roll(after, move, 1) if move else after
        ends = jnp.where((lane >= place) & (lane < place + EDGE), before, ends)
        ends = jnp.where((lane >= place + EDGE) & (lane < place + 2 * EDGE), after, ends)
    rate_ref[Z_LO : Z_LO + 1, :] = ends

    n_coarse = 2 * half // FINE
    first = z_lo * 2 * half
    fine_step = lax.broadcasted_iota(jnp.int32, (FINE, LANES), 0).astype(F32)
    coarse_step = (
        first + FINE * lax.broadcasted_iota(jnp.int32, (n_coarse, LANES), 0)
    ).astype(F32)
    for i in range(Z_LO + 1):
        span = pl.ds(i * LANES, LANES)
        rate = rate_ref[i : i + 1, :]
        fine_sin, fine_cos = sin_cos(rate * fine_step)
        coarse_sin, coarse_cos = sin_cos(rate * coarse_step)
        fine_ref[0, :, span], fine_ref[1, :, span] = fine_sin, fine_cos
        spare_ref[0], spare_ref[1] = coarse_sin, coarse_cos
        coarse_ref[0, :, span] = coarse_sin[n_coarse // 2 :]
        coarse_ref[1, :, span] = coarse_cos[n_coarse // 2 :]
        for a in range(n_coarse // 2):
            fill(
                near_ref,
                a * FINE,
                i,
                (spare_ref[0, a : a + 1, :], spare_ref[1, a : a + 1, :]),
                (fine_sin, fine_cos),
            )


def fill(table_ref, row, i, coarse, fine):
    depth = table_ref.shape[1] // 2
    (s, c), (fine_sin, fine_cos) = coarse, fine
    table_ref[row : row + FINE, i * LANES : (i + 1) * LANES] = (
        c * fine_cos - s * fine_sin
    ).astype(BF16)
    table_ref[row : row + FINE, depth + i * LANES : depth + (i + 1) * LANES] = (
        s * fine_cos + c * fine_sin
    ).astype(BF16)


def sum_pulses(
    tap_rows_ref,
    near_ref,
    fine_ref,
    coarse_ref,
    lifted_ref,
    column_ref,
    edge_ref,
    out_ref,
    mine_ref,
    edge_out_ref,
    pad_ref,
    blend_ref,
    far_ref,
    total_ref,
    spare_ref,
):
    z_hi, z_lo, x, yc = place_of()
    width = lifted_ref.shape[2]
    half_pulses = LANES // Z_HI
    main = Z_LO * LANES
    depth = main + LANES
    blocks, columns = out_ref.shape[0], out_ref.shape[1] - EDGE

    zero = jnp.zeros((2 * EDGE, width), F32)
    pad_ref[: 2 * EDGE] = zero
    pad_ref[2 * EDGE + LANES :] = zero
    for i in range(Z_LO):
        for h in range(Z_HI):
            pad_ref[pl.ds(2 * EDGE + h * half_pulses, half_pulses), :] = lifted_ref[
                h * Z_LO + i, :half_pulses, :
            ].astype(F32)
        blended = jnp.zeros((LANES + 2 * EDGE, width), F32)
        for t in range(2 * TAPS_K + 1):
            blended = blended + tap_rows_ref[t : t + 1, :] * pad_ref[
                pl.ds(EDGE - TAPS_K + t, LANES + 2 * EDGE), :
            ]
        turned = pltpu.roll(blended, width // 2, 1)
        lane_full = lax.broadcasted_iota(jnp.int32, blended.shape, 1)
        turned = jnp.where(lane_full < width // 2, -turned, turned)
        for k, value in enumerate((blended, turned)):
            value = value.astype(BF16)
            blend_ref[pl.ds(k * depth + i * LANES, LANES), :] = value[EDGE : EDGE + LANES]
            outside = jnp.concatenate([value[:EDGE], value[EDGE + LANES :]], axis=0)
            blend_ref[pl.ds(k * depth + main + i * 2 * EDGE, 2 * EDGE), :] = outside

    for i in range(Z_LO + 1):
        span = pl.ds(i * LANES, LANES)
        fine = fine_ref[0, :, span], fine_ref[1, :, span]
        for a in range(far_ref.shape[0] // FINE):
            coarse = coarse_ref[0, a : a + 1, span], coarse_ref[1, a : a + 1, span]
            fill(far_ref, a * FINE, i, coarse, fine)
    for block in range(blocks):
        table_ref = near_ref if block < blocks // 2 else far_ref
        row = block % (blocks // 2) * columns
        total = jnp.dot(
            table_ref[row : row + columns, :],
            blend_ref[...],
            preferred_element_type=F32,
        )
        total_ref[block] = total
        out_ref[block, :columns, :] = total.astype(BF16)
    mine_ref[...] = total_ref[x]

    def came(half, z):
        return joined(lifted_ref[half * Z_LO + z % Z_LO, half_pulses:, :])

    first_band = (z_hi == 1) & (yc == 0)
    last_band = (z_hi == 0) & (yc == N_YC - 1)
    foreign = came(1 - z_hi, z_lo)
    above = jnp.where(first_band, foreign, edge_ref[0:4])
    below = jnp.where(last_band, foreign, edge_ref[4:8])
    edge_out_ref[0:4] = above
    edge_out_ref[4:8] = below
    own = with_corners(column_ref[0:4], above, below)
    left = came(z_hi, z_lo + Z_LO - 1)
    left_fixed = with_corners(left, above, came(1 - z_hi, z_lo + Z_LO - 1))
    left = jnp.where(last_band, left_fixed, left)
    right = came(z_hi, z_lo + 1)
    right_fixed = with_corners(right, came(1 - z_hi, z_lo + 1), below)
    right = jnp.where(first_band, right_fixed, right)
    out_ref[:, columns:, :] = jnp.zeros((blocks, EDGE, LANES), BF16)
    after = two_parts(jnp.where(x < N_X - 1, own, left), spare_ref)
    before = two_parts(jnp.where(x > 0, own, right), spare_ref)
    out_ref[(x + 1) % N_X, columns:, :] = after
    out_ref[(x + N_X - 1) % N_X, columns:, :] = before


def finish(
    rows_ref, sums_ref, mine_ref, edge_ref, image_ref, out_ref, pad_ref, side_ref, flow_ref
):
    _, z_lo, x, _ = place_of()
    group = z_lo * N_X + x
    comps, rows, columns = image_ref.shape
    tall = pad_ref.shape[1]
    total = mine_ref[...]
    for k in range(1, N_X):
        total = total + sums_ref[(x + k) % N_X, :columns, :].astype(F32)
    step, weight = rows_ref[STEP : STEP + 1, :1], rows_ref[STEP + 1 : STEP + 2, :1]
    total = (total * step).T.reshape(image_ref.shape)

    zero = jnp.zeros((2, LANES), F32)
    left = joined(sums_ref[(x + N_X - 1) % N_X, columns:, :])[2:4]
    right = joined(sums_ref[(x + 1) % N_X, columns:, :])[0:2]
    side_ref[...] = jnp.zeros_like(side_ref)
    side_ref[0:2, :] = jnp.where(group > 0, left, zero)
    side_ref[2:4, :] = jnp.where(group < Z_LO * N_X - 1, right, zero)
    sides = side_ref[...].T[:tall]
    lane = lax.broadcasted_iota(jnp.int32, (tall, LANES), 1)
    blank = jnp.zeros((tall, LANES), F32)
    pad_ref[...] = jnp.zeros_like(pad_ref)
    for comp in range(comps):
        pad_ref[comp, EDGE : EDGE + rows, LANES : LANES + columns] = image_ref[comp]
        for half in range(2):
            span = pl.ds((1 + half) * LANES, LANES)
            pad_ref[comp, TOP : TOP + 1, span] = edge_ref[2 * comp + half : 2 * comp + half + 1, :]
            pad_ref[comp, LOW : LOW + 1, span] = edge_ref[4 + 2 * comp + half : 5 + 2 * comp + half, :]
        pad_ref[comp, :, :LANES] = jnp.where(lane == LANES - 1, sides[:, comp : comp + 1], blank)
        pad_ref[comp, :, LANES + columns :] = jnp.where(
            lane == 0, sides[:, 2 + comp : 3 + comp], blank
        )

    high, wide = rows + EDGE, columns + LANES
    row_step, col_step = [], []
    square = jnp.zeros((high, wide), F32) + smooth_eps
    for comp in range(comps):
        here = pad_ref[comp, :high, :]
        following = pltpu.roll(here, here.shape[1] - 1, 1)[:, :wide]
        here = here[:, :wide]
        row_step.append(pad_ref[comp, 1 : high + 1, :wide] - here)
        col_step.append(following - here)
        square = square + row_step[-1] * row_step[-1] + col_step[-1] * col_step[-1]
    inverse = lax.rsqrt(square)
    for comp in range(comps):
        row_flow = row_step[comp] * inverse
        col_flow = col_step[comp] * inverse
        flow_ref[...] = row_flow
        across = col_flow - pltpu.roll(col_flow, 1, 1)
        down = row_flow[EDGE:, LANES:] - flow_ref[EDGE - 1 : high - 1, LANES:]
        variation = -(down + across[EDGE:, LANES:])
        out_ref[comp] = image_ref[comp] - (total[comp] + weight * variation)


def in_hbm(*values):
    return tuple(pltpu.with_memory_space_constraint(value, pltpu.HBM) for value in values)


def call(kernel, out_shape, in_specs, args, scratch=(), cost=None, out_specs=None):
    if out_specs is None:
        out_specs = [VMEM] * len(out_shape) if isinstance(out_shape, tuple) else VMEM
    return pl.pallas_call(
        kernel,
        out_shape=out_shape,
        in_specs=in_specs,
        out_specs=out_specs,
        scratch_shapes=scratch,
        cost_estimate=cost,
        compiler_params=pltpu.CompilerParams(vmem_limit_bytes=16 * 1024 * 1024),
    )(*args)


def local(
    pulse_data,
    window_start,
    footprint,
    range_to_row_weight,
    slow_taps,
    ramp_rate,
    image_now,
    step_and_variation_weight,
):
    band_count = lax.axis_size("band")
    groups = lax.axis_size("aper")
    comps, pulses, bins = pulse_data.shape
    band_rows, window_len = range_to_row_weight.shape
    columns = image_now.shape[2]
    shape = jax.ShapeDtypeStruct

    block = window_len // LANES * comps * pulses
    windows, sent_weight = call(
        cut_windows,
        (
            shape((N_YC, Z_HI * block + EDGE, LANES), BF16),
            shape(range_to_row_weight.shape, BF16),
        ),
        [HBM] * 5,
        in_hbm(window_start, footprint, pulse_data, image_now, range_to_row_weight),
        [
            pltpu.SMEM(window_start.shape, jnp.int32),
            pltpu.SMEM(footprint.shape, jnp.int32),
            pltpu.VMEM(pulse_data.shape, BF16),
            pltpu.VMEM((2, comps, EDGE, columns), F32),
            pltpu.VMEM((pulses * comps * (bins // LANES + 1), LANES), F32),
            pltpu.VMEM((band_count * block, LANES), F32),
            pltpu.VMEM((EDGE, LANES), F32),
            pltpu.SemaphoreType.DMA((6,)),
        ],
    )
    other_weight = lax.ppermute(sent_weight, ("aper", "band"), halves_swapped())
    in_plane = [[h * N_YC + i for i in range(N_YC)] for h in range(Z_HI)]
    windows = lax.all_to_all(windows, "band", 0, 0, axis_index_groups=in_plane, tiled=True)
    side, weights = call(
        side_columns,
        (shape((EDGE, LANES), F32), shape((Z_HI, band_rows, window_len), BF16)),
        [HBM, HBM, VMEM],
        (*in_hbm(image_now, range_to_row_weight), other_weight),
        [
            pltpu.VMEM((LANES, LANES), F32),
            pltpu.VMEM((2, comps, band_rows, LANES), F32),
            pltpu.SemaphoreType.DMA((3,)),
        ],
        pl.CostEstimate(flops=1 << 34, bytes_accessed=1 << 27, transcendentals=0),
    )
    width = comps * band_rows
    lifted, edges = call(
        lift_windows,
        (
            shape((N_Z, N_YC * pulses + EDGE, width), BF16),
            shape((EDGE, LANES), F32),
        ),
        [VMEM] * 3,
        (windows, weights, side),
        [pltpu.VMEM((EDGE, LANES), F32)],
    )
    lifted = lax.all_to_all(lifted, ("aper", "band"), 0, 0, axis_index_groups=z_rings(), tiled=True)
    depth = (Z_LO + 1) * LANES
    half = N_X * columns // 2
    near, fine, coarse, tap_rows = call(
        make_table,
        (
            shape((half, 2 * depth), BF16),
            shape((2, FINE, depth), F32),
            shape((2, half // FINE, depth), F32),
            shape((EDGE, LANES), F32),
        ),
        [ANY, HBM, HBM, HBM],
        (
            edges,
            *in_hbm(ramp_rate.reshape(groups, LANES), slow_taps, step_and_variation_weight),
        ),
        [
            pltpu.VMEM((groups, LANES), F32),
            pltpu.SMEM(slow_taps.shape, F32),
            pltpu.SMEM(step_and_variation_weight.shape, F32),
            pltpu.VMEM((2 * EDGE, LANES), F32),
            pltpu.VMEM((2, 2 * half // FINE, LANES), F32),
            pltpu.SemaphoreType.DMA((3,)),
        ],
        pl.CostEstimate(flops=1 << 24, bytes_accessed=1 << 23, transcendentals=0),
    )
    sums, mine, edges = call(
        sum_pulses,
        (
            shape((N_X, columns + EDGE, width), BF16),
            shape((columns, width), F32),
            shape((EDGE, LANES), F32),
        ),
        [VMEM] * 7,
        (tap_rows, near, fine, coarse, lifted, side, edges),
        [
            pltpu.VMEM((LANES + 4 * EDGE, width), F32),
            pltpu.VMEM((2 * depth, width), BF16),
            pltpu.VMEM((half, 2 * depth), BF16),
            pltpu.VMEM((N_X, columns, width), F32),
            pltpu.VMEM((EDGE, LANES), F32),
        ],
    )
    along_x = [[z * N_X + x for x in range(N_X)] for z in range(Z_LO)]
    sums = lax.all_to_all(sums, "aper", 0, 0, axis_index_groups=along_x, tiled=True)
    return call(
        finish,
        shape(image_now.shape, F32),
        [VMEM] * 5,
        (tap_rows, sums, mine, edges, image_now),
        [
            pltpu.VMEM((comps, band_rows + 2 * EDGE, columns + 2 * LANES), F32),
            pltpu.VMEM((LANES, LANES), F32),
            pltpu.VMEM((band_rows + EDGE, columns + LANES), F32),
        ],
    )


def solution(mesh):
    return jax.shard_map(
        local,
        mesh=mesh,
        in_specs=(
            P(None, ("aper", "band"), None),
            P(("aper", "band"), None),
            P(("aper", "band"), None),
            P("band", None),
            P(),
            P(),
            P(None, "band", "aper"),
            P(),
        ),
        out_specs=P(None, "band", "aper"),
        check_vma=False,
    )
```

```python
import functools
import math

import jax
import jax.numpy as jnp
from jax import lax
from jax.experimental import pallas as pl
from jax.experimental.pallas import tpu as pltpu
from jax.sharding import PartitionSpec as P

TAPS_K = 2
LANES = 128
EDGE = 8
Z_HI, Z_LO, N_X, N_YC = 2, 8, 4, 8
N_Z = Z_HI * Z_LO
FIRST_Z = 8
smooth_eps = 0.05
BF16, F32 = jnp.bfloat16, jnp.float32
VMEM = pl.BlockSpec(memory_space=pltpu.VMEM)
SMEM = pl.BlockSpec(memory_space=pltpu.SMEM)
ANY = pl.BlockSpec(memory_space=pl.ANY)
HBM = pl.BlockSpec(memory_space=pltpu.HBM)


def device_index(z_hi, z_lo, x, yc):
    return ((z_lo * N_X + x) * Z_HI + z_hi) * N_YC + yc


def z_rings():
    order = [(FIRST_Z + k) % N_Z for k in range(N_Z)]
    return [
        [device_index(z // Z_LO, z % Z_LO, x, yc) for z in order]
        for x in range(N_X)
        for yc in range(N_YC)
    ]


def in_ring(z):
    return (z + N_Z - FIRST_Z) % N_Z


def halves_swapped():
    return [
        (device_index(h, z, x, yc), device_index(1 - h, (z + Z_LO // 2) % Z_LO, x, yc))
        for h in range(Z_HI)
        for z in range(Z_LO)
        for x in range(N_X)
        for yc in range(N_YC)
    ]


def place_of():
    group, band = lax.axis_index("aper"), lax.axis_index("band")
    return band // N_YC, group // N_X, group % N_X, band % N_YC


def two_parts(value, spare_ref):
    first = value.astype(BF16).astype(F32)
    spare_ref[0:4] = first
    spare_ref[4:8] = value - first
    return spare_ref[...].astype(BF16)


def joined(rows):
    rows = rows.astype(F32)
    return rows[0:4] + rows[4:8]


TOP, LOW = EDGE - 1, EDGE + 64


def with_corners(columns, above, below):
    lane = lax.broadcasted_iota(jnp.int32, columns.shape, 1)
    row = lax.broadcasted_iota(jnp.int32, columns.shape, 0)
    above = pltpu.roll(above, TOP, 1)
    below = pltpu.roll(below, (LOW + 1) % LANES, 1)
    for comp in range(2):
        columns = jnp.where((lane == TOP) & (row == comp), above[2 * comp : 2 * comp + 1], columns)
        columns = jnp.where(
            (lane == LOW) & (row == 2 + comp), below[2 * comp + 1 : 2 * comp + 2], columns
        )
    return columns


def cut_windows(wanted, start_hbm, foot_hbm, pulse_hbm, image_hbm, *refs):
    (
        out_hbm,
        start_ref,
        foot_ref,
        pulse_ref,
        edge_ref,
        flat_ref,
        window_ref,
        packed_ref,
        spare_ref,
        sem,
        out_sem,
    ) = refs[-11:]

    @pl.when(place_of()[0] == wanted)
    def _():
        rows = image_hbm.shape[1]
        copies = [
            pltpu.make_async_copy(pulse_hbm, pulse_ref, sem.at[0]),
            pltpu.make_async_copy(start_hbm, start_ref, sem.at[1]),
            pltpu.make_async_copy(foot_hbm, foot_ref, sem.at[2]),
            pltpu.make_async_copy(image_hbm.at[:, pl.ds(0, EDGE), :], edge_ref.at[0], sem.at[3]),
            pltpu.make_async_copy(image_hbm.at[:, pl.ds(rows - EDGE, EDGE), :], edge_ref.at[1], sem.at[4]),
        ]
        for copy in copies:
            copy.start()
        window_ref[...] = jnp.zeros_like(window_ref)
        comps, pulses, bins = pulse_ref.shape
        parts = bins // LANES
        pitch = comps * (parts + 1)
        block = window_ref.shape[0] // (Z_HI * N_YC)
        for copy in copies:
            copy.wait()
        for part in range(parts):
            for comp in range(comps):
                flat_ref[pl.ds(part * comps + comp, pulses, stride=pitch), :] = pulse_ref[
                    comp, :, part * LANES : (part + 1) * LANES
                ].astype(F32)
        lane = lax.broadcasted_iota(jnp.int32, (block // pulses, LANES), 1)
        for pulse in range(pulses):
            for k in range(foot_ref.shape[1]):
                band = foot_ref[pulse, k]
                start = start_ref[pulse, band]
                row = pulse * pitch + comps * (start >> 7)
                shift = start & (LANES - 1)
                here = flat_ref[pl.ds(row, block // pulses), :]
                following = flat_ref[pl.ds(row + comps, block // pulses), :]
                both = jnp.where(lane >= shift, here, following)
                both = pltpu.roll(both, (LANES - shift) & (LANES - 1), 1)
                place = ((band & (N_YC - 1)) * Z_HI + (band >> 3)) * block + pulse
                window_ref[pl.ds(place, block // pulses, stride=pulses), :] = both
        tall = Z_HI * block
        packed_ref[:, tall:, :] = jnp.zeros((N_YC, EDGE, LANES), BF16)
        yc = place_of()[3]
        for side, line, to in ((0, 0, yc + N_YC - 1), (1, EDGE - 1, yc + 1)):
            edge = [edge_ref[side, comp, line : line + 1, :] for comp in range(comps)]
            edge = [e[:, i * LANES : (i + 1) * LANES] for e in edge for i in range(2)]
            packed_ref[to % N_YC, tall:, :] = two_parts(jnp.concatenate(edge, axis=0), spare_ref)
        leaving = []
        for to in range(N_YC):
            packed_ref[to, :tall, :] = window_ref[to * tall : (to + 1) * tall, :].astype(BF16)
            leaving.append(pltpu.make_async_copy(packed_ref.at[to], out_hbm.at[to], out_sem.at[to]))
            leaving[-1].start()
        for copy in leaving:
            copy.wait()


def side_columns(image_hbm, weight_hbm, other_ref, out_ref, weight_ref, pad_ref, block_ref, sem):
    z_hi = place_of()[0]
    rows, columns = image_hbm.shape[1:]
    copies = [
        pltpu.make_async_copy(weight_hbm, weight_ref.at[z_hi], sem.at[0]),
        pltpu.make_async_copy(image_hbm.at[:, :, pl.ds(0, LANES)], block_ref.at[0], sem.at[1]),
        pltpu.make_async_copy(
            image_hbm.at[:, :, pl.ds(columns - LANES, LANES)], block_ref.at[1], sem.at[2]
        ),
    ]
    for copy in copies:
        copy.start()
    weight_ref[1 - z_hi] = other_ref[...]
    pad_ref[...] = jnp.zeros_like(pad_ref)
    out_ref[...] = jnp.zeros_like(out_ref)
    for copy in copies:
        copy.wait()
    for comp in range(2):
        for side, line in ((0, 0), (1, LANES - 1)):
            pad_ref[EDGE : EDGE + rows, :] = block_ref[side, comp]
            out_ref[2 * side + comp : 2 * side + comp + 1, :] = pad_ref[...].T[line : line + 1, :]


def lift_windows(
    window_ref, weight_ref, column_ref, out_ref, edge_ref, spare_ref
):
    z_hi, _, _, yc = place_of()
    sources, height = window_ref.shape[0], window_ref.shape[1] - EDGE
    half = height // Z_HI
    band_rows, window_len = weight_ref.shape[1:]
    parts = window_len // LANES
    rows = half // parts
    tall = sources * rows // 2

    above = joined(window_ref[(yc + N_YC - 1) % N_YC, height:, :])
    below = joined(window_ref[(yc + 1) % N_YC, height:, :])
    foreign = jnp.where(yc == 0, above, below)
    above = jnp.where(yc > 0, above, jnp.zeros_like(above))
    below = jnp.where(yc < N_YC - 1, below, jnp.zeros_like(below))
    edge_ref[0:4] = above
    edge_ref[4:8] = below
    columns = with_corners(column_ref[0:4], above, below)

    dims = (((1,), (1,)), ((), ()))
    for z_half in range(Z_HI):
        extra = jnp.where(z_half == z_hi, columns, foreign)
        lifted = jnp.zeros((sources * rows, band_rows), F32)
        for part in range(parts):
            first = z_half * half + part * rows
            piece = window_ref[:, pl.ds(first, rows), :].reshape(sources * rows, LANES)
            lifted = lifted + lax.dot_general(
                piece,
                weight_ref[z_half, :, part * LANES : (part + 1) * LANES],
                dims,
                preferred_element_type=F32,
            )
        lifted = lifted.reshape(sources, 2, rows // 2, band_rows)
        both = jnp.concatenate([lifted[:, 0], lifted[:, 1]], axis=-1)
        both = both.reshape(tall, 2 * band_rows).astype(BF16)
        extra = two_parts(extra, spare_ref)
        for z in range(Z_LO):
            out_ref[in_ring(z_half * Z_LO + z), :tall, :] = both
            out_ref[in_ring(z_half * Z_LO + z), tall:, :] = extra


def sin_cos(angle):
    turns = jnp.round(angle * (2.0 / math.pi))
    rest = angle - turns * 1.5703125
    rest = rest - turns * 4.837512969970703125e-4
    rest = rest - turns * 7.54978995489188216e-8
    square = rest * rest
    sine = -1.9515295891e-4 * square + 8.3321608736e-3
    sine = (sine * square - 1.6666654611e-1) * square * rest + rest
    cosine = 2.443315711809948e-5 * square - 1.388731625493765e-3
    cosine = (cosine * square + 4.166664568298827e-2) * square * square - 0.5 * square + 1.0
    quarter = turns.astype(jnp.int32) & 3
    swap = (quarter & 1) == 1
    sin_out = jnp.where(swap, cosine, sine)
    cos_out = jnp.where(swap, sine, cosine)
    sin_out = jnp.where(quarter >= 2, -sin_out, sin_out)
    cos_out = jnp.where((quarter == 1) | (quarter == 2), -cos_out, cos_out)
    return sin_out, cos_out


FINE = 16
STEP = 2 * TAPS_K + 1


def make_table(
    after_ref,
    ramp_hbm,
    taps_hbm,
    step_hbm,
    near_ref,
    fine_ref,
    coarse_ref,
    tap_rows_ref,
    ramp_ref,
    taps_ref,
    step_ref,
    rate_ref,
    spare_ref,
    sem,
):
    del after_ref
    copies = [
        pltpu.make_async_copy(ramp_hbm, ramp_ref, sem.at[0]),
        pltpu.make_async_copy(taps_hbm, taps_ref, sem.at[1]),
        pltpu.make_async_copy(step_hbm, step_ref, sem.at[2]),
    ]
    for copy in copies:
        copy.start()
    _, z_lo, x, _ = place_of()
    n_groups = ramp_ref.shape[0]
    half = near_ref.shape[0]
    for copy in copies:
        copy.wait()
    for t in range(2 * TAPS_K + 1):
        tap_rows_ref[t : t + 1, :] = jnp.full((1, LANES), taps_ref[t], F32)
    scale = 1.0 / math.sqrt(n_groups * LANES)
    tap_rows_ref[STEP : STEP + 1, :] = jnp.full((1, LANES), step_ref[0] * scale, F32)
    tap_rows_ref[STEP + 1 : STEP + 2, :] = jnp.full((1, LANES), step_ref[0] * step_ref[1], F32)

    lane = lax.broadcasted_iota(jnp.int32, (1, LANES), 1)
    ends = jnp.zeros((1, LANES), F32)
    for i in range(Z_LO):
        group = i * N_X + x
        rate_ref[i : i + 1, :] = ramp_ref[pl.ds(group, 1), :]
        before = ramp_ref[pl.ds((group + n_groups - 1) % n_groups, 1), :]
        after = ramp_ref[pl.ds((group + 1) % n_groups, 1), :]
        place = 2 * EDGE * i
        move = (place + EDGE) % LANES
        before = pltpu.roll(before, move, 1) if move else before
        after = pltpu.roll(after, move, 1) if move else after
        ends = jnp.where((lane >= place) & (lane < place + EDGE), before, ends)
        ends = jnp.where((lane >= place + EDGE) & (lane < place + 2 * EDGE), after, ends)
    rate_ref[Z_LO : Z_LO + 1, :] = ends

    n_coarse = 2 * half // FINE
    first = z_lo * 2 * half
    fine_step = lax.broadcasted_iota(jnp.int32, (FINE, LANES), 0).astype(F32)
    coarse_step = (
        first + FINE * lax.broadcasted_iota(jnp.int32, (n_coarse, LANES), 0)
    ).astype(F32)
    for i in range(Z_LO + 1):
        span = pl.ds(i * LANES, LANES)
        rate = rate_ref[i : i + 1, :]
        fine_sin, fine_cos = sin_cos(rate * fine_step)
        coarse_sin, coarse_cos = sin_cos(rate * coarse_step)
        fine_ref[0, :, span], fine_ref[1, :, span] = fine_sin, fine_cos
        spare_ref[0], spare_ref[1] = coarse_sin, coarse_cos
        coarse_ref[0, :, span] = coarse_sin[n_coarse // 2 :]
        coarse_ref[1, :, span] = coarse_cos[n_coarse // 2 :]
        for a in range(n_coarse // 2):
            fill(
                near_ref,
                a * FINE,
                i,
                (spare_ref[0, a : a + 1, :], spare_ref[1, a : a + 1, :]),
                (fine_sin, fine_cos),
            )


def fill(table_ref, row, i, coarse, fine):
    depth = table_ref.shape[1] // 2
    (s, c), (fine_sin, fine_cos) = coarse, fine
    table_ref[row : row + FINE, i * LANES : (i + 1) * LANES] = (
        c * fine_cos - s * fine_sin
    ).astype(BF16)
    table_ref[row : row + FINE, depth + i * LANES : depth + (i + 1) * LANES] = (
        s * fine_cos + c * fine_sin
    ).astype(BF16)


def sum_pulses(
    tap_rows_ref,
    near_ref,
    fine_ref,
    coarse_ref,
    lifted_ref,
    column_ref,
    edge_ref,
    out_ref,
    mine_ref,
    edge_out_ref,
    pad_ref,
    blend_ref,
    far_ref,
    total_ref,
    spare_ref,
):
    z_hi, z_lo, x, yc = place_of()
    width = lifted_ref.shape[2]
    half_pulses = LANES // Z_HI
    main = Z_LO * LANES
    depth = main + LANES
    blocks, columns = out_ref.shape[0], out_ref.shape[1] - EDGE

    zero = jnp.zeros((2 * EDGE, width), F32)
    pad_ref[: 2 * EDGE] = zero
    pad_ref[2 * EDGE + LANES :] = zero
    for i in range(Z_LO):
        for h in range(Z_HI):
            pad_ref[pl.ds(2 * EDGE + h * half_pulses, half_pulses), :] = lifted_ref[
                in_ring(h * Z_LO + i), :half_pulses, :
            ].astype(F32)
        blended = jnp.zeros((LANES + 2 * EDGE, width), F32)
        for t in range(2 * TAPS_K + 1):
            blended = blended + tap_rows_ref[t : t + 1, :] * pad_ref[
                pl.ds(EDGE - TAPS_K + t, LANES + 2 * EDGE), :
            ]
        turned = pltpu.roll(blended, width // 2, 1)
        lane_full = lax.broadcasted_iota(jnp.int32, blended.shape, 1)
        turned = jnp.where(lane_full < width // 2, -turned, turned)
        for k, value in enumerate((blended, turned)):
            value = value.astype(BF16)
            blend_ref[pl.ds(k * depth + i * LANES, LANES), :] = value[EDGE : EDGE + LANES]
            outside = jnp.concatenate([value[:EDGE], value[EDGE + LANES :]], axis=0)
            blend_ref[pl.ds(k * depth + main + i * 2 * EDGE, 2 * EDGE), :] = outside

    for i in range(Z_LO + 1):
        span = pl.ds(i * LANES, LANES)
        fine = fine_ref[0, :, span], fine_ref[1, :, span]
        for a in range(far_ref.shape[0] // FINE):
            coarse = coarse_ref[0, a : a + 1, span], coarse_ref[1, a : a + 1, span]
            fill(far_ref, a * FINE, i, coarse, fine)
    for block in range(blocks):
        table_ref = near_ref if block < blocks // 2 else far_ref
        row = block % (blocks // 2) * columns
        total = jnp.dot(
            table_ref[row : row + columns, :],
            blend_ref[...],
            preferred_element_type=F32,
        )
        total_ref[block] = total
        out_ref[block, :columns, :] = total.astype(BF16)
    mine_ref[...] = total_ref[x]

    def came(half, z):
        return joined(lifted_ref[in_ring(half * Z_LO + z % Z_LO), half_pulses:, :])

    first_band = (z_hi == 1) & (yc == 0)
    last_band = (z_hi == 0) & (yc == N_YC - 1)
    foreign = came(1 - z_hi, z_lo)
    above = jnp.where(first_band, foreign, edge_ref[0:4])
    below = jnp.where(last_band, foreign, edge_ref[4:8])
    edge_out_ref[0:4] = above
    edge_out_ref[4:8] = below
    own = with_corners(column_ref[0:4], above, below)
    left = came(z_hi, z_lo + Z_LO - 1)
    left_fixed = with_corners(left, above, came(1 - z_hi, z_lo + Z_LO - 1))
    left = jnp.where(last_band, left_fixed, left)
    right = came(z_hi, z_lo + 1)
    right_fixed = with_corners(right, came(1 - z_hi, z_lo + 1), below)
    right = jnp.where(first_band, right_fixed, right)
    out_ref[:, columns:, :] = jnp.zeros((blocks, EDGE, LANES), BF16)
    after = two_parts(jnp.where(x < N_X - 1, own, left), spare_ref)
    before = two_parts(jnp.where(x > 0, own, right), spare_ref)
    out_ref[(x + 1) % N_X, columns:, :] = after
    out_ref[(x + N_X - 1) % N_X, columns:, :] = before


def finish(
    rows_ref, sums_ref, mine_ref, edge_ref, image_ref, out_ref, pad_ref, side_ref, flow_ref
):
    _, z_lo, x, _ = place_of()
    group = z_lo * N_X + x
    comps, rows, columns = image_ref.shape
    tall = pad_ref.shape[1]
    total = mine_ref[...]
    for k in range(1, N_X):
        total = total + sums_ref[(x + k) % N_X, :columns, :].astype(F32)
    step, weight = rows_ref[STEP : STEP + 1, :1], rows_ref[STEP + 1 : STEP + 2, :1]
    total = (total * step).T.reshape(image_ref.shape)

    zero = jnp.zeros((2, LANES), F32)
    left = joined(sums_ref[(x + N_X - 1) % N_X, columns:, :])[2:4]
    right = joined(sums_ref[(x + 1) % N_X, columns:, :])[0:2]
    side_ref[...] = jnp.zeros_like(side_ref)
    side_ref[0:2, :] = jnp.where(group > 0, left, zero)
    side_ref[2:4, :] = jnp.where(group < Z_LO * N_X - 1, right, zero)
    sides = side_ref[...].T[:tall]
    lane = lax.broadcasted_iota(jnp.int32, (tall, LANES), 1)
    blank = jnp.zeros((tall, LANES), F32)
    pad_ref[...] = jnp.zeros_like(pad_ref)
    for comp in range(comps):
        pad_ref[comp, EDGE : EDGE + rows, LANES : LANES + columns] = image_ref[comp]
        for half in range(2):
            span = pl.ds((1 + half) * LANES, LANES)
            pad_ref[comp, TOP : TOP + 1, span] = edge_ref[2 * comp + half : 2 * comp + half + 1, :]
            pad_ref[comp, LOW : LOW + 1, span] = edge_ref[4 + 2 * comp + half : 5 + 2 * comp + half, :]
        pad_ref[comp, :, :LANES] = jnp.where(lane == LANES - 1, sides[:, comp : comp + 1], blank)
        pad_ref[comp, :, LANES + columns :] = jnp.where(
            lane == 0, sides[:, 2 + comp : 3 + comp], blank
        )

    high, wide = rows + EDGE, columns + LANES
    row_step, col_step = [], []
    square = jnp.zeros((high, wide), F32) + smooth_eps
    for comp in range(comps):
        here = pad_ref[comp, :high, :]
        following = pltpu.roll(here, here.shape[1] - 1, 1)[:, :wide]
        here = here[:, :wide]
        row_step.append(pad_ref[comp, 1 : high + 1, :wide] - here)
        col_step.append(following - here)
        square = square + row_step[-1] * row_step[-1] + col_step[-1] * col_step[-1]
    inverse = lax.rsqrt(square)
    for comp in range(comps):
        row_flow = row_step[comp] * inverse
        col_flow = col_step[comp] * inverse
        flow_ref[...] = row_flow
        across = col_flow - pltpu.roll(col_flow, 1, 1)
        down = row_flow[EDGE:, LANES:] - flow_ref[EDGE - 1 : high - 1, LANES:]
        variation = -(down + across[EDGE:, LANES:])
        out_ref[comp] = image_ref[comp] - (total[comp] + weight * variation)


def in_hbm(*values):
    return tuple(pltpu.with_memory_space_constraint(value, pltpu.HBM) for value in values)


def call(kernel, out_shape, in_specs, args, scratch=(), cost=None, out_specs=None):
    if out_specs is None:
        out_specs = [VMEM] * len(out_shape) if isinstance(out_shape, tuple) else VMEM
    return pl.pallas_call(
        kernel,
        out_shape=out_shape,
        in_specs=in_specs,
        out_specs=out_specs,
        scratch_shapes=scratch,
        cost_estimate=cost,
        compiler_params=pltpu.CompilerParams(vmem_limit_bytes=16 * 1024 * 1024),
    )(*args)


def local(
    pulse_data,
    window_start,
    footprint,
    range_to_row_weight,
    slow_taps,
    ramp_rate,
    image_now,
    step_and_variation_weight,
):
    band_count = lax.axis_size("band")
    groups = lax.axis_size("aper")
    comps, pulses, bins = pulse_data.shape
    band_rows, window_len = range_to_row_weight.shape
    columns = image_now.shape[2]
    shape = jax.ShapeDtypeStruct

    block = window_len // LANES * comps * pulses
    given = in_hbm(window_start, footprint, pulse_data, image_now)
    windows = ()
    weight = range_to_row_weight
    for wanted in range(Z_HI):
        windows = pl.pallas_call(
            functools.partial(cut_windows, wanted),
            out_shape=pltpu.HBM((N_YC, Z_HI * block + EDGE, LANES), BF16),
            in_specs=[HBM] * (len(given) + len(windows)),
            out_specs=HBM,
            scratch_shapes=[
                pltpu.SMEM(window_start.shape, jnp.int32),
                pltpu.SMEM(footprint.shape, jnp.int32),
                pltpu.VMEM(pulse_data.shape, BF16),
                pltpu.VMEM((2, comps, EDGE, columns), F32),
                pltpu.VMEM((pulses * comps * (bins // LANES + 1), LANES), F32),
                pltpu.VMEM((band_count * block, LANES), F32),
                pltpu.VMEM((N_YC, Z_HI * block + EDGE, LANES), BF16),
                pltpu.VMEM((EDGE, LANES), F32),
                pltpu.SemaphoreType.DMA((5,)),
                pltpu.SemaphoreType.DMA((N_YC,)),
            ],
            input_output_aliases={len(given): 0} if windows else {},
            compiler_params=pltpu.CompilerParams(vmem_limit_bytes=16 * 1024 * 1024),
        )(*given, *windows)
        if wanted == 0:
            weight, windows = lax.optimization_barrier((weight, windows))
            other_weight = lax.ppermute(weight, ("aper", "band"), halves_swapped())
            windows = (windows,)
    in_plane = [[h * N_YC + i for i in range(N_YC)] for h in range(Z_HI)]
    windows = lax.all_to_all(windows, "band", 0, 0, axis_index_groups=in_plane, tiled=True)
    side, weights = call(
        side_columns,
        (shape((EDGE, LANES), F32), shape((Z_HI, band_rows, window_len), BF16)),
        [HBM, HBM, VMEM],
        (*in_hbm(image_now, range_to_row_weight), other_weight),
        [
            pltpu.VMEM((LANES, LANES), F32),
            pltpu.VMEM((2, comps, band_rows, LANES), F32),
            pltpu.SemaphoreType.DMA((3,)),
        ],
        pl.CostEstimate(flops=1 << 34, bytes_accessed=1 << 27, transcendentals=0),
    )
    width = comps * band_rows
    lifted, edges = call(
        lift_windows,
        (
            shape((N_Z, N_YC * pulses + EDGE, width), BF16),
            shape((EDGE, LANES), F32),
        ),
        [VMEM] * 3,
        (windows, weights, side),
        [pltpu.VMEM((EDGE, LANES), F32)],
    )
    lifted = lax.all_to_all(lifted, ("aper", "band"), 0, 0, axis_index_groups=z_rings(), tiled=True)
    depth = (Z_LO + 1) * LANES
    half = N_X * columns // 2
    near, fine, coarse, tap_rows = call(
        make_table,
        (
            shape((half, 2 * depth), BF16),
            shape((2, FINE, depth), F32),
            shape((2, half // FINE, depth), F32),
            shape((EDGE, LANES), F32),
        ),
        [ANY, HBM, HBM, HBM],
        (
            edges,
            *in_hbm(ramp_rate.reshape(groups, LANES), slow_taps, step_and_variation_weight),
        ),
        [
            pltpu.VMEM((groups, LANES), F32),
            pltpu.SMEM(slow_taps.shape, F32),
            pltpu.SMEM(step_and_variation_weight.shape, F32),
            pltpu.VMEM((2 * EDGE, LANES), F32),
            pltpu.VMEM((2, 2 * half // FINE, LANES), F32),
            pltpu.SemaphoreType.DMA((3,)),
        ],
        pl.CostEstimate(flops=1 << 24, bytes_accessed=1 << 23, transcendentals=0),
    )
    sums, mine, edges = call(
        sum_pulses,
        (
            shape((N_X, columns + EDGE, width), BF16),
            shape((columns, width), F32),
            shape((EDGE, LANES), F32),
        ),
        [VMEM] * 7,
        (tap_rows, near, fine, coarse, lifted, side, edges),
        [
            pltpu.VMEM((LANES + 4 * EDGE, width), F32),
            pltpu.VMEM((2 * depth, width), BF16),
            pltpu.VMEM((half, 2 * depth), BF16),
            pltpu.VMEM((N_X, columns, width), F32),
            pltpu.VMEM((EDGE, LANES), F32),
        ],
    )
    along_x = [[z * N_X + x for x in range(N_X)] for z in range(Z_LO)]
    sums = lax.all_to_all(sums, "aper", 0, 0, axis_index_groups=along_x, tiled=True)
    return call(
        finish,
        shape(image_now.shape, F32),
        [VMEM] * 5,
        (tap_rows, sums, mine, edges, image_now),
        [
            pltpu.VMEM((comps, band_rows + 2 * EDGE, columns + 2 * LANES), F32),
            pltpu.VMEM((LANES, LANES), F32),
            pltpu.VMEM((band_rows + EDGE, columns + LANES), F32),
        ],
    )


def solution(mesh):
    return jax.shard_map(
        local,
        mesh=mesh,
        in_specs=(
            P(None, ("aper", "band"), None),
            P(("aper", "band"), None),
            P(("aper", "band"), None),
            P("band", None),
            P(),
            P(),
            P(None, "band", "aper"),
            P(),
        ),
        out_specs=P(None, "band", "aper"),
        check_vma=False,
    )
```

```python
import functools
import math

import jax
import jax.numpy as jnp
from jax import lax
from jax.experimental import pallas as pl
from jax.experimental.pallas import tpu as pltpu
from jax.sharding import PartitionSpec as P

TAPS_K = 2
LANES = 128
EDGE = 8
Z_HI, Z_LO, N_X, N_YC = 2, 8, 4, 8
N_Z = Z_HI * Z_LO
FIRST_Z = 8
smooth_eps = 0.05
BF16, F32 = jnp.bfloat16, jnp.float32
VMEM = pl.BlockSpec(memory_space=pltpu.VMEM)
SMEM = pl.BlockSpec(memory_space=pltpu.SMEM)
ANY = pl.BlockSpec(memory_space=pl.ANY)
HBM = pl.BlockSpec(memory_space=pltpu.HBM)


def device_index(z_hi, z_lo, x, yc):
    return ((z_lo * N_X + x) * Z_HI + z_hi) * N_YC + yc


def z_rings():
    order = [(FIRST_Z + k) % N_Z for k in range(N_Z)]
    return [
        [device_index(z // Z_LO, z % Z_LO, x, yc) for z in order]
        for x in range(N_X)
        for yc in range(N_YC)
    ]


def in_ring(z):
    return (z + N_Z - FIRST_Z) % N_Z


def halves_swapped():
    return [
        (device_index(h, z, x, yc), device_index(1 - h, (z + Z_LO // 2) % Z_LO, x, yc))
        for h in range(Z_HI)
        for z in range(Z_LO)
        for x in range(N_X)
        for yc in range(N_YC)
    ]


def place_of():
    group, band = lax.axis_index("aper"), lax.axis_index("band")
    return band // N_YC, group // N_X, group % N_X, band % N_YC


def two_parts(value, spare_ref):
    first = value.astype(BF16).astype(F32)
    spare_ref[0:4] = first
    spare_ref[4:8] = value - first
    return spare_ref[...].astype(BF16)


def joined(rows):
    rows = rows.astype(F32)
    return rows[0:4] + rows[4:8]


TOP, LOW = EDGE - 1, EDGE + 64


def with_corners(columns, above, below):
    lane = lax.broadcasted_iota(jnp.int32, columns.shape, 1)
    row = lax.broadcasted_iota(jnp.int32, columns.shape, 0)
    above = pltpu.roll(above, TOP, 1)
    below = pltpu.roll(below, (LOW + 1) % LANES, 1)
    for comp in range(2):
        columns = jnp.where((lane == TOP) & (row == comp), above[2 * comp : 2 * comp + 1], columns)
        columns = jnp.where(
            (lane == LOW) & (row == 2 + comp), below[2 * comp + 1 : 2 * comp + 2], columns
        )
    return columns


def cut_windows(wanted, start_hbm, foot_hbm, pulse_hbm, image_hbm, *refs):
    (
        out_hbm,
        start_ref,
        foot_ref,
        pulse_ref,
        edge_ref,
        flat_ref,
        window_ref,
        packed_ref,
        spare_ref,
        sem,
        out_sem,
    ) = refs[-11:]

    @pl.when(place_of()[0] == wanted)
    def _():
        rows = image_hbm.shape[1]
        copies = [
            pltpu.make_async_copy(pulse_hbm, pulse_ref, sem.at[0]),
            pltpu.make_async_copy(start_hbm, start_ref, sem.at[1]),
            pltpu.make_async_copy(foot_hbm, foot_ref, sem.at[2]),
            pltpu.make_async_copy(image_hbm.at[:, pl.ds(0, EDGE), :], edge_ref.at[0], sem.at[3]),
            pltpu.make_async_copy(image_hbm.at[:, pl.ds(rows - EDGE, EDGE), :], edge_ref.at[1], sem.at[4]),
        ]
        for copy in copies:
            copy.start()
        window_ref[...] = jnp.zeros_like(window_ref)
        comps, pulses, bins = pulse_ref.shape
        parts = bins // LANES
        pitch = comps * (parts + 1)
        block = window_ref.shape[0] // (Z_HI * N_YC)
        for copy in copies:
            copy.wait()
        for part in range(parts):
            for comp in range(comps):
                flat_ref[pl.ds(part * comps + comp, pulses, stride=pitch), :] = pulse_ref[
                    comp, :, part * LANES : (part + 1) * LANES
                ].astype(F32)
        lane = lax.broadcasted_iota(jnp.int32, (block // pulses, LANES), 1)
        for pulse in range(pulses):
            for k in range(foot_ref.shape[1]):
                band = foot_ref[pulse, k]
                start = start_ref[pulse, band]
                row = pulse * pitch + comps * (start >> 7)
                shift = start & (LANES - 1)
                here = flat_ref[pl.ds(row, block // pulses), :]
                following = flat_ref[pl.ds(row + comps, block // pulses), :]
                both = jnp.where(lane >= shift, here, following)
                both = pltpu.roll(both, (LANES - shift) & (LANES - 1), 1)
                place = ((band & (N_YC - 1)) * Z_HI + (band >> 3)) * block + pulse
                window_ref[pl.ds(place, block // pulses, stride=pulses), :] = both
        tall = Z_HI * block
        packed_ref[:, tall:, :] = jnp.zeros((N_YC, EDGE, LANES), BF16)
        yc = place_of()[3]
        for side, line, to in ((0, 0, yc + N_YC - 1), (1, EDGE - 1, yc + 1)):
            edge = [edge_ref[side, comp, line : line + 1, :] for comp in range(comps)]
            edge = [e[:, i * LANES : (i + 1) * LANES] for e in edge for i in range(2)]
            packed_ref[to % N_YC, tall:, :] = two_parts(jnp.concatenate(edge, axis=0), spare_ref)
        leaving = []
        for to in range(N_YC):
            packed_ref[to, :tall, :] = window_ref[to * tall : (to + 1) * tall, :].astype(BF16)
            leaving.append(pltpu.make_async_copy(packed_ref.at[to], out_hbm.at[to], out_sem.at[to]))
            leaving[-1].start()
        for copy in leaving:
            copy.wait()


def side_columns(image_hbm, weight_hbm, other_ref, out_ref, weight_ref, pad_ref, block_ref, sem):
    z_hi = place_of()[0]
    rows, columns = image_hbm.shape[1:]
    copies = [
        pltpu.make_async_copy(weight_hbm, weight_ref.at[z_hi], sem.at[0]),
        pltpu.make_async_copy(image_hbm.at[:, :, pl.ds(0, LANES)], block_ref.at[0], sem.at[1]),
        pltpu.make_async_copy(
            image_hbm.at[:, :, pl.ds(columns - LANES, LANES)], block_ref.at[1], sem.at[2]
        ),
    ]
    for copy in copies:
        copy.start()
    weight_ref[1 - z_hi] = other_ref[...]
    pad_ref[...] = jnp.zeros_like(pad_ref)
    out_ref[...] = jnp.zeros_like(out_ref)
    for copy in copies:
        copy.wait()
    for comp in range(2):
        for side, line in ((0, 0), (1, LANES - 1)):
            pad_ref[EDGE : EDGE + rows, :] = block_ref[side, comp]
            out_ref[2 * side + comp : 2 * side + comp + 1, :] = pad_ref[...].T[line : line + 1, :]


def lift_windows(
    window_ref, weight_ref, column_ref, after_ref, out_ref, edge_ref, spare_ref
):
    del after_ref
    z_hi, _, _, yc = place_of()
    sources, height = window_ref.shape[0], window_ref.shape[1] - EDGE
    half = height // Z_HI
    band_rows, window_len = weight_ref.shape[1:]
    parts = window_len // LANES
    rows = half // parts
    tall = sources * rows // 2

    above = joined(window_ref[(yc + N_YC - 1) % N_YC, height:, :])
    below = joined(window_ref[(yc + 1) % N_YC, height:, :])
    foreign = jnp.where(yc == 0, above, below)
    above = jnp.where(yc > 0, above, jnp.zeros_like(above))
    below = jnp.where(yc < N_YC - 1, below, jnp.zeros_like(below))
    edge_ref[0:4] = above
    edge_ref[4:8] = below
    columns = with_corners(column_ref[0:4], above, below)

    dims = (((1,), (1,)), ((), ()))
    for z_half in range(Z_HI):
        extra = jnp.where(z_half == z_hi, columns, foreign)
        lifted = jnp.zeros((sources * rows, band_rows), F32)
        for part in range(parts):
            first = z_half * half + part * rows
            piece = window_ref[:, pl.ds(first, rows), :].reshape(sources * rows, LANES)
            lifted = lifted + lax.dot_general(
                piece,
                weight_ref[z_half, :, part * LANES : (part + 1) * LANES],
                dims,
                preferred_element_type=F32,
            )
        lifted = lifted.reshape(sources, 2, rows // 2, band_rows)
        both = jnp.concatenate([lifted[:, 0], lifted[:, 1]], axis=-1)
        both = both.reshape(tall, 2 * band_rows).astype(BF16)
        extra = two_parts(extra, spare_ref)
        for z in range(Z_LO):
            out_ref[in_ring(z_half * Z_LO + z), :tall, :] = both
            out_ref[in_ring(z_half * Z_LO + z), tall:, :] = extra


def sin_cos(angle):
    turns = jnp.round(angle * (2.0 / math.pi))
    rest = angle - turns * 1.5703125
    rest = rest - turns * 4.837512969970703125e-4
    rest = rest - turns * 7.54978995489188216e-8
    square = rest * rest
    sine = -1.9515295891e-4 * square + 8.3321608736e-3
    sine = (sine * square - 1.6666654611e-1) * square * rest + rest
    cosine = 2.443315711809948e-5 * square - 1.388731625493765e-3
    cosine = (cosine * square + 4.166664568298827e-2) * square * square - 0.5 * square + 1.0
    quarter = turns.astype(jnp.int32) & 3
    swap = (quarter & 1) == 1
    sin_out = jnp.where(swap, cosine, sine)
    cos_out = jnp.where(swap, sine, cosine)
    sin_out = jnp.where(quarter >= 2, -sin_out, sin_out)
    cos_out = jnp.where((quarter == 1) | (quarter == 2), -cos_out, cos_out)
    return sin_out, cos_out


FINE = 16
STEP = 2 * TAPS_K + 1


def make_table(
    after_ref,
    ramp_hbm,
    taps_hbm,
    step_hbm,
    near_ref,
    fine_ref,
    coarse_ref,
    tap_rows_ref,
    ramp_ref,
    taps_ref,
    step_ref,
    rate_ref,
    spare_ref,
    sem,
):
    del after_ref
    copies = [
        pltpu.make_async_copy(ramp_hbm, ramp_ref, sem.at[0]),
        pltpu.make_async_copy(taps_hbm, taps_ref, sem.at[1]),
        pltpu.make_async_copy(step_hbm, step_ref, sem.at[2]),
    ]
    for copy in copies:
        copy.start()
    _, z_lo, x, _ = place_of()
    n_groups = ramp_ref.shape[0]
    half = near_ref.shape[0]
    for copy in copies:
        copy.wait()
    for t in range(2 * TAPS_K + 1):
        tap_rows_ref[t : t + 1, :] = jnp.full((1, LANES), taps_ref[t], F32)
    scale = 1.0 / math.sqrt(n_groups * LANES)
    tap_rows_ref[STEP : STEP + 1, :] = jnp.full((1, LANES), step_ref[0] * scale, F32)
    tap_rows_ref[STEP + 1 : STEP + 2, :] = jnp.full((1, LANES), step_ref[0] * step_ref[1], F32)

    lane = lax.broadcasted_iota(jnp.int32, (1, LANES), 1)
    ends = jnp.zeros((1, LANES), F32)
    for i in range(Z_LO):
        group = i * N_X + x
        rate_ref[i : i + 1, :] = ramp_ref[pl.ds(group, 1), :]
        before = ramp_ref[pl.ds((group + n_groups - 1) % n_groups, 1), :]
        after = ramp_ref[pl.ds((group + 1) % n_groups, 1), :]
        place = 2 * EDGE * i
        move = (place + EDGE) % LANES
        before = pltpu.roll(before, move, 1) if move else before
        after = pltpu.roll(after, move, 1) if move else after
        ends = jnp.where((lane >= place) & (lane < place + EDGE), before, ends)
        ends = jnp.where((lane >= place + EDGE) & (lane < place + 2 * EDGE), after, ends)
    rate_ref[Z_LO : Z_LO + 1, :] = ends

    n_coarse = 2 * half // FINE
    first = z_lo * 2 * half
    fine_step = lax.broadcasted_iota(jnp.int32, (FINE, LANES), 0).astype(F32)
    coarse_step = (
        first + FINE * lax.broadcasted_iota(jnp.int32, (n_coarse, LANES), 0)
    ).astype(F32)
    for i in range(Z_LO + 1):
        span = pl.ds(i * LANES, LANES)
        rate = rate_ref[i : i + 1, :]
        fine_sin, fine_cos = sin_cos(rate * fine_step)
        coarse_sin, coarse_cos = sin_cos(rate * coarse_step)
        fine_ref[0, :, span], fine_ref[1, :, span] = fine_sin, fine_cos
        spare_ref[0], spare_ref[1] = coarse_sin, coarse_cos
        coarse_ref[0, :, span] = coarse_sin[n_coarse // 2 :]
        coarse_ref[1, :, span] = coarse_cos[n_coarse // 2 :]
        for a in range(n_coarse // 2):
            fill(
                near_ref,
                a * FINE,
                i,
                (spare_ref[0, a : a + 1, :], spare_ref[1, a : a + 1, :]),
                (fine_sin, fine_cos),
            )


def fill(table_ref, row, i, coarse, fine):
    depth = table_ref.shape[1] // 2
    (s, c), (fine_sin, fine_cos) = coarse, fine
    table_ref[row : row + FINE, i * LANES : (i + 1) * LANES] = (
        c * fine_cos - s * fine_sin
    ).astype(BF16)
    table_ref[row : row + FINE, depth + i * LANES : depth + (i + 1) * LANES] = (
        s * fine_cos + c * fine_sin
    ).astype(BF16)


def sum_pulses(
    tap_rows_ref,
    near_ref,
    fine_ref,
    coarse_ref,
    lifted_ref,
    column_ref,
    edge_ref,
    out_ref,
    mine_ref,
    edge_out_ref,
    pad_ref,
    blend_ref,
    far_ref,
    total_ref,
    spare_ref,
):
    z_hi, z_lo, x, yc = place_of()
    width = lifted_ref.shape[2]
    half_pulses = LANES // Z_HI
    main = Z_LO * LANES
    depth = main + LANES
    blocks, columns = out_ref.shape[0], out_ref.shape[1] - EDGE

    zero = jnp.zeros((2 * EDGE, width), F32)
    pad_ref[: 2 * EDGE] = zero
    pad_ref[2 * EDGE + LANES :] = zero
    for i in range(Z_LO):
        for h in range(Z_HI):
            pad_ref[pl.ds(2 * EDGE + h * half_pulses, half_pulses), :] = lifted_ref[
                in_ring(h * Z_LO + i), :half_pulses, :
            ].astype(F32)
        blended = jnp.zeros((LANES + 2 * EDGE, width), F32)
        for t in range(2 * TAPS_K + 1):
            blended = blended + tap_rows_ref[t : t + 1, :] * pad_ref[
                pl.ds(EDGE - TAPS_K + t, LANES + 2 * EDGE), :
            ]
        turned = pltpu.roll(blended, width // 2, 1)
        lane_full = lax.broadcasted_iota(jnp.int32, blended.shape, 1)
        turned = jnp.where(lane_full < width // 2, -turned, turned)
        for k, value in enumerate((blended, turned)):
            value = value.astype(BF16)
            blend_ref[pl.ds(k * depth + i * LANES, LANES), :] = value[EDGE : EDGE + LANES]
            outside = jnp.concatenate([value[:EDGE], value[EDGE + LANES :]], axis=0)
            blend_ref[pl.ds(k * depth + main + i * 2 * EDGE, 2 * EDGE), :] = outside

    for i in range(Z_LO + 1):
        span = pl.ds(i * LANES, LANES)
        fine = fine_ref[0, :, span], fine_ref[1, :, span]
        for a in range(far_ref.shape[0] // FINE):
            coarse = coarse_ref[0, a : a + 1, span], coarse_ref[1, a : a + 1, span]
            fill(far_ref, a * FINE, i, coarse, fine)
    for side, table_ref in enumerate((near_ref, far_ref)):
        total = jnp.dot(table_ref[...], blend_ref[...], preferred_element_type=F32)
        for block in range(blocks // 2):
            part = total[block * columns : (block + 1) * columns]
            total_ref[side * (blocks // 2) + block] = part
            out_ref[side * (blocks // 2) + block, :columns, :] = part.astype(BF16)
    mine_ref[...] = total_ref[x]

    def came(half, z):
        return joined(lifted_ref[in_ring(half * Z_LO + z % Z_LO), half_pulses:, :])

    first_band = (z_hi == 1) & (yc == 0)
    last_band = (z_hi == 0) & (yc == N_YC - 1)
    foreign = came(1 - z_hi, z_lo)
    above = jnp.where(first_band, foreign, edge_ref[0:4])
    below = jnp.where(last_band, foreign, edge_ref[4:8])
    edge_out_ref[0:4] = above
    edge_out_ref[4:8] = below
    own = with_corners(column_ref[0:4], above, below)
    left = came(z_hi, z_lo + Z_LO - 1)
    left_fixed = with_corners(left, above, came(1 - z_hi, z_lo + Z_LO - 1))
    left = jnp.where(last_band, left_fixed, left)
    right = came(z_hi, z_lo + 1)
    right_fixed = with_corners(right, came(1 - z_hi, z_lo + 1), below)
    right = jnp.where(first_band, right_fixed, right)
    out_ref[:, columns:, :] = jnp.zeros((blocks, EDGE, LANES), BF16)
    after = two_parts(jnp.where(x < N_X - 1, own, left), spare_ref)
    before = two_parts(jnp.where(x > 0, own, right), spare_ref)
    out_ref[(x + 1) % N_X, columns:, :] = after
    out_ref[(x + N_X - 1) % N_X, columns:, :] = before


def finish(
    rows_ref, sums_ref, mine_ref, edge_ref, image_ref, out_ref, pad_ref, side_ref, flow_ref
):
    _, z_lo, x, _ = place_of()
    group = z_lo * N_X + x
    comps, rows, columns = image_ref.shape
    tall = pad_ref.shape[1]
    total = mine_ref[...]
    for k in range(1, N_X):
        total = total + sums_ref[(x + k) % N_X, :columns, :].astype(F32)
    step, weight = rows_ref[STEP : STEP + 1, :1], rows_ref[STEP + 1 : STEP + 2, :1]
    total = (total * step).T.reshape(image_ref.shape)

    zero = jnp.zeros((2, LANES), F32)
    left = joined(sums_ref[(x + N_X - 1) % N_X, columns:, :])[2:4]
    right = joined(sums_ref[(x + 1) % N_X, columns:, :])[0:2]
    side_ref[...] = jnp.zeros_like(side_ref)
    side_ref[0:2, :] = jnp.where(group > 0, left, zero)
    side_ref[2:4, :] = jnp.where(group < Z_LO * N_X - 1, right, zero)
    sides = side_ref[...].T[:tall]
    lane = lax.broadcasted_iota(jnp.int32, (tall, LANES), 1)
    blank = jnp.zeros((tall, LANES), F32)
    pad_ref[...] = jnp.zeros_like(pad_ref)
    for comp in range(comps):
        pad_ref[comp, EDGE : EDGE + rows, LANES : LANES + columns] = image_ref[comp]
        for half in range(2):
            span = pl.ds((1 + half) * LANES, LANES)
            pad_ref[comp, TOP : TOP + 1, span] = edge_ref[2 * comp + half : 2 * comp + half + 1, :]
            pad_ref[comp, LOW : LOW + 1, span] = edge_ref[4 + 2 * comp + half : 5 + 2 * comp + half, :]
        pad_ref[comp, :, :LANES] = jnp.where(lane == LANES - 1, sides[:, comp : comp + 1], blank)
        pad_ref[comp, :, LANES + columns :] = jnp.where(
            lane == 0, sides[:, 2 + comp : 3 + comp], blank
        )

    high, wide = rows + EDGE, columns + LANES
    row_step, col_step = [], []
    square = jnp.zeros((high, wide), F32) + smooth_eps
    for comp in range(comps):
        here = pad_ref[comp, :high, :]
        following = pltpu.roll(here, here.shape[1] - 1, 1)[:, :wide]
        here = here[:, :wide]
        row_step.append(pad_ref[comp, 1 : high + 1, :wide] - here)
        col_step.append(following - here)
        square = square + row_step[-1] * row_step[-1] + col_step[-1] * col_step[-1]
    inverse = lax.rsqrt(square)
    for comp in range(comps):
        row_flow = row_step[comp] * inverse
        col_flow = col_step[comp] * inverse
        flow_ref[...] = row_flow
        across = col_flow - pltpu.roll(col_flow, 1, 1)
        down = row_flow[EDGE:, LANES:] - flow_ref[EDGE - 1 : high - 1, LANES:]
        variation = -(down + across[EDGE:, LANES:])
        out_ref[comp] = image_ref[comp] - (total[comp] + weight * variation)


def in_hbm(*values):
    return tuple(pltpu.with_memory_space_constraint(value, pltpu.HBM) for value in values)


def call(kernel, out_shape, in_specs, args, scratch=(), cost=None, out_specs=None):
    if out_specs is None:
        out_specs = [VMEM] * len(out_shape) if isinstance(out_shape, tuple) else VMEM
    return pl.pallas_call(
        kernel,
        out_shape=out_shape,
        in_specs=in_specs,
        out_specs=out_specs,
        scratch_shapes=scratch,
        cost_estimate=cost,
        compiler_params=pltpu.CompilerParams(vmem_limit_bytes=16 * 1024 * 1024),
    )(*args)


def local(
    pulse_data,
    window_start,
    footprint,
    range_to_row_weight,
    slow_taps,
    ramp_rate,
    image_now,
    step_and_variation_weight,
):
    band_count = lax.axis_size("band")
    groups = lax.axis_size("aper")
    comps, pulses, bins = pulse_data.shape
    band_rows, window_len = range_to_row_weight.shape
    columns = image_now.shape[2]
    shape = jax.ShapeDtypeStruct

    block = window_len // LANES * comps * pulses
    given = in_hbm(window_start, footprint, pulse_data, image_now)
    windows = ()
    weight = range_to_row_weight
    for wanted in range(Z_HI):
        windows = pl.pallas_call(
            functools.partial(cut_windows, wanted),
            out_shape=pltpu.HBM((N_YC, Z_HI * block + EDGE, LANES), BF16),
            in_specs=[HBM] * (len(given) + len(windows)),
            out_specs=HBM,
            scratch_shapes=[
                pltpu.SMEM(window_start.shape, jnp.int32),
                pltpu.SMEM(footprint.shape, jnp.int32),
                pltpu.VMEM(pulse_data.shape, BF16),
                pltpu.VMEM((2, comps, EDGE, columns), F32),
                pltpu.VMEM((pulses * comps * (bins // LANES + 1), LANES), F32),
                pltpu.VMEM((band_count * block, LANES), F32),
                pltpu.VMEM((N_YC, Z_HI * block + EDGE, LANES), BF16),
                pltpu.VMEM((EDGE, LANES), F32),
                pltpu.SemaphoreType.DMA((5,)),
                pltpu.SemaphoreType.DMA((N_YC,)),
            ],
            input_output_aliases={len(given): 0} if windows else {},
            compiler_params=pltpu.CompilerParams(vmem_limit_bytes=16 * 1024 * 1024),
        )(*given, *windows)
        if wanted == 0:
            weight, windows = lax.optimization_barrier((weight, windows))
            other_weight = lax.ppermute(weight, ("aper", "band"), halves_swapped())
            windows = (windows,)
    half = N_X * columns // 2
    depth = (Z_LO + 1) * LANES
    near, fine, coarse, tap_rows = call(
        make_table,
        (
            shape((half, 2 * depth), BF16),
            shape((2, FINE, depth), F32),
            shape((2, half // FINE, depth), F32),
            shape((EDGE, LANES), F32),
        ),
        [HBM] * 4,
        (
            *in_hbm(
                windows,
                ramp_rate.reshape(groups, LANES),
                slow_taps,
                step_and_variation_weight,
            ),
        ),
        [
            pltpu.VMEM((groups, LANES), F32),
            pltpu.SMEM(slow_taps.shape, F32),
            pltpu.SMEM(step_and_variation_weight.shape, F32),
            pltpu.VMEM((2 * EDGE, LANES), F32),
            pltpu.VMEM((2, 2 * half // FINE, LANES), F32),
            pltpu.SemaphoreType.DMA((3,)),
        ],
        pl.CostEstimate(flops=1 << 24, bytes_accessed=1 << 23, transcendentals=0),
    )
    in_plane = [[h * N_YC + i for i in range(N_YC)] for h in range(Z_HI)]
    windows = lax.all_to_all(windows, "band", 0, 0, axis_index_groups=in_plane, tiled=True)
    side, weights = call(
        side_columns,
        (shape((EDGE, LANES), F32), shape((Z_HI, band_rows, window_len), BF16)),
        [HBM, HBM, VMEM],
        (*in_hbm(image_now, range_to_row_weight), other_weight),
        [
            pltpu.VMEM((LANES, LANES), F32),
            pltpu.VMEM((2, comps, band_rows, LANES), F32),
            pltpu.SemaphoreType.DMA((3,)),
        ],
        pl.CostEstimate(flops=1 << 34, bytes_accessed=1 << 27, transcendentals=0),
    )
    width = comps * band_rows
    lifted, edges = call(
        lift_windows,
        (
            shape((N_Z, N_YC * pulses + EDGE, width), BF16),
            shape((EDGE, LANES), F32),
        ),
        [VMEM] * 3 + [ANY],
        (windows, weights, side, tap_rows),
        [pltpu.VMEM((EDGE, LANES), F32)],
    )
    lifted = lax.all_to_all(lifted, ("aper", "band"), 0, 0, axis_index_groups=z_rings(), tiled=True)
    sums, mine, edges = call(
        sum_pulses,
        (
            shape((N_X, columns + EDGE, width), BF16),
            shape((columns, width), F32),
            shape((EDGE, LANES), F32),
        ),
        [VMEM] * 7,
        (tap_rows, near, fine, coarse, lifted, side, edges),
        [
            pltpu.VMEM((LANES + 4 * EDGE, width), F32),
            pltpu.VMEM((2 * depth, width), BF16),
            pltpu.VMEM((half, 2 * depth), BF16),
            pltpu.VMEM((N_X, columns, width), F32),
            pltpu.VMEM((EDGE, LANES), F32),
        ],
    )
    along_x = [[z * N_X + x for x in range(N_X)] for z in range(Z_LO)]
    sums = lax.all_to_all(sums, "aper", 0, 0, axis_index_groups=along_x, tiled=True)
    return call(
        finish,
        shape(image_now.shape, F32),
        [VMEM] * 5,
        (tap_rows, sums, mine, edges, image_now),
        [
            pltpu.VMEM((comps, band_rows + 2 * EDGE, columns + 2 * LANES), F32),
            pltpu.VMEM((LANES, LANES), F32),
            pltpu.VMEM((band_rows + EDGE, columns + LANES), F32),
        ],
    )


def solution(mesh):
    return jax.shard_map(
        local,
        mesh=mesh,
        in_specs=(
            P(None, ("aper", "band"), None),
            P(("aper", "band"), None),
            P(("aper", "band"), None),
            P("band", None),
            P(),
            P(),
            P(None, "band", "aper"),
            P(),
        ),
        out_specs=P(None, "band", "aper"),
        check_vma=False,
    )
```

```python
import functools
import math

import jax
import jax.numpy as jnp
from jax import lax
from jax.experimental import pallas as pl
from jax.experimental.pallas import tpu as pltpu
from jax.sharding import PartitionSpec as P

TAPS_K = 2
LANES = 128
EDGE = 8
Z_HI, Z_LO, N_X, N_YC = 2, 8, 4, 8
N_Z = Z_HI * Z_LO
FIRST_Z = 8
smooth_eps = 0.05
BF16, F32 = jnp.bfloat16, jnp.float32
VMEM = pl.BlockSpec(memory_space=pltpu.VMEM)
SMEM = pl.BlockSpec(memory_space=pltpu.SMEM)
ANY = pl.BlockSpec(memory_space=pl.ANY)
HBM = pl.BlockSpec(memory_space=pltpu.HBM)


def device_index(z_hi, z_lo, x, yc):
    return ((z_lo * N_X + x) * Z_HI + z_hi) * N_YC + yc


def z_rings():
    order = [(FIRST_Z + k) % N_Z for k in range(N_Z)]
    return [
        [device_index(z // Z_LO, z % Z_LO, x, yc) for z in order]
        for x in range(N_X)
        for yc in range(N_YC)
    ]


def in_ring(z):
    return (z + N_Z - FIRST_Z) % N_Z


def halves_swapped():
    return [
        (device_index(h, z, x, yc), device_index(1 - h, (z + Z_LO // 2) % Z_LO, x, yc))
        for h in range(Z_HI)
        for z in range(Z_LO)
        for x in range(N_X)
        for yc in range(N_YC)
    ]


def place_of():
    group, band = lax.axis_index("aper"), lax.axis_index("band")
    return band // N_YC, group // N_X, group % N_X, band % N_YC


def two_parts(value, spare_ref):
    first = value.astype(BF16).astype(F32)
    spare_ref[0:4] = first
    spare_ref[4:8] = value - first
    return spare_ref[...].astype(BF16)


def joined(rows):
    rows = rows.astype(F32)
    return rows[0:4] + rows[4:8]


TOP, LOW = EDGE - 1, EDGE + 64


def with_corners(columns, above, below):
    lane = lax.broadcasted_iota(jnp.int32, columns.shape, 1)
    row = lax.broadcasted_iota(jnp.int32, columns.shape, 0)
    above = pltpu.roll(above, TOP, 1)
    below = pltpu.roll(below, (LOW + 1) % LANES, 1)
    for comp in range(2):
        columns = jnp.where((lane == TOP) & (row == comp), above[2 * comp : 2 * comp + 1], columns)
        columns = jnp.where(
            (lane == LOW) & (row == 2 + comp), below[2 * comp + 1 : 2 * comp + 2], columns
        )
    return columns


def cut_windows(wanted, start_hbm, foot_hbm, pulse_hbm, image_hbm, *refs):
    (
        out_hbm,
        start_ref,
        foot_ref,
        pulse_ref,
        edge_ref,
        flat_ref,
        window_ref,
        packed_ref,
        spare_ref,
        sem,
        out_sem,
    ) = refs[-11:]

    @pl.when(place_of()[0] == wanted)
    def _():
        rows = image_hbm.shape[1]
        copies = [
            pltpu.make_async_copy(pulse_hbm, pulse_ref, sem.at[0]),
            pltpu.make_async_copy(start_hbm, start_ref, sem.at[1]),
            pltpu.make_async_copy(foot_hbm, foot_ref, sem.at[2]),
            pltpu.make_async_copy(image_hbm.at[:, pl.ds(0, EDGE), :], edge_ref.at[0], sem.at[3]),
            pltpu.make_async_copy(image_hbm.at[:, pl.ds(rows - EDGE, EDGE), :], edge_ref.at[1], sem.at[4]),
        ]
        for copy in copies:
            copy.start()
        window_ref[...] = jnp.zeros_like(window_ref)
        comps, pulses, bins = pulse_ref.shape
        parts = bins // LANES
        pitch = comps * (parts + 1)
        block = (window_ref.shape[0] - EDGE) // (Z_HI * N_YC)
        for copy in copies:
            copy.wait()
        for part in range(parts):
            for comp in range(comps):
                flat_ref[pl.ds(part * comps + comp, pulses, stride=pitch), :] = pulse_ref[
                    comp, :, part * LANES : (part + 1) * LANES
                ].astype(F32)
        lane = lax.broadcasted_iota(jnp.int32, (block // pulses, LANES), 1)
        for pulse in range(pulses):
            for k in range(foot_ref.shape[1]):
                band = foot_ref[pulse, k]
                start = start_ref[pulse, band]
                row = pulse * pitch + comps * (start >> 7)
                shift = start & (LANES - 1)
                here = flat_ref[pl.ds(row, block // pulses), :]
                following = flat_ref[pl.ds(row + comps, block // pulses), :]
                both = jnp.where(lane >= shift, here, following)
                both = pltpu.roll(both, (LANES - shift) & (LANES - 1), 1)
                place = ((band & (N_YC - 1)) * Z_HI + (band >> 3)) * block + pulse
                window_ref[pl.ds(place, block // pulses, stride=pulses), :] = both
        tall = Z_HI * block
        packed_ref[:, tall // EDGE] = jnp.zeros((N_YC, EDGE, LANES), BF16)
        yc = place_of()[3]
        for side, line, to in ((0, 0, yc + N_YC - 1), (1, EDGE - 1, yc + 1)):
            edge = [edge_ref[side, comp, line : line + 1, :] for comp in range(comps)]
            edge = [e[:, i * LANES : (i + 1) * LANES] for e in edge for i in range(2)]
            packed_ref[to % N_YC, tall // EDGE] = two_parts(jnp.concatenate(edge, axis=0), spare_ref)
        leaving = []
        for to in range(N_YC):
            part = window_ref[to * tall : (to + 1) * tall, :].reshape(tall // EDGE, EDGE, LANES)
            packed_ref[to, : tall // EDGE] = part.astype(BF16)
            leaving.append(pltpu.make_async_copy(packed_ref.at[to], out_hbm.at[to], out_sem.at[to]))
            leaving[-1].start()
        for copy in leaving:
            copy.wait()


def side_columns(image_hbm, weight_hbm, other_ref, out_ref, weight_ref, pad_ref, block_ref, sem):
    z_hi = place_of()[0]
    rows, columns = image_hbm.shape[1:]
    copies = [
        pltpu.make_async_copy(weight_hbm, weight_ref.at[z_hi], sem.at[0]),
        pltpu.make_async_copy(image_hbm.at[:, :, pl.ds(0, LANES)], block_ref.at[0], sem.at[1]),
        pltpu.make_async_copy(
            image_hbm.at[:, :, pl.ds(columns - LANES, LANES)], block_ref.at[1], sem.at[2]
        ),
    ]
    for copy in copies:
        copy.start()
    weight_ref[1 - z_hi] = other_ref[...]
    pad_ref[...] = jnp.zeros_like(pad_ref)
    out_ref[...] = jnp.zeros_like(out_ref)
    for copy in copies:
        copy.wait()
    for comp in range(2):
        for side, line in ((0, 0), (1, LANES - 1)):
            pad_ref[EDGE : EDGE + rows, :] = block_ref[side, comp]
            out_ref[2 * side + comp : 2 * side + comp + 1, :] = pad_ref[...].T[line : line + 1, :]


def lift_windows(
    window_ref, weight_ref, column_ref, after_ref, out_ref, edge_ref, spare_ref
):
    del after_ref
    z_hi, _, _, yc = place_of()
    sources, height = window_ref.shape[0], window_ref.shape[1] - 1
    half = height // Z_HI
    band_rows, window_len = weight_ref.shape[1:]
    parts = window_len // LANES
    tiles = half // parts
    rows = tiles * EDGE
    tall = sources * rows // 2

    above = joined(window_ref[(yc + N_YC - 1) % N_YC, height])
    below = joined(window_ref[(yc + 1) % N_YC, height])
    foreign = jnp.where(yc == 0, above, below)
    above = jnp.where(yc > 0, above, jnp.zeros_like(above))
    below = jnp.where(yc < N_YC - 1, below, jnp.zeros_like(below))
    edge_ref[0:4] = above
    edge_ref[4:8] = below
    columns = with_corners(column_ref[0:4], above, below)

    dims = (((1,), (1,)), ((), ()))
    for z_half in range(Z_HI):
        extra = jnp.where(z_half == z_hi, columns, foreign)
        lifted = jnp.zeros((sources * rows, band_rows), F32)
        for part in range(parts):
            first = z_half * half + part * tiles
            piece = window_ref[:, pl.ds(first, tiles)].astype(F32)
            piece = piece.reshape(sources * rows, LANES).astype(BF16)
            lifted = lifted + lax.dot_general(
                piece,
                weight_ref[z_half, :, part * LANES : (part + 1) * LANES],
                dims,
                preferred_element_type=F32,
            )
        lifted = lifted.reshape(sources, 2, rows // 2, band_rows)
        both = jnp.concatenate([lifted[:, 0], lifted[:, 1]], axis=-1)
        both = both.reshape(tall // EDGE, EDGE, 2 * band_rows).astype(BF16)
        extra = two_parts(extra, spare_ref)
        for z in range(Z_LO):
            out_ref[in_ring(z_half * Z_LO + z), : tall // EDGE] = both
            out_ref[in_ring(z_half * Z_LO + z), tall // EDGE] = extra


def sin_cos(angle):
    turns = jnp.round(angle * (2.0 / math.pi))
    rest = angle - turns * 1.5703125
    rest = rest - turns * 4.837512969970703125e-4
    rest = rest - turns * 7.54978995489188216e-8
    square = rest * rest
    sine = -1.9515295891e-4 * square + 8.3321608736e-3
    sine = (sine * square - 1.6666654611e-1) * square * rest + rest
    cosine = 2.443315711809948e-5 * square - 1.388731625493765e-3
    cosine = (cosine * square + 4.166664568298827e-2) * square * square - 0.5 * square + 1.0
    quarter = turns.astype(jnp.int32) & 3
    swap = (quarter & 1) == 1
    sin_out = jnp.where(swap, cosine, sine)
    cos_out = jnp.where(swap, sine, cosine)
    sin_out = jnp.where(quarter >= 2, -sin_out, sin_out)
    cos_out = jnp.where((quarter == 1) | (quarter == 2), -cos_out, cos_out)
    return sin_out, cos_out


FINE = 16
STEP = 2 * TAPS_K + 1


def make_table(
    after_ref,
    ramp_hbm,
    taps_hbm,
    step_hbm,
    near_ref,
    fine_ref,
    coarse_ref,
    tap_rows_ref,
    ramp_ref,
    taps_ref,
    step_ref,
    rate_ref,
    spare_ref,
    sem,
):
    del after_ref
    copies = [
        pltpu.make_async_copy(ramp_hbm, ramp_ref, sem.at[0]),
        pltpu.make_async_copy(taps_hbm, taps_ref, sem.at[1]),
        pltpu.make_async_copy(step_hbm, step_ref, sem.at[2]),
    ]
    for copy in copies:
        copy.start()
    _, z_lo, x, _ = place_of()
    n_groups = ramp_ref.shape[0]
    half = near_ref.shape[0]
    for copy in copies:
        copy.wait()
    for t in range(2 * TAPS_K + 1):
        tap_rows_ref[t : t + 1, :] = jnp.full((1, LANES), taps_ref[t], F32)
    scale = 1.0 / math.sqrt(n_groups * LANES)
    tap_rows_ref[STEP : STEP + 1, :] = jnp.full((1, LANES), step_ref[0] * scale, F32)
    tap_rows_ref[STEP + 1 : STEP + 2, :] = jnp.full((1, LANES), step_ref[0] * step_ref[1], F32)

    lane = lax.broadcasted_iota(jnp.int32, (1, LANES), 1)
    ends = jnp.zeros((1, LANES), F32)
    for i in range(Z_LO):
        group = i * N_X + x
        rate_ref[i : i + 1, :] = ramp_ref[pl.ds(group, 1), :]
        before = ramp_ref[pl.ds((group + n_groups - 1) % n_groups, 1), :]
        after = ramp_ref[pl.ds((group + 1) % n_groups, 1), :]
        place = 2 * EDGE * i
        move = (place + EDGE) % LANES
        before = pltpu.roll(before, move, 1) if move else before
        after = pltpu.roll(after, move, 1) if move else after
        ends = jnp.where((lane >= place) & (lane < place + EDGE), before, ends)
        ends = jnp.where((lane >= place + EDGE) & (lane < place + 2 * EDGE), after, ends)
    rate_ref[Z_LO : Z_LO + 1, :] = ends

    n_coarse = 2 * half // FINE
    first = z_lo * 2 * half
    fine_step = lax.broadcasted_iota(jnp.int32, (FINE, LANES), 0).astype(F32)
    coarse_step = (
        first + FINE * lax.broadcasted_iota(jnp.int32, (n_coarse, LANES), 0)
    ).astype(F32)
    for i in range(Z_LO + 1):
        span = pl.ds(i * LANES, LANES)
        rate = rate_ref[i : i + 1, :]
        fine_sin, fine_cos = sin_cos(rate * fine_step)
        coarse_sin, coarse_cos = sin_cos(rate * coarse_step)
        fine_ref[0, :, span], fine_ref[1, :, span] = fine_sin, fine_cos
        spare_ref[0], spare_ref[1] = coarse_sin, coarse_cos
        coarse_ref[0, :, span] = coarse_sin[n_coarse // 2 :]
        coarse_ref[1, :, span] = coarse_cos[n_coarse // 2 :]
        for a in range(n_coarse // 2):
            fill(
                near_ref,
                a * FINE,
                i,
                (spare_ref[0, a : a + 1, :], spare_ref[1, a : a + 1, :]),
                (fine_sin, fine_cos),
            )


def fill(table_ref, row, i, coarse, fine):
    depth = table_ref.shape[1] // 2
    (s, c), (fine_sin, fine_cos) = coarse, fine
    table_ref[row : row + FINE, i * LANES : (i + 1) * LANES] = (
        c * fine_cos - s * fine_sin
    ).astype(BF16)
    table_ref[row : row + FINE, depth + i * LANES : depth + (i + 1) * LANES] = (
        s * fine_cos + c * fine_sin
    ).astype(BF16)


def sum_pulses(
    tap_rows_ref,
    near_ref,
    fine_ref,
    coarse_ref,
    lifted_ref,
    column_ref,
    edge_ref,
    out_ref,
    mine_ref,
    edge_out_ref,
    pad_ref,
    blend_ref,
    far_ref,
    total_ref,
    spare_ref,
):
    z_hi, z_lo, x, yc = place_of()
    width = lifted_ref.shape[3]
    half_pulses = LANES // Z_HI
    main = Z_LO * LANES
    depth = main + LANES
    blocks, tiles = out_ref.shape[0], out_ref.shape[1] - 1
    columns = tiles * EDGE

    zero = jnp.zeros((2 * EDGE, width), F32)
    pad_ref[: 2 * EDGE] = zero
    pad_ref[2 * EDGE + LANES :] = zero
    for i in range(Z_LO):
        for h in range(Z_HI):
            part = lifted_ref[in_ring(h * Z_LO + i), : half_pulses // EDGE].astype(F32)
            pad_ref[pl.ds(2 * EDGE + h * half_pulses, half_pulses), :] = part.reshape(
                half_pulses, width
            )
        blended = jnp.zeros((LANES + 2 * EDGE, width), F32)
        for t in range(2 * TAPS_K + 1):
            blended = blended + tap_rows_ref[t : t + 1, :] * pad_ref[
                pl.ds(EDGE - TAPS_K + t, LANES + 2 * EDGE), :
            ]
        turned = pltpu.roll(blended, width // 2, 1)
        lane_full = lax.broadcasted_iota(jnp.int32, blended.shape, 1)
        turned = jnp.where(lane_full < width // 2, -turned, turned)
        for k, value in enumerate((blended, turned)):
            value = value.astype(BF16)
            blend_ref[pl.ds(k * depth + i * LANES, LANES), :] = value[EDGE : EDGE + LANES]
            outside = jnp.concatenate([value[:EDGE], value[EDGE + LANES :]], axis=0)
            blend_ref[pl.ds(k * depth + main + i * 2 * EDGE, 2 * EDGE), :] = outside

    for i in range(Z_LO + 1):
        span = pl.ds(i * LANES, LANES)
        fine = fine_ref[0, :, span], fine_ref[1, :, span]
        for a in range(far_ref.shape[0] // FINE):
            coarse = coarse_ref[0, a : a + 1, span], coarse_ref[1, a : a + 1, span]
            fill(far_ref, a * FINE, i, coarse, fine)
    for side, table_ref in enumerate((near_ref, far_ref)):
        total = jnp.dot(table_ref[...], blend_ref[...], preferred_element_type=F32)
        for block in range(blocks // 2):
            part = total[block * columns : (block + 1) * columns]
            total_ref[side * (blocks // 2) + block] = part
            out_ref[side * (blocks // 2) + block, :tiles] = part.reshape(tiles, EDGE, width).astype(
                BF16
            )
    mine_ref[...] = total_ref[x]

    def came(half, z):
        return joined(lifted_ref[in_ring(half * Z_LO + z % Z_LO), half_pulses // EDGE])

    first_band = (z_hi == 1) & (yc == 0)
    last_band = (z_hi == 0) & (yc == N_YC - 1)
    foreign = came(1 - z_hi, z_lo)
    above = jnp.where(first_band, foreign, edge_ref[0:4])
    below = jnp.where(last_band, foreign, edge_ref[4:8])
    edge_out_ref[0:4] = above
    edge_out_ref[4:8] = below
    own = with_corners(column_ref[0:4], above, below)
    left = came(z_hi, z_lo + Z_LO - 1)
    left_fixed = with_corners(left, above, came(1 - z_hi, z_lo + Z_LO - 1))
    left = jnp.where(last_band, left_fixed, left)
    right = came(z_hi, z_lo + 1)
    right_fixed = with_corners(right, came(1 - z_hi, z_lo + 1), below)
    right = jnp.where(first_band, right_fixed, right)
    out_ref[:, tiles] = jnp.zeros((blocks, EDGE, LANES), BF16)
    after = two_parts(jnp.where(x < N_X - 1, own, left), spare_ref)
    before = two_parts(jnp.where(x > 0, own, right), spare_ref)
    out_ref[(x + 1) % N_X, tiles] = after
    out_ref[(x + N_X - 1) % N_X, tiles] = before


def finish(
    rows_ref, sums_ref, mine_ref, edge_ref, image_ref, out_ref, pad_ref, side_ref, flow_ref
):
    _, z_lo, x, _ = place_of()
    group = z_lo * N_X + x
    comps, rows, columns = image_ref.shape
    tall = pad_ref.shape[1]
    total = mine_ref[...]
    for k in range(1, N_X):
        part = sums_ref[(x + k) % N_X, : columns // EDGE].astype(F32)
        total = total + part.reshape(total.shape)
    step, weight = rows_ref[STEP : STEP + 1, :1], rows_ref[STEP + 1 : STEP + 2, :1]
    total = (total * step).T.reshape(image_ref.shape)

    zero = jnp.zeros((2, LANES), F32)
    left = joined(sums_ref[(x + N_X - 1) % N_X, columns // EDGE])[2:4]
    right = joined(sums_ref[(x + 1) % N_X, columns // EDGE])[0:2]
    side_ref[...] = jnp.zeros_like(side_ref)
    side_ref[0:2, :] = jnp.where(group > 0, left, zero)
    side_ref[2:4, :] = jnp.where(group < Z_LO * N_X - 1, right, zero)
    sides = side_ref[...].T[:tall]
    lane = lax.broadcasted_iota(jnp.int32, (tall, LANES), 1)
    blank = jnp.zeros((tall, LANES), F32)
    pad_ref[...] = jnp.zeros_like(pad_ref)
    for comp in range(comps):
        pad_ref[comp, EDGE : EDGE + rows, LANES : LANES + columns] = image_ref[comp]
        for half in range(2):
            span = pl.ds((1 + half) * LANES, LANES)
            pad_ref[comp, TOP : TOP + 1, span] = edge_ref[2 * comp + half : 2 * comp + half + 1, :]
            pad_ref[comp, LOW : LOW + 1, span] = edge_ref[4 + 2 * comp + half : 5 + 2 * comp + half, :]
        pad_ref[comp, :, :LANES] = jnp.where(lane == LANES - 1, sides[:, comp : comp + 1], blank)
        pad_ref[comp, :, LANES + columns :] = jnp.where(
            lane == 0, sides[:, 2 + comp : 3 + comp], blank
        )

    high, wide = rows + EDGE, columns + LANES
    row_step, col_step = [], []
    square = jnp.zeros((high, wide), F32) + smooth_eps
    for comp in range(comps):
        here = pad_ref[comp, :high, :]
        following = pltpu.roll(here, here.shape[1] - 1, 1)[:, :wide]
        here = here[:, :wide]
        row_step.append(pad_ref[comp, 1 : high + 1, :wide] - here)
        col_step.append(following - here)
        square = square + row_step[-1] * row_step[-1] + col_step[-1] * col_step[-1]
    inverse = lax.rsqrt(square)
    for comp in range(comps):
        row_flow = row_step[comp] * inverse
        col_flow = col_step[comp] * inverse
        flow_ref[...] = row_flow
        across = col_flow - pltpu.roll(col_flow, 1, 1)
        down = row_flow[EDGE:, LANES:] - flow_ref[EDGE - 1 : high - 1, LANES:]
        variation = -(down + across[EDGE:, LANES:])
        out_ref[comp] = image_ref[comp] - (total[comp] + weight * variation)


def in_hbm(*values):
    return tuple(pltpu.with_memory_space_constraint(value, pltpu.HBM) for value in values)


def call(kernel, out_shape, in_specs, args, scratch=(), cost=None, out_specs=None):
    if out_specs is None:
        out_specs = [VMEM] * len(out_shape) if isinstance(out_shape, tuple) else VMEM
    return pl.pallas_call(
        kernel,
        out_shape=out_shape,
        in_specs=in_specs,
        out_specs=out_specs,
        scratch_shapes=scratch,
        cost_estimate=cost,
        compiler_params=pltpu.CompilerParams(vmem_limit_bytes=16 * 1024 * 1024),
    )(*args)


def local(
    pulse_data,
    window_start,
    footprint,
    range_to_row_weight,
    slow_taps,
    ramp_rate,
    image_now,
    step_and_variation_weight,
):
    band_count = lax.axis_size("band")
    groups = lax.axis_size("aper")
    comps, pulses, bins = pulse_data.shape
    band_rows, window_len = range_to_row_weight.shape
    columns = image_now.shape[2]
    shape = jax.ShapeDtypeStruct

    block = window_len // LANES * comps * pulses
    given = in_hbm(window_start, footprint, pulse_data, image_now)
    windows = ()
    weight = range_to_row_weight
    for wanted in range(Z_HI):
        windows = pl.pallas_call(
            functools.partial(cut_windows, wanted),
            out_shape=pltpu.HBM((N_YC, Z_HI * block // EDGE + 1, EDGE, LANES), BF16),
            in_specs=[HBM] * (len(given) + len(windows)),
            out_specs=HBM,
            scratch_shapes=[
                pltpu.SMEM(window_start.shape, jnp.int32),
                pltpu.SMEM(footprint.shape, jnp.int32),
                pltpu.VMEM(pulse_data.shape, BF16),
                pltpu.VMEM((2, comps, EDGE, columns), F32),
                pltpu.VMEM(((pulses + 1) * comps * (bins // LANES + 1), LANES), F32),
                pltpu.VMEM((band_count * block + EDGE, LANES), F32),
                pltpu.VMEM((N_YC, Z_HI * block // EDGE + 1, EDGE, LANES), BF16),
                pltpu.VMEM((EDGE, LANES), F32),
                pltpu.SemaphoreType.DMA((5,)),
                pltpu.SemaphoreType.DMA((N_YC,)),
            ],
            input_output_aliases={len(given): 0} if windows else {},
            compiler_params=pltpu.CompilerParams(vmem_limit_bytes=16 * 1024 * 1024),
        )(*given, *windows)
        if wanted == 0:
            weight, windows = lax.optimization_barrier((weight, windows))
            other_weight = lax.ppermute(weight, ("aper", "band"), halves_swapped())
            windows = (windows,)
    half = N_X * columns // 2
    depth = (Z_LO + 1) * LANES
    near, fine, coarse, tap_rows = call(
        make_table,
        (
            shape((half, 2 * depth), BF16),
            shape((2, FINE, depth), F32),
            shape((2, half // FINE, depth), F32),
            shape((EDGE, LANES), F32),
        ),
        [HBM] * 4,
        (
            *in_hbm(
                windows,
                ramp_rate.reshape(groups, LANES),
                slow_taps,
                step_and_variation_weight,
            ),
        ),
        [
            pltpu.VMEM((groups, LANES), F32),
            pltpu.SMEM(slow_taps.shape, F32),
            pltpu.SMEM(step_and_variation_weight.shape, F32),
            pltpu.VMEM((2 * EDGE, LANES), F32),
            pltpu.VMEM((2, 2 * half // FINE, LANES), F32),
            pltpu.SemaphoreType.DMA((3,)),
        ],
        pl.CostEstimate(flops=1 << 24, bytes_accessed=1 << 23, transcendentals=0),
    )
    in_plane = [[h * N_YC + i for i in range(N_YC)] for h in range(Z_HI)]
    windows = lax.all_to_all(windows, "band", 0, 0, axis_index_groups=in_plane, tiled=True)
    side, weights = call(
        side_columns,
        (shape((EDGE, LANES), F32), shape((Z_HI, band_rows, window_len), BF16)),
        [HBM, HBM, VMEM],
        (*in_hbm(image_now, range_to_row_weight), other_weight),
        [
            pltpu.VMEM((LANES, LANES), F32),
            pltpu.VMEM((2, comps, band_rows, LANES), F32),
            pltpu.SemaphoreType.DMA((3,)),
        ],
        pl.CostEstimate(flops=1 << 34, bytes_accessed=1 << 27, transcendentals=0),
    )
    width = comps * band_rows
    lifted, edges = call(
        lift_windows,
        (
            shape((N_Z, N_YC * pulses // EDGE + 1, EDGE, width), BF16),
            shape((EDGE, LANES), F32),
        ),
        [VMEM] * 3 + [ANY],
        (windows, weights, side, tap_rows),
        [pltpu.VMEM((EDGE, LANES), F32)],
    )
    lifted = lax.all_to_all(lifted, ("aper", "band"), 0, 0, axis_index_groups=z_rings(), tiled=True)
    sums, mine, edges = call(
        sum_pulses,
        (
            shape((N_X, columns // EDGE + 1, EDGE, width), BF16),
            shape((columns, width), F32),
            shape((EDGE, LANES), F32),
        ),
        [VMEM] * 7,
        (tap_rows, near, fine, coarse, lifted, side, edges),
        [
            pltpu.VMEM((LANES + 4 * EDGE, width), F32),
            pltpu.VMEM((2 * depth, width), BF16),
            pltpu.VMEM((half, 2 * depth), BF16),
            pltpu.VMEM((N_X, columns, width), F32),
            pltpu.VMEM((EDGE, LANES), F32),
        ],
    )
    along_x = [[z * N_X + x for x in range(N_X)] for z in range(Z_LO)]
    sums = lax.all_to_all(sums, "aper", 0, 0, axis_index_groups=along_x, tiled=True)
    return call(
        finish,
        shape(image_now.shape, F32),
        [VMEM] * 5,
        (tap_rows, sums, mine, edges, image_now),
        [
            pltpu.VMEM((comps, band_rows + 2 * EDGE, columns + 2 * LANES), F32),
            pltpu.VMEM((LANES, LANES), F32),
            pltpu.VMEM((band_rows + EDGE, columns + LANES), F32),
        ],
    )


def solution(mesh):
    return jax.shard_map(
        local,
        mesh=mesh,
        in_specs=(
            P(None, ("aper", "band"), None),
            P(("aper", "band"), None),
            P(("aper", "band"), None),
            P("band", None),
            P(),
            P(),
            P(None, "band", "aper"),
            P(),
        ),
        out_specs=P(None, "band", "aper"),
        check_vma=False,
    )
```

```python
import functools
import math

import jax
import jax.numpy as jnp
from jax import lax
from jax.experimental import pallas as pl
from jax.experimental.pallas import tpu as pltpu
from jax.sharding import PartitionSpec as P

TAPS_K = 2
LANES = 128
EDGE = 8
Z_HI, Z_LO, N_X, N_YC = 2, 8, 4, 8
N_Z = Z_HI * Z_LO
FIRST_Z = 8
FIRST_YC = 4
FIRST_X = 2
smooth_eps = 0.05
BF16, F32 = jnp.bfloat16, jnp.float32
VMEM = pl.BlockSpec(memory_space=pltpu.VMEM)
SMEM = pl.BlockSpec(memory_space=pltpu.SMEM)
ANY = pl.BlockSpec(memory_space=pl.ANY)
HBM = pl.BlockSpec(memory_space=pltpu.HBM)


def device_index(z_hi, z_lo, x, yc):
    return ((z_lo * N_X + x) * Z_HI + z_hi) * N_YC + yc


def z_rings():
    order = [(FIRST_Z + k) % N_Z for k in range(N_Z)]
    return [
        [device_index(z // Z_LO, z % Z_LO, x, yc) for z in order]
        for x in range(N_X)
        for yc in range(N_YC)
    ]


def in_plane(yc):
    return (yc + N_YC - FIRST_YC) % N_YC


def in_row(x):
    return (x + N_X - FIRST_X) % N_X


def in_ring(z):
    return (z + N_Z - FIRST_Z) % N_Z


def halves_swapped():
    return [
        (device_index(h, z, x, yc), device_index(1 - h, (z + Z_LO // 2) % Z_LO, x, yc))
        for h in range(Z_HI)
        for z in range(Z_LO)
        for x in range(N_X)
        for yc in range(N_YC)
    ]


def place_of():
    group, band = lax.axis_index("aper"), lax.axis_index("band")
    return band // N_YC, group // N_X, group % N_X, band % N_YC


def two_parts(value, spare_ref):
    first = value.astype(BF16).astype(F32)
    spare_ref[0:4] = first
    spare_ref[4:8] = value - first
    return spare_ref[...].astype(BF16)


def joined(rows):
    rows = rows.astype(F32)
    return rows[0:4] + rows[4:8]


TOP, LOW = EDGE - 1, EDGE + 64


def with_corners(columns, above, below):
    lane = lax.broadcasted_iota(jnp.int32, columns.shape, 1)
    row = lax.broadcasted_iota(jnp.int32, columns.shape, 0)
    above = pltpu.roll(above, TOP, 1)
    below = pltpu.roll(below, (LOW + 1) % LANES, 1)
    for comp in range(2):
        columns = jnp.where((lane == TOP) & (row == comp), above[2 * comp : 2 * comp + 1], columns)
        columns = jnp.where(
            (lane == LOW) & (row == 2 + comp), below[2 * comp + 1 : 2 * comp + 2], columns
        )
    return columns


def cut_windows(wanted, start_hbm, foot_hbm, pulse_hbm, image_hbm, *refs):
    (
        out_hbm,
        start_ref,
        foot_ref,
        pulse_ref,
        edge_ref,
        flat_ref,
        window_ref,
        packed_ref,
        spare_ref,
        sem,
        out_sem,
    ) = refs[-11:]

    @pl.when(place_of()[0] == wanted)
    def _():
        rows = image_hbm.shape[1]
        copies = [
            pltpu.make_async_copy(pulse_hbm, pulse_ref, sem.at[0]),
            pltpu.make_async_copy(start_hbm, start_ref, sem.at[1]),
            pltpu.make_async_copy(foot_hbm, foot_ref, sem.at[2]),
            pltpu.make_async_copy(image_hbm.at[:, pl.ds(0, EDGE), :], edge_ref.at[0], sem.at[3]),
            pltpu.make_async_copy(image_hbm.at[:, pl.ds(rows - EDGE, EDGE), :], edge_ref.at[1], sem.at[4]),
        ]
        for copy in copies:
            copy.start()
        window_ref[...] = jnp.zeros_like(window_ref)
        comps, pulses, bins = pulse_ref.shape
        parts = bins // LANES
        pitch = comps * (parts + 1)
        block = (window_ref.shape[0] - EDGE) // (Z_HI * N_YC)
        for copy in copies:
            copy.wait()
        for part in range(parts):
            for comp in range(comps):
                flat_ref[pl.ds(part * comps + comp, pulses, stride=pitch), :] = pulse_ref[
                    comp, :, part * LANES : (part + 1) * LANES
                ].astype(F32)
        lane = lax.broadcasted_iota(jnp.int32, (block // pulses, LANES), 1)
        for pulse in range(pulses):
            for k in range(foot_ref.shape[1]):
                band = foot_ref[pulse, k]
                start = start_ref[pulse, band]
                row = pulse * pitch + comps * (start >> 7)
                shift = start & (LANES - 1)
                here = flat_ref[pl.ds(row, block // pulses), :]
                following = flat_ref[pl.ds(row + comps, block // pulses), :]
                both = jnp.where(lane >= shift, here, following)
                both = pltpu.roll(both, (LANES - shift) & (LANES - 1), 1)
                place = (((band + N_YC - FIRST_YC) & (N_YC - 1)) * Z_HI + (band >> 3)) * block + pulse
                window_ref[pl.ds(place, block // pulses, stride=pulses), :] = both
        tall = Z_HI * block
        packed_ref[:, tall // EDGE] = jnp.zeros((N_YC, EDGE, LANES), BF16)
        yc = place_of()[3]
        for side, line, to in ((0, 0, yc + N_YC - 1), (1, EDGE - 1, yc + 1)):
            edge = [edge_ref[side, comp, line : line + 1, :] for comp in range(comps)]
            edge = [e[:, i * LANES : (i + 1) * LANES] for e in edge for i in range(2)]
            packed_ref[in_plane(to), tall // EDGE] = two_parts(jnp.concatenate(edge, axis=0), spare_ref)
        leaving = []
        for to in range(N_YC):
            part = window_ref[to * tall : (to + 1) * tall, :].reshape(tall // EDGE, EDGE, LANES)
            packed_ref[to, : tall // EDGE] = part.astype(BF16)
            leaving.append(pltpu.make_async_copy(packed_ref.at[to], out_hbm.at[to], out_sem.at[to]))
            leaving[-1].start()
        for copy in leaving:
            copy.wait()


def side_columns(image_hbm, weight_hbm, other_ref, out_ref, weight_ref, pad_ref, block_ref, sem):
    z_hi = place_of()[0]
    rows, columns = image_hbm.shape[1:]
    copies = [
        pltpu.make_async_copy(weight_hbm, weight_ref.at[z_hi], sem.at[0]),
        pltpu.make_async_copy(image_hbm.at[:, :, pl.ds(0, LANES)], block_ref.at[0], sem.at[1]),
        pltpu.make_async_copy(
            image_hbm.at[:, :, pl.ds(columns - LANES, LANES)], block_ref.at[1], sem.at[2]
        ),
    ]
    for copy in copies:
        copy.start()
    weight_ref[1 - z_hi] = other_ref[...]
    pad_ref[...] = jnp.zeros_like(pad_ref)
    out_ref[...] = jnp.zeros_like(out_ref)
    for copy in copies:
        copy.wait()
    for comp in range(2):
        for side, line in ((0, 0), (1, LANES - 1)):
            pad_ref[EDGE : EDGE + rows, :] = block_ref[side, comp]
            out_ref[2 * side + comp : 2 * side + comp + 1, :] = pad_ref[...].T[line : line + 1, :]


def lift_windows(
    window_ref, weight_ref, column_ref, after_ref, out_ref, edge_ref, spare_ref
):
    del after_ref
    z_hi, _, _, yc = place_of()
    sources, height = window_ref.shape[0], window_ref.shape[1] - 1
    half = height // Z_HI
    band_rows, window_len = weight_ref.shape[1:]
    parts = window_len // LANES
    tiles = half // parts
    rows = tiles * EDGE
    tall = sources * rows // 2

    above = joined(window_ref[in_plane(yc + N_YC - 1), height])
    below = joined(window_ref[in_plane(yc + 1), height])
    foreign = jnp.where(yc == 0, above, below)
    above = jnp.where(yc > 0, above, jnp.zeros_like(above))
    below = jnp.where(yc < N_YC - 1, below, jnp.zeros_like(below))
    edge_ref[0:4] = above
    edge_ref[4:8] = below
    columns = with_corners(column_ref[0:4], above, below)

    dims = (((1,), (1,)), ((), ()))
    for z_half in range(Z_HI):
        extra = jnp.where(z_half == z_hi, columns, foreign)
        lifted = jnp.zeros((sources * rows, band_rows), F32)
        for part in range(parts):
            first = z_half * half + part * tiles
            piece = window_ref[:, pl.ds(first, tiles)].astype(F32)
            piece = piece.reshape(sources * rows, LANES).astype(BF16)
            lifted = lifted + lax.dot_general(
                piece,
                weight_ref[z_half, :, part * LANES : (part + 1) * LANES],
                dims,
                preferred_element_type=F32,
            )
        lifted = lifted.reshape(sources, 2, rows // 2, band_rows)
        both = jnp.concatenate([lifted[:, 0], lifted[:, 1]], axis=-1)
        both = both.reshape(tall // EDGE, EDGE, 2 * band_rows).astype(BF16)
        extra = two_parts(extra, spare_ref)
        for z in range(Z_LO):
            for source in range(sources):
                out_ref[in_ring(z_half * Z_LO + z), source] = both[in_plane(source)]
            out_ref[in_ring(z_half * Z_LO + z), tall // EDGE] = extra


def sin_cos(angle):
    turns = jnp.round(angle * (2.0 / math.pi))
    rest = angle - turns * 1.5703125
    rest = rest - turns * 4.837512969970703125e-4
    rest = rest - turns * 7.54978995489188216e-8
    square = rest * rest
    sine = -1.9515295891e-4 * square + 8.3321608736e-3
    sine = (sine * square - 1.6666654611e-1) * square * rest + rest
    cosine = 2.443315711809948e-5 * square - 1.388731625493765e-3
    cosine = (cosine * square + 4.166664568298827e-2) * square * square - 0.5 * square + 1.0
    quarter = turns.astype(jnp.int32) & 3
    swap = (quarter & 1) == 1
    sin_out = jnp.where(swap, cosine, sine)
    cos_out = jnp.where(swap, sine, cosine)
    sin_out = jnp.where(quarter >= 2, -sin_out, sin_out)
    cos_out = jnp.where((quarter == 1) | (quarter == 2), -cos_out, cos_out)
    return sin_out, cos_out


FINE = 16
STEP = 2 * TAPS_K + 1


def make_table(
    after_ref,
    ramp_hbm,
    taps_hbm,
    step_hbm,
    near_ref,
    fine_ref,
    coarse_ref,
    tap_rows_ref,
    ramp_ref,
    taps_ref,
    step_ref,
    rate_ref,
    spare_ref,
    sem,
):
    del after_ref
    copies = [
        pltpu.make_async_copy(ramp_hbm, ramp_ref, sem.at[0]),
        pltpu.make_async_copy(taps_hbm, taps_ref, sem.at[1]),
        pltpu.make_async_copy(step_hbm, step_ref, sem.at[2]),
    ]
    for copy in copies:
        copy.start()
    _, z_lo, x, _ = place_of()
    n_groups = ramp_ref.shape[0]
    half = near_ref.shape[0]
    for copy in copies:
        copy.wait()
    for t in range(2 * TAPS_K + 1):
        tap_rows_ref[t : t + 1, :] = jnp.full((1, LANES), taps_ref[t], F32)
    scale = 1.0 / math.sqrt(n_groups * LANES)
    tap_rows_ref[STEP : STEP + 1, :] = jnp.full((1, LANES), step_ref[0] * scale, F32)
    tap_rows_ref[STEP + 1 : STEP + 2, :] = jnp.full((1, LANES), step_ref[0] * step_ref[1], F32)

    lane = lax.broadcasted_iota(jnp.int32, (1, LANES), 1)
    ends = jnp.zeros((1, LANES), F32)
    for i in range(Z_LO):
        group = i * N_X + x
        rate_ref[i : i + 1, :] = ramp_ref[pl.ds(group, 1), :]
        before = ramp_ref[pl.ds((group + n_groups - 1) % n_groups, 1), :]
        after = ramp_ref[pl.ds((group + 1) % n_groups, 1), :]
        place = 2 * EDGE * i
        move = (place + EDGE) % LANES
        before = pltpu.roll(before, move, 1) if move else before
        after = pltpu.roll(after, move, 1) if move else after
        ends = jnp.where((lane >= place) & (lane < place + EDGE), before, ends)
        ends = jnp.where((lane >= place + EDGE) & (lane < place + 2 * EDGE), after, ends)
    rate_ref[Z_LO : Z_LO + 1, :] = ends

    n_coarse = 2 * half // FINE
    first = z_lo * 2 * half
    fine_step = lax.broadcasted_iota(jnp.int32, (FINE, LANES), 0).astype(F32)
    coarse_step = (
        first + FINE * lax.broadcasted_iota(jnp.int32, (n_coarse, LANES), 0)
    ).astype(F32)
    for i in range(Z_LO + 1):
        span = pl.ds(i * LANES, LANES)
        rate = rate_ref[i : i + 1, :]
        fine_sin, fine_cos = sin_cos(rate * fine_step)
        coarse_sin, coarse_cos = sin_cos(rate * coarse_step)
        fine_ref[0, :, span], fine_ref[1, :, span] = fine_sin, fine_cos
        spare_ref[0], spare_ref[1] = coarse_sin, coarse_cos
        coarse_ref[0, :, span] = coarse_sin[n_coarse // 2 :]
        coarse_ref[1, :, span] = coarse_cos[n_coarse // 2 :]
        for a in range(n_coarse // 2):
            fill(
                near_ref,
                a * FINE,
                i,
                (spare_ref[0, a : a + 1, :], spare_ref[1, a : a + 1, :]),
                (fine_sin, fine_cos),
            )


def fill(table_ref, row, i, coarse, fine):
    depth = table_ref.shape[1] // 2
    (s, c), (fine_sin, fine_cos) = coarse, fine
    table_ref[row : row + FINE, i * LANES : (i + 1) * LANES] = (
        c * fine_cos - s * fine_sin
    ).astype(BF16)
    table_ref[row : row + FINE, depth + i * LANES : depth + (i + 1) * LANES] = (
        s * fine_cos + c * fine_sin
    ).astype(BF16)


def sum_pulses(
    tap_rows_ref,
    near_ref,
    fine_ref,
    coarse_ref,
    lifted_ref,
    column_ref,
    edge_ref,
    out_ref,
    mine_ref,
    edge_out_ref,
    pad_ref,
    blend_ref,
    far_ref,
    total_ref,
    spare_ref,
):
    z_hi, z_lo, x, yc = place_of()
    width = lifted_ref.shape[3]
    half_pulses = LANES // Z_HI
    main = Z_LO * LANES
    depth = main + LANES
    blocks, tiles = out_ref.shape[0], out_ref.shape[1] - 1
    columns = tiles * EDGE

    zero = jnp.zeros((2 * EDGE, width), F32)
    pad_ref[: 2 * EDGE] = zero
    pad_ref[2 * EDGE + LANES :] = zero
    for i in range(Z_LO):
        for h in range(Z_HI):
            part = lifted_ref[in_ring(h * Z_LO + i), : half_pulses // EDGE].astype(F32)
            pad_ref[pl.ds(2 * EDGE + h * half_pulses, half_pulses), :] = part.reshape(
                half_pulses, width
            )
        blended = jnp.zeros((LANES + 2 * EDGE, width), F32)
        for t in range(2 * TAPS_K + 1):
            blended = blended + tap_rows_ref[t : t + 1, :] * pad_ref[
                pl.ds(EDGE - TAPS_K + t, LANES + 2 * EDGE), :
            ]
        turned = pltpu.roll(blended, width // 2, 1)
        lane_full = lax.broadcasted_iota(jnp.int32, blended.shape, 1)
        turned = jnp.where(lane_full < width // 2, -turned, turned)
        for k, value in enumerate((blended, turned)):
            value = value.astype(BF16)
            blend_ref[pl.ds(k * depth + i * LANES, LANES), :] = value[EDGE : EDGE + LANES]
            outside = jnp.concatenate([value[:EDGE], value[EDGE + LANES :]], axis=0)
            blend_ref[pl.ds(k * depth + main + i * 2 * EDGE, 2 * EDGE), :] = outside

    for i in range(Z_LO + 1):
        span = pl.ds(i * LANES, LANES)
        fine = fine_ref[0, :, span], fine_ref[1, :, span]
        for a in range(far_ref.shape[0] // FINE):
            coarse = coarse_ref[0, a : a + 1, span], coarse_ref[1, a : a + 1, span]
            fill(far_ref, a * FINE, i, coarse, fine)
    for side, table_ref in enumerate((near_ref, far_ref)):
        total = jnp.dot(table_ref[...], blend_ref[...], preferred_element_type=F32)
        for block in range(blocks // 2):
            part = total[block * columns : (block + 1) * columns]
            total_ref[side * (blocks // 2) + block] = part
            out_ref[in_row(side * (blocks // 2) + block), :tiles] = part.reshape(tiles, EDGE, width).astype(
                BF16
            )
    mine_ref[...] = total_ref[x]

    def came(half, z):
        return joined(lifted_ref[in_ring(half * Z_LO + z % Z_LO), half_pulses // EDGE])

    first_band = (z_hi == 1) & (yc == 0)
    last_band = (z_hi == 0) & (yc == N_YC - 1)
    foreign = came(1 - z_hi, z_lo)
    above = jnp.where(first_band, foreign, edge_ref[0:4])
    below = jnp.where(last_band, foreign, edge_ref[4:8])
    edge_out_ref[0:4] = above
    edge_out_ref[4:8] = below
    own = with_corners(column_ref[0:4], above, below)
    left = came(z_hi, z_lo + Z_LO - 1)
    left_fixed = with_corners(left, above, came(1 - z_hi, z_lo + Z_LO - 1))
    left = jnp.where(last_band, left_fixed, left)
    right = came(z_hi, z_lo + 1)
    right_fixed = with_corners(right, came(1 - z_hi, z_lo + 1), below)
    right = jnp.where(first_band, right_fixed, right)
    out_ref[:, tiles] = jnp.zeros((blocks, EDGE, LANES), BF16)
    after = two_parts(jnp.where(x < N_X - 1, own, left), spare_ref)
    before = two_parts(jnp.where(x > 0, own, right), spare_ref)
    out_ref[in_row(x + 1), tiles] = after
    out_ref[in_row(x + N_X - 1), tiles] = before


def finish(
    rows_ref, sums_ref, mine_ref, edge_ref, image_ref, out_ref, pad_ref, side_ref, flow_ref
):
    _, z_lo, x, _ = place_of()
    group = z_lo * N_X + x
    comps, rows, columns = image_ref.shape
    tall = pad_ref.shape[1]
    total = mine_ref[...]
    for k in range(1, N_X):
        part = sums_ref[in_row(x + k), : columns // EDGE].astype(F32)
        total = total + part.reshape(total.shape)
    step, weight = rows_ref[STEP : STEP + 1, :1], rows_ref[STEP + 1 : STEP + 2, :1]
    total = (total * step).T.reshape(image_ref.shape)

    zero = jnp.zeros((2, LANES), F32)
    left = joined(sums_ref[in_row(x + N_X - 1), columns // EDGE])[2:4]
    right = joined(sums_ref[in_row(x + 1), columns // EDGE])[0:2]
    side_ref[...] = jnp.zeros_like(side_ref)
    side_ref[0:2, :] = jnp.where(group > 0, left, zero)
    side_ref[2:4, :] = jnp.where(group < Z_LO * N_X - 1, right, zero)
    sides = side_ref[...].T[:tall]
    lane = lax.broadcasted_iota(jnp.int32, (tall, LANES), 1)
    blank = jnp.zeros((tall, LANES), F32)
    pad_ref[...] = jnp.zeros_like(pad_ref)
    for comp in range(comps):
        pad_ref[comp, EDGE : EDGE + rows, LANES : LANES + columns] = image_ref[comp]
        for half in range(2):
            span = pl.ds((1 + half) * LANES, LANES)
            pad_ref[comp, TOP : TOP + 1, span] = edge_ref[2 * comp + half : 2 * comp + half + 1, :]
            pad_ref[comp, LOW : LOW + 1, span] = edge_ref[4 + 2 * comp + half : 5 + 2 * comp + half, :]
        pad_ref[comp, :, :LANES] = jnp.where(lane == LANES - 1, sides[:, comp : comp + 1], blank)
        pad_ref[comp, :, LANES + columns :] = jnp.where(
            lane == 0, sides[:, 2 + comp : 3 + comp], blank
        )

    high, wide = rows + EDGE, columns + LANES
    row_step, col_step = [], []
    square = jnp.zeros((high, wide), F32) + smooth_eps
    for comp in range(comps):
        here = pad_ref[comp, :high, :]
        following = pltpu.roll(here, here.shape[1] - 1, 1)[:, :wide]
        here = here[:, :wide]
        row_step.append(pad_ref[comp, 1 : high + 1, :wide] - here)
        col_step.append(following - here)
        square = square + row_step[-1] * row_step[-1] + col_step[-1] * col_step[-1]
    inverse = lax.rsqrt(square)
    for comp in range(comps):
        row_flow = row_step[comp] * inverse
        col_flow = col_step[comp] * inverse
        flow_ref[...] = row_flow
        across = col_flow - pltpu.roll(col_flow, 1, 1)
        down = row_flow[EDGE:, LANES:] - flow_ref[EDGE - 1 : high - 1, LANES:]
        variation = -(down + across[EDGE:, LANES:])
        out_ref[comp] = image_ref[comp] - (total[comp] + weight * variation)


def in_hbm(*values):
    return tuple(pltpu.with_memory_space_constraint(value, pltpu.HBM) for value in values)


def call(kernel, out_shape, in_specs, args, scratch=(), cost=None, out_specs=None):
    if out_specs is None:
        out_specs = [VMEM] * len(out_shape) if isinstance(out_shape, tuple) else VMEM
    return pl.pallas_call(
        kernel,
        out_shape=out_shape,
        in_specs=in_specs,
        out_specs=out_specs,
        scratch_shapes=scratch,
        cost_estimate=cost,
        compiler_params=pltpu.CompilerParams(vmem_limit_bytes=16 * 1024 * 1024),
    )(*args)


def local(
    pulse_data,
    window_start,
    footprint,
    range_to_row_weight,
    slow_taps,
    ramp_rate,
    image_now,
    step_and_variation_weight,
):
    band_count = lax.axis_size("band")
    groups = lax.axis_size("aper")
    comps, pulses, bins = pulse_data.shape
    band_rows, window_len = range_to_row_weight.shape
    columns = image_now.shape[2]
    shape = jax.ShapeDtypeStruct

    block = window_len // LANES * comps * pulses
    given = in_hbm(window_start, footprint, pulse_data, image_now)
    windows = ()
    weight = range_to_row_weight
    for wanted in range(Z_HI):
        windows = pl.pallas_call(
            functools.partial(cut_windows, wanted),
            out_shape=pltpu.HBM((N_YC, Z_HI * block // EDGE + 1, EDGE, LANES), BF16),
            in_specs=[HBM] * (len(given) + len(windows)),
            out_specs=HBM,
            scratch_shapes=[
                pltpu.SMEM(window_start.shape, jnp.int32),
                pltpu.SMEM(footprint.shape, jnp.int32),
                pltpu.VMEM(pulse_data.shape, BF16),
                pltpu.VMEM((2, comps, EDGE, columns), F32),
                pltpu.VMEM(((pulses + 1) * comps * (bins // LANES + 1), LANES), F32),
                pltpu.VMEM((band_count * block + EDGE, LANES), F32),
                pltpu.VMEM((N_YC, Z_HI * block // EDGE + 1, EDGE, LANES), BF16),
                pltpu.VMEM((EDGE, LANES), F32),
                pltpu.SemaphoreType.DMA((5,)),
                pltpu.SemaphoreType.DMA((N_YC,)),
            ],
            input_output_aliases={len(given): 0} if windows else {},
            compiler_params=pltpu.CompilerParams(vmem_limit_bytes=16 * 1024 * 1024),
        )(*given, *windows)
        if wanted == 0:
            weight, windows = lax.optimization_barrier((weight, windows))
            other_weight = lax.ppermute(weight, ("aper", "band"), halves_swapped())
            windows = (windows,)
    half = N_X * columns // 2
    depth = (Z_LO + 1) * LANES
    near, fine, coarse, tap_rows = call(
        make_table,
        (
            shape((half, 2 * depth), BF16),
            shape((2, FINE, depth), F32),
            shape((2, half // FINE, depth), F32),
            shape((EDGE, LANES), F32),
        ),
        [HBM] * 4,
        (
            *in_hbm(
                windows,
                ramp_rate.reshape(groups, LANES),
                slow_taps,
                step_and_variation_weight,
            ),
        ),
        [
            pltpu.VMEM((groups, LANES), F32),
            pltpu.SMEM(slow_taps.shape, F32),
            pltpu.SMEM(step_and_variation_weight.shape, F32),
            pltpu.VMEM((2 * EDGE, LANES), F32),
            pltpu.VMEM((2, 2 * half // FINE, LANES), F32),
            pltpu.SemaphoreType.DMA((3,)),
        ],
        pl.CostEstimate(flops=1 << 24, bytes_accessed=1 << 23, transcendentals=0),
    )
    planes = [
        [h * N_YC + (FIRST_YC + i) % N_YC for i in range(N_YC)] for h in range(Z_HI)
    ]
    windows = lax.all_to_all(windows, "band", 0, 0, axis_index_groups=planes, tiled=True)
    side, weights = call(
        side_columns,
        (shape((EDGE, LANES), F32), shape((Z_HI, band_rows, window_len), BF16)),
        [HBM, HBM, VMEM],
        (*in_hbm(image_now, range_to_row_weight), other_weight),
        [
            pltpu.VMEM((LANES, LANES), F32),
            pltpu.VMEM((2, comps, band_rows, LANES), F32),
            pltpu.SemaphoreType.DMA((3,)),
        ],
        pl.CostEstimate(flops=1 << 34, bytes_accessed=1 << 27, transcendentals=0),
    )
    width = comps * band_rows
    lifted, edges = call(
        lift_windows,
        (
            shape((N_Z, N_YC * pulses // EDGE + 1, EDGE, width), BF16),
            shape((EDGE, LANES), F32),
        ),
        [VMEM] * 3 + [ANY],
        (windows, weights, side, tap_rows),
        [pltpu.VMEM((EDGE, LANES), F32)],
    )
    lifted = lax.all_to_all(lifted, ("aper", "band"), 0, 0, axis_index_groups=z_rings(), tiled=True)
    sums, mine, edges = call(
        sum_pulses,
        (
            shape((N_X, columns // EDGE + 1, EDGE, width), BF16),
            shape((columns, width), F32),
            shape((EDGE, LANES), F32),
        ),
        [VMEM] * 7,
        (tap_rows, near, fine, coarse, lifted, side, edges),
        [
            pltpu.VMEM((LANES + 4 * EDGE, width), F32),
            pltpu.VMEM((2 * depth, width), BF16),
            pltpu.VMEM((half, 2 * depth), BF16),
            pltpu.VMEM((N_X, columns, width), F32),
            pltpu.VMEM((EDGE, LANES), F32),
        ],
    )
    along_x = [
        [z * N_X + (FIRST_X + k) % N_X for k in range(N_X)] for z in range(Z_LO)
    ]
    sums = lax.all_to_all(sums, "aper", 0, 0, axis_index_groups=along_x, tiled=True)
    return call(
        finish,
        shape(image_now.shape, F32),
        [VMEM] * 5,
        (tap_rows, sums, mine, edges, image_now),
        [
            pltpu.VMEM((comps, band_rows + 2 * EDGE, columns + 2 * LANES), F32),
            pltpu.VMEM((LANES, LANES), F32),
            pltpu.VMEM((band_rows + EDGE, columns + LANES), F32),
        ],
    )


def solution(mesh):
    return jax.shard_map(
        local,
        mesh=mesh,
        in_specs=(
            P(None, ("aper", "band"), None),
            P(("aper", "band"), None),
            P(("aper", "band"), None),
            P("band", None),
            P(),
            P(),
            P(None, "band", "aper"),
            P(),
        ),
        out_specs=P(None, "band", "aper"),
        check_vma=False,
    )
```

```python
import functools
import math

import jax
import jax.numpy as jnp
from jax import lax
from jax.experimental import pallas as pl
from jax.experimental.pallas import tpu as pltpu
from jax.sharding import PartitionSpec as P

TAPS_K = 2
LANES = 128
EDGE = 8
Z_HI, Z_LO, N_X, N_YC = 2, 8, 4, 8
N_Z = Z_HI * Z_LO
FIRST_Z = 8
FIRST_YC = 5
FIRST_X = 2
smooth_eps = 0.05
BF16, F32 = jnp.bfloat16, jnp.float32
VMEM = pl.BlockSpec(memory_space=pltpu.VMEM)
SMEM = pl.BlockSpec(memory_space=pltpu.SMEM)
ANY = pl.BlockSpec(memory_space=pl.ANY)
HBM = pl.BlockSpec(memory_space=pltpu.HBM)


def device_index(z_hi, z_lo, x, yc):
    return ((z_lo * N_X + x) * Z_HI + z_hi) * N_YC + yc


def z_rings():
    order = [(FIRST_Z + k) % N_Z for k in range(N_Z)]
    return [
        [device_index(z // Z_LO, z % Z_LO, x, yc) for z in order]
        for x in range(N_X)
        for yc in range(N_YC)
    ]


def in_plane(yc):
    return (yc + N_YC - FIRST_YC) % N_YC


def in_row(x):
    return (x + N_X - FIRST_X) % N_X


def in_ring(z):
    return (z + N_Z - FIRST_Z) % N_Z


def halves_swapped():
    return [
        (device_index(h, z, x, yc), device_index(1 - h, (z + Z_LO // 2) % Z_LO, x, yc))
        for h in range(Z_HI)
        for z in range(Z_LO)
        for x in range(N_X)
        for yc in range(N_YC)
    ]


def place_of():
    group, band = lax.axis_index("aper"), lax.axis_index("band")
    return band // N_YC, group // N_X, group % N_X, band % N_YC


def two_parts(value, spare_ref):
    first = value.astype(BF16).astype(F32)
    spare_ref[0:4] = first
    spare_ref[4:8] = value - first
    return spare_ref[...].astype(BF16)


def joined(rows):
    rows = rows.astype(F32)
    return rows[0:4] + rows[4:8]


TOP, LOW = EDGE - 1, EDGE + 64


def with_corners(columns, above, below):
    lane = lax.broadcasted_iota(jnp.int32, columns.shape, 1)
    row = lax.broadcasted_iota(jnp.int32, columns.shape, 0)
    above = pltpu.roll(above, TOP, 1)
    below = pltpu.roll(below, (LOW + 1) % LANES, 1)
    for comp in range(2):
        columns = jnp.where((lane == TOP) & (row == comp), above[2 * comp : 2 * comp + 1], columns)
        columns = jnp.where(
            (lane == LOW) & (row == 2 + comp), below[2 * comp + 1 : 2 * comp + 2], columns
        )
    return columns


def cut_windows(wanted, start_hbm, foot_hbm, pulse_hbm, image_hbm, *refs):
    (
        out_hbm,
        start_ref,
        foot_ref,
        pulse_ref,
        edge_ref,
        flat_ref,
        window_ref,
        packed_ref,
        spare_ref,
        sem,
        out_sem,
    ) = refs[-11:]

    @pl.when(place_of()[0] == wanted)
    def _():
        rows = image_hbm.shape[1]
        copies = [
            pltpu.make_async_copy(pulse_hbm, pulse_ref, sem.at[0]),
            pltpu.make_async_copy(start_hbm, start_ref, sem.at[1]),
            pltpu.make_async_copy(foot_hbm, foot_ref, sem.at[2]),
            pltpu.make_async_copy(image_hbm.at[:, pl.ds(0, EDGE), :], edge_ref.at[0], sem.at[3]),
            pltpu.make_async_copy(image_hbm.at[:, pl.ds(rows - EDGE, EDGE), :], edge_ref.at[1], sem.at[4]),
        ]
        for copy in copies:
            copy.start()
        window_ref[...] = jnp.zeros_like(window_ref)
        comps, pulses, bins = pulse_ref.shape
        parts = bins // LANES
        pitch = comps * (parts + 1)
        block = (window_ref.shape[0] - EDGE) // (Z_HI * N_YC)
        for copy in copies:
            copy.wait()
        for part in range(parts):
            for comp in range(comps):
                flat_ref[pl.ds(part * comps + comp, pulses, stride=pitch), :] = pulse_ref[
                    comp, :, part * LANES : (part + 1) * LANES
                ].astype(F32)
        lane = lax.broadcasted_iota(jnp.int32, (block // pulses, LANES), 1)
        for pulse in range(pulses):
            for k in range(foot_ref.shape[1]):
                band = foot_ref[pulse, k]
                start = start_ref[pulse, band]
                row = pulse * pitch + comps * (start >> 7)
                shift = start & (LANES - 1)
                here = flat_ref[pl.ds(row, block // pulses), :]
                following = flat_ref[pl.ds(row + comps, block // pulses), :]
                both = jnp.where(lane >= shift, here, following)
                both = pltpu.roll(both, (LANES - shift) & (LANES - 1), 1)
                place = (((band + N_YC - FIRST_YC) & (N_YC - 1)) * Z_HI + (band >> 3)) * block + pulse
                window_ref[pl.ds(place, block // pulses, stride=pulses), :] = both
        tall = Z_HI * block
        packed_ref[:, tall // EDGE] = jnp.zeros((N_YC, EDGE, LANES), BF16)
        yc = place_of()[3]
        for side, line, to in ((0, 0, yc + N_YC - 1), (1, EDGE - 1, yc + 1)):
            edge = [edge_ref[side, comp, line : line + 1, :] for comp in range(comps)]
            edge = [e[:, i * LANES : (i + 1) * LANES] for e in edge for i in range(2)]
            packed_ref[in_plane(to), tall // EDGE] = two_parts(jnp.concatenate(edge, axis=0), spare_ref)
        leaving = []
        for to in range(N_YC):
            part = window_ref[to * tall : (to + 1) * tall, :].reshape(tall // EDGE, EDGE, LANES)
            packed_ref[to, : tall // EDGE] = part.astype(BF16)
            leaving.append(pltpu.make_async_copy(packed_ref.at[to], out_hbm.at[to], out_sem.at[to]))
            leaving[-1].start()
        for copy in leaving:
            copy.wait()


def side_columns(image_hbm, weight_hbm, other_ref, out_ref, weight_ref, pad_ref, block_ref, sem):
    z_hi = place_of()[0]
    rows, columns = image_hbm.shape[1:]
    copies = [
        pltpu.make_async_copy(weight_hbm, weight_ref.at[z_hi], sem.at[0]),
        pltpu.make_async_copy(image_hbm.at[:, :, pl.ds(0, LANES)], block_ref.at[0], sem.at[1]),
        pltpu.make_async_copy(
            image_hbm.at[:, :, pl.ds(columns - LANES, LANES)], block_ref.at[1], sem.at[2]
        ),
    ]
    for copy in copies:
        copy.start()
    weight_ref[1 - z_hi] = other_ref[...]
    pad_ref[...] = jnp.zeros_like(pad_ref)
    out_ref[...] = jnp.zeros_like(out_ref)
    for copy in copies:
        copy.wait()
    for comp in range(2):
        for side, line in ((0, 0), (1, LANES - 1)):
            pad_ref[EDGE : EDGE + rows, :] = block_ref[side, comp]
            out_ref[2 * side + comp : 2 * side + comp + 1, :] = pad_ref[...].T[line : line + 1, :]


def lift_windows(
    window_ref, weight_ref, column_ref, after_ref, out_ref, edge_ref, spare_ref
):
    del after_ref
    z_hi, _, _, yc = place_of()
    sources, height = window_ref.shape[0], window_ref.shape[1] - 1
    half = height // Z_HI
    band_rows, window_len = weight_ref.shape[1:]
    parts = window_len // LANES
    tiles = half // parts
    rows = tiles * EDGE
    tall = sources * rows // 2

    above = joined(window_ref[in_plane(yc + N_YC - 1), height])
    below = joined(window_ref[in_plane(yc + 1), height])
    foreign = jnp.where(yc == 0, above, below)
    above = jnp.where(yc > 0, above, jnp.zeros_like(above))
    below = jnp.where(yc < N_YC - 1, below, jnp.zeros_like(below))
    edge_ref[0:4] = above
    edge_ref[4:8] = below
    columns = with_corners(column_ref[0:4], above, below)

    dims = (((1,), (1,)), ((), ()))
    for z_half in range(Z_HI):
        extra = jnp.where(z_half == z_hi, columns, foreign)
        lifted = jnp.zeros((sources * rows, band_rows), F32)
        for part in range(parts):
            first = z_half * half + part * tiles
            piece = window_ref[:, pl.ds(first, tiles)].astype(F32)
            piece = piece.reshape(sources * rows, LANES).astype(BF16)
            lifted = lifted + lax.dot_general(
                piece,
                weight_ref[z_half, :, part * LANES : (part + 1) * LANES],
                dims,
                preferred_element_type=F32,
            )
        lifted = lifted.reshape(sources, 2, rows // 2, band_rows)
        both = jnp.concatenate([lifted[:, 0], lifted[:, 1]], axis=-1)
        both = both.reshape(tall // EDGE, EDGE, 2 * band_rows).astype(BF16)
        extra = two_parts(extra, spare_ref)
        for z in range(Z_LO):
            for source in range(sources):
                out_ref[in_ring(z_half * Z_LO + z), source] = both[in_plane(source)]
            out_ref[in_ring(z_half * Z_LO + z), tall // EDGE] = extra


def sin_cos(angle):
    turns = jnp.round(angle * (2.0 / math.pi))
    rest = angle - turns * 1.5703125
    rest = rest - turns * 4.837512969970703125e-4
    rest = rest - turns * 7.54978995489188216e-8
    square = rest * rest
    sine = -1.9515295891e-4 * square + 8.3321608736e-3
    sine = (sine * square - 1.6666654611e-1) * square * rest + rest
    cosine = 2.443315711809948e-5 * square - 1.388731625493765e-3
    cosine = (cosine * square + 4.166664568298827e-2) * square * square - 0.5 * square + 1.0
    quarter = turns.astype(jnp.int32) & 3
    swap = (quarter & 1) == 1
    sin_out = jnp.where(swap, cosine, sine)
    cos_out = jnp.where(swap, sine, cosine)
    sin_out = jnp.where(quarter >= 2, -sin_out, sin_out)
    cos_out = jnp.where((quarter == 1) | (quarter == 2), -cos_out, cos_out)
    return sin_out, cos_out


FINE = 16
STEP = 2 * TAPS_K + 1


def make_table(
    after_ref,
    ramp_hbm,
    taps_hbm,
    step_hbm,
    near_ref,
    fine_ref,
    coarse_ref,
    tap_rows_ref,
    ramp_ref,
    taps_ref,
    step_ref,
    rate_ref,
    spare_ref,
    sem,
):
    del after_ref
    copies = [
        pltpu.make_async_copy(ramp_hbm, ramp_ref, sem.at[0]),
        pltpu.make_async_copy(taps_hbm, taps_ref, sem.at[1]),
        pltpu.make_async_copy(step_hbm, step_ref, sem.at[2]),
    ]
    for copy in copies:
        copy.start()
    _, z_lo, x, _ = place_of()
    n_groups = ramp_ref.shape[0]
    half = near_ref.shape[0]
    for copy in copies:
        copy.wait()
    for t in range(2 * TAPS_K + 1):
        tap_rows_ref[t : t + 1, :] = jnp.full((1, LANES), taps_ref[t], F32)
    scale = 1.0 / math.sqrt(n_groups * LANES)
    tap_rows_ref[STEP : STEP + 1, :] = jnp.full((1, LANES), step_ref[0] * scale, F32)
    tap_rows_ref[STEP + 1 : STEP + 2, :] = jnp.full((1, LANES), step_ref[0] * step_ref[1], F32)

    lane = lax.broadcasted_iota(jnp.int32, (1, LANES), 1)
    ends = jnp.zeros((1, LANES), F32)
    for i in range(Z_LO):
        group = i * N_X + x
        rate_ref[i : i + 1, :] = ramp_ref[pl.ds(group, 1), :]
        before = ramp_ref[pl.ds((group + n_groups - 1) % n_groups, 1), :]
        after = ramp_ref[pl.ds((group + 1) % n_groups, 1), :]
        place = 2 * EDGE * i
        move = (place + EDGE) % LANES
        before = pltpu.roll(before, move, 1) if move else before
        after = pltpu.roll(after, move, 1) if move else after
        ends = jnp.where((lane >= place) & (lane < place + EDGE), before, ends)
        ends = jnp.where((lane >= place + EDGE) & (lane < place + 2 * EDGE), after, ends)
    rate_ref[Z_LO : Z_LO + 1, :] = ends

    n_coarse = 2 * half // FINE
    first = z_lo * 2 * half
    fine_step = lax.broadcasted_iota(jnp.int32, (FINE, LANES), 0).astype(F32)
    coarse_step = (
        first + FINE * lax.broadcasted_iota(jnp.int32, (n_coarse, LANES), 0)
    ).astype(F32)
    for i in range(Z_LO + 1):
        span = pl.ds(i * LANES, LANES)
        rate = rate_ref[i : i + 1, :]
        fine_sin, fine_cos = sin_cos(rate * fine_step)
        coarse_sin, coarse_cos = sin_cos(rate * coarse_step)
        fine_ref[0, :, span], fine_ref[1, :, span] = fine_sin, fine_cos
        spare_ref[0], spare_ref[1] = coarse_sin, coarse_cos
        coarse_ref[0, :, span] = coarse_sin[n_coarse // 2 :]
        coarse_ref[1, :, span] = coarse_cos[n_coarse // 2 :]
        for a in range(n_coarse // 2):
            fill(
                near_ref,
                a * FINE,
                i,
                (spare_ref[0, a : a + 1, :], spare_ref[1, a : a + 1, :]),
                (fine_sin, fine_cos),
            )


def fill(table_ref, row, i, coarse, fine):
    depth = table_ref.shape[1] // 2
    (s, c), (fine_sin, fine_cos) = coarse, fine
    table_ref[row : row + FINE, i * LANES : (i + 1) * LANES] = (
        c * fine_cos - s * fine_sin
    ).astype(BF16)
    table_ref[row : row + FINE, depth + i * LANES : depth + (i + 1) * LANES] = (
        s * fine_cos + c * fine_sin
    ).astype(BF16)


def sum_pulses(
    tap_rows_ref,
    near_ref,
    fine_ref,
    coarse_ref,
    lifted_ref,
    column_ref,
    edge_ref,
    out_ref,
    mine_ref,
    edge_out_ref,
    pad_ref,
    blend_ref,
    far_ref,
    total_ref,
    spare_ref,
):
    z_hi, z_lo, x, yc = place_of()
    width = lifted_ref.shape[3]
    half_pulses = LANES // Z_HI
    main = Z_LO * LANES
    depth = main + LANES
    blocks, tiles = out_ref.shape[0], out_ref.shape[1] - 1
    columns = tiles * EDGE

    zero = jnp.zeros((2 * EDGE, width), F32)
    pad_ref[: 2 * EDGE] = zero
    pad_ref[2 * EDGE + LANES :] = zero
    for i in range(Z_LO):
        for h in range(Z_HI):
            part = lifted_ref[in_ring(h * Z_LO + i), : half_pulses // EDGE].astype(F32)
            pad_ref[pl.ds(2 * EDGE + h * half_pulses, half_pulses), :] = part.reshape(
                half_pulses, width
            )
        blended = jnp.zeros((LANES + 2 * EDGE, width), F32)
        for t in range(2 * TAPS_K + 1):
            blended = blended + tap_rows_ref[t : t + 1, :] * pad_ref[
                pl.ds(EDGE - TAPS_K + t, LANES + 2 * EDGE), :
            ]
        turned = pltpu.roll(blended, width // 2, 1)
        lane_full = lax.broadcasted_iota(jnp.int32, blended.shape, 1)
        turned = jnp.where(lane_full < width // 2, -turned, turned)
        for k, value in enumerate((blended, turned)):
            value = value.astype(BF16)
            blend_ref[pl.ds(k * depth + i * LANES, LANES), :] = value[EDGE : EDGE + LANES]
            outside = jnp.concatenate([value[:EDGE], value[EDGE + LANES :]], axis=0)
            blend_ref[pl.ds(k * depth + main + i * 2 * EDGE, 2 * EDGE), :] = outside

    for i in range(Z_LO + 1):
        span = pl.ds(i * LANES, LANES)
        fine = fine_ref[0, :, span], fine_ref[1, :, span]
        for a in range(far_ref.shape[0] // FINE):
            coarse = coarse_ref[0, a : a + 1, span], coarse_ref[1, a : a + 1, span]
            fill(far_ref, a * FINE, i, coarse, fine)
    for side, table_ref in enumerate((near_ref, far_ref)):
        total = jnp.dot(table_ref[...], blend_ref[...], preferred_element_type=F32)
        for block in range(blocks // 2):
            part = total[block * columns : (block + 1) * columns]
            total_ref[side * (blocks // 2) + block] = part
            out_ref[in_row(side * (blocks // 2) + block), :tiles] = part.reshape(tiles, EDGE, width).astype(
                BF16
            )
    mine_ref[...] = total_ref[x]

    def came(half, z):
        return joined(lifted_ref[in_ring(half * Z_LO + z % Z_LO), half_pulses // EDGE])

    first_band = (z_hi == 1) & (yc == 0)
    last_band = (z_hi == 0) & (yc == N_YC - 1)
    foreign = came(1 - z_hi, z_lo)
    above = jnp.where(first_band, foreign, edge_ref[0:4])
    below = jnp.where(last_band, foreign, edge_ref[4:8])
    edge_out_ref[0:4] = above
    edge_out_ref[4:8] = below
    own = with_corners(column_ref[0:4], above, below)
    left = came(z_hi, z_lo + Z_LO - 1)
    left_fixed = with_corners(left, above, came(1 - z_hi, z_lo + Z_LO - 1))
    left = jnp.where(last_band, left_fixed, left)
    right = came(z_hi, z_lo + 1)
    right_fixed = with_corners(right, came(1 - z_hi, z_lo + 1), below)
    right = jnp.where(first_band, right_fixed, right)
    out_ref[:, tiles] = jnp.zeros((blocks, EDGE, LANES), BF16)
    after = two_parts(jnp.where(x < N_X - 1, own, left), spare_ref)
    before = two_parts(jnp.where(x > 0, own, right), spare_ref)
    out_ref[in_row(x + 1), tiles] = after
    out_ref[in_row(x + N_X - 1), tiles] = before


def finish(
    rows_ref, sums_ref, mine_ref, edge_ref, image_ref, out_ref, pad_ref, side_ref, flow_ref
):
    _, z_lo, x, _ = place_of()
    group = z_lo * N_X + x
    comps, rows, columns = image_ref.shape
    tall = pad_ref.shape[1]
    total = mine_ref[...]
    for k in range(1, N_X):
        part = sums_ref[in_row(x + k), : columns // EDGE].astype(F32)
        total = total + part.reshape(total.shape)
    step, weight = rows_ref[STEP : STEP + 1, :1], rows_ref[STEP + 1 : STEP + 2, :1]
    total = (total * step).T.reshape(image_ref.shape)

    zero = jnp.zeros((2, LANES), F32)
    left = joined(sums_ref[in_row(x + N_X - 1), columns // EDGE])[2:4]
    right = joined(sums_ref[in_row(x + 1), columns // EDGE])[0:2]
    side_ref[...] = jnp.zeros_like(side_ref)
    side_ref[0:2, :] = jnp.where(group > 0, left, zero)
    side_ref[2:4, :] = jnp.where(group < Z_LO * N_X - 1, right, zero)
    sides = side_ref[...].T[:tall]
    lane = lax.broadcasted_iota(jnp.int32, (tall, LANES), 1)
    blank = jnp.zeros((tall, LANES), F32)
    pad_ref[...] = jnp.zeros_like(pad_ref)
    for comp in range(comps):
        pad_ref[comp, EDGE : EDGE + rows, LANES : LANES + columns] = image_ref[comp]
        for half in range(2):
            span = pl.ds((1 + half) * LANES, LANES)
            pad_ref[comp, TOP : TOP + 1, span] = edge_ref[2 * comp + half : 2 * comp + half + 1, :]
            pad_ref[comp, LOW : LOW + 1, span] = edge_ref[4 + 2 * comp + half : 5 + 2 * comp + half, :]
        pad_ref[comp, :, :LANES] = jnp.where(lane == LANES - 1, sides[:, comp : comp + 1], blank)
        pad_ref[comp, :, LANES + columns :] = jnp.where(
            lane == 0, sides[:, 2 + comp : 3 + comp], blank
        )

    high, wide = rows + EDGE, columns + LANES
    row_step, col_step = [], []
    square = jnp.zeros((high, wide), F32) + smooth_eps
    for comp in range(comps):
        here = pad_ref[comp, :high, :]
        following = pltpu.roll(here, here.shape[1] - 1, 1)[:, :wide]
        here = here[:, :wide]
        row_step.append(pad_ref[comp, 1 : high + 1, :wide] - here)
        col_step.append(following - here)
        square = square + row_step[-1] * row_step[-1] + col_step[-1] * col_step[-1]
    inverse = lax.rsqrt(square)
    for comp in range(comps):
        row_flow = row_step[comp] * inverse
        col_flow = col_step[comp] * inverse
        flow_ref[...] = row_flow
        across = col_flow - pltpu.roll(col_flow, 1, 1)
        down = row_flow[EDGE:, LANES:] - flow_ref[EDGE - 1 : high - 1, LANES:]
        variation = -(down + across[EDGE:, LANES:])
        out_ref[comp] = image_ref[comp] - (total[comp] + weight * variation)


def in_hbm(*values):
    return tuple(pltpu.with_memory_space_constraint(value, pltpu.HBM) for value in values)


def call(kernel, out_shape, in_specs, args, scratch=(), cost=None, out_specs=None):
    if out_specs is None:
        out_specs = [VMEM] * len(out_shape) if isinstance(out_shape, tuple) else VMEM
    return pl.pallas_call(
        kernel,
        out_shape=out_shape,
        in_specs=in_specs,
        out_specs=out_specs,
        scratch_shapes=scratch,
        cost_estimate=cost,
        compiler_params=pltpu.CompilerParams(vmem_limit_bytes=16 * 1024 * 1024),
    )(*args)


def local(
    pulse_data,
    window_start,
    footprint,
    range_to_row_weight,
    slow_taps,
    ramp_rate,
    image_now,
    step_and_variation_weight,
):
    band_count = lax.axis_size("band")
    groups = lax.axis_size("aper")
    comps, pulses, bins = pulse_data.shape
    band_rows, window_len = range_to_row_weight.shape
    columns = image_now.shape[2]
    shape = jax.ShapeDtypeStruct

    block = window_len // LANES * comps * pulses
    given = in_hbm(window_start, footprint, pulse_data, image_now)
    windows = ()
    weight = range_to_row_weight
    for wanted in range(Z_HI):
        windows = pl.pallas_call(
            functools.partial(cut_windows, wanted),
            out_shape=pltpu.HBM((N_YC, Z_HI * block // EDGE + 1, EDGE, LANES), BF16),
            in_specs=[HBM] * (len(given) + len(windows)),
            out_specs=HBM,
            scratch_shapes=[
                pltpu.SMEM(window_start.shape, jnp.int32),
                pltpu.SMEM(footprint.shape, jnp.int32),
                pltpu.VMEM(pulse_data.shape, BF16),
                pltpu.VMEM((2, comps, EDGE, columns), F32),
                pltpu.VMEM(((pulses + 1) * comps * (bins // LANES + 1), LANES), F32),
                pltpu.VMEM((band_count * block + EDGE, LANES), F32),
                pltpu.VMEM((N_YC, Z_HI * block // EDGE + 1, EDGE, LANES), BF16),
                pltpu.VMEM((EDGE, LANES), F32),
                pltpu.SemaphoreType.DMA((5,)),
                pltpu.SemaphoreType.DMA((N_YC,)),
            ],
            input_output_aliases={len(given): 0} if windows else {},
            compiler_params=pltpu.CompilerParams(vmem_limit_bytes=16 * 1024 * 1024),
        )(*given, *windows)
        if wanted == 0:
            weight, windows = lax.optimization_barrier((weight, windows))
            other_weight = lax.ppermute(weight, ("aper", "band"), halves_swapped())
            windows = (windows,)
    half = N_X * columns // 2
    depth = (Z_LO + 1) * LANES
    near, fine, coarse, tap_rows = call(
        make_table,
        (
            shape((half, 2 * depth), BF16),
            shape((2, FINE, depth), F32),
            shape((2, half // FINE, depth), F32),
            shape((EDGE, LANES), F32),
        ),
        [HBM] * 4,
        (
            *in_hbm(
                windows,
                ramp_rate.reshape(groups, LANES),
                slow_taps,
                step_and_variation_weight,
            ),
        ),
        [
            pltpu.VMEM((groups, LANES), F32),
            pltpu.SMEM(slow_taps.shape, F32),
            pltpu.SMEM(step_and_variation_weight.shape, F32),
            pltpu.VMEM((2 * EDGE, LANES), F32),
            pltpu.VMEM((2, 2 * half // FINE, LANES), F32),
            pltpu.SemaphoreType.DMA((3,)),
        ],
        pl.CostEstimate(flops=1 << 24, bytes_accessed=1 << 23, transcendentals=0),
    )
    planes = [
        [h * N_YC + (FIRST_YC + i) % N_YC for i in range(N_YC)] for h in range(Z_HI)
    ]
    windows = lax.all_to_all(windows, "band", 0, 0, axis_index_groups=planes, tiled=True)
    side, weights = call(
        side_columns,
        (shape((EDGE, LANES), F32), shape((Z_HI, band_rows, window_len), BF16)),
        [HBM, HBM, VMEM],
        (*in_hbm(image_now, range_to_row_weight), other_weight),
        [
            pltpu.VMEM((LANES, LANES), F32),
            pltpu.VMEM((2, comps, band_rows, LANES), F32),
            pltpu.SemaphoreType.DMA((3,)),
        ],
        pl.CostEstimate(flops=1 << 34, bytes_accessed=1 << 27, transcendentals=0),
    )
    width = comps * band_rows
    lifted, edges = call(
        lift_windows,
        (
            shape((N_Z, N_YC * pulses // EDGE + 1, EDGE, width), BF16),
            shape((EDGE, LANES), F32),
        ),
        [VMEM] * 3 + [ANY],
        (windows, weights, side, tap_rows),
        [pltpu.VMEM((EDGE, LANES), F32)],
    )
    lifted = lax.all_to_all(lifted, ("aper", "band"), 0, 0, axis_index_groups=z_rings(), tiled=True)
    sums, mine, edges = call(
        sum_pulses,
        (
            shape((N_X, columns // EDGE + 1, EDGE, width), BF16),
            shape((columns, width), F32),
            shape((EDGE, LANES), F32),
        ),
        [VMEM] * 7,
        (tap_rows, near, fine, coarse, lifted, side, edges),
        [
            pltpu.VMEM((LANES + 4 * EDGE, width), F32),
            pltpu.VMEM((2 * depth, width), BF16),
            pltpu.VMEM((half, 2 * depth), BF16),
            pltpu.VMEM((N_X, columns, width), F32),
            pltpu.VMEM((EDGE, LANES), F32),
        ],
    )
    along_x = [
        [z * N_X + (FIRST_X + k) % N_X for k in range(N_X)] for z in range(Z_LO)
    ]
    sums = lax.all_to_all(sums, "aper", 0, 0, axis_index_groups=along_x, tiled=True)
    return call(
        finish,
        shape(image_now.shape, F32),
        [VMEM] * 5,
        (tap_rows, sums, mine, edges, image_now),
        [
            pltpu.VMEM((comps, band_rows + 2 * EDGE, columns + 2 * LANES), F32),
            pltpu.VMEM((LANES, LANES), F32),
            pltpu.VMEM((band_rows + EDGE, columns + LANES), F32),
        ],
    )


def solution(mesh):
    return jax.shard_map(
        local,
        mesh=mesh,
        in_specs=(
            P(None, ("aper", "band"), None),
            P(("aper", "band"), None),
            P(("aper", "band"), None),
            P("band", None),
            P(),
            P(),
            P(None, "band", "aper"),
            P(),
        ),
        out_specs=P(None, "band", "aper"),
        check_vma=False,
    )
```
